512 devices in a mesh: section: 8 (over y, core), tile: 64 (over x, z).
Axes of the slice: x: 4, y: 4, z: 16, core: 2. Of those that a mesh axis runs over, the one named last changes fastest.
Arguments:
- latent_feat: bfloat16 [4096, 128, 256], P(('section', 'tile')), may hold values from -6 to 6
- reward_grad: bfloat16 [2048, 64, 192], P('section', 'tile'), may hold values from -6 to 6
- patches: bfloat16 [2048, 3072], P('section', 'tile'), may hold values from -1 to 1
- up_weight: bfloat16 [3, 3, 256, 256], replicated, may hold values from -0.125 to 0.125
- up_bias: float32 [256], replicated, may hold values from -3 to 3
- norm_gain: float32 [256], replicated, may hold values from 0.5 to 2
- norm_bias: float32 [256], replicated, may hold values from -3 to 3
- out_weight: bfloat16 [3, 3, 256, 3], replicated, may hold values from -1.25 to 1.25
- stem_weight: bfloat16 [48, 192], replicated, may hold values from -0.875 to 0.875
- stem_bias: float32 [192], replicated, may hold values from -4 to 4
- stem_gain: float32 [192], replicated, may hold values from 0.5 to 2
- tile_count: int32 [512], replicated, may hold values from 1 to 3, as said below
- tile_cols: int32 [512, 3], replicated, may hold values from 0 to 112, as said below
Outputs:
- latent_grad: bfloat16 [4096, 128, 256], P(('section', 'tile'))
The draws below stay inside these ranges and needn't reach their ends.
Inputs may be any that keep to these rules, and one draw needn't show every extreme that they name: `tile_count`: each block has between 1 and 3 live tiles; some block has 3. `tile_cols`: slots k >= tile_count[b] are unused. Tiles of one block may cover the same columns.
All inputs are finite; a program needn't handle non-finite values.
Results may differ from the reference program's by a relative error of at most 0.0064.
Values may be sent and summed in bfloat16 or wider, within the bound.
A program may use at most 64 MiB of HBM per device.

```python
import math
import jax
import jax.numpy as jnp
from jax import lax

CH = 256
GROUPS = 32
STEM = 192
PATCH = 4
PIX = 48
TL = 16
MARGIN = 4
CENTRE = 8
MAXT = 3
IMAGES = 1
WL = 128
BLOCKS = 512
ROWS = 4096
PR = 2048
PC = 64


def draw_tile_count(key, part):
    key = jax.random.fold_in(key, 11)
    levels = jax.random.randint(key, (BLOCKS,), 0, 8)
    counts = 1 + (levels >= 5).astype(jnp.int32) + (levels >= 7).astype(jnp.int32)
    spot = jax.random.randint(jax.random.fold_in(key, 5), (), 0, BLOCKS)
    return counts.at[spot].set(MAXT).astype(jnp.int32)


def draw_tile_cols(key, part):
    key = jax.random.fold_in(key, 23)
    anchors = jax.random.randint(key, (BLOCKS, MAXT), 0, WL - TL + 1)
    low_spot = jax.random.randint(jax.random.fold_in(key, 7), (), 0, BLOCKS)
    high_spot = jax.random.randint(jax.random.fold_in(key, 9), (), 0, BLOCKS)
    anchors = anchors.at[low_spot, 0].set(0)
    anchors = anchors.at[high_spot, MAXT - 1].set(WL - TL)
    return anchors.astype(jnp.int32)


def block_levels(key, shape, shards, low, top_value):
    def one(axis_at, shards_of):
        heights = jax.random.uniform(jax.random.fold_in(jax.random.fold_in(key, 6), axis_at), (shards_of,), jnp.float32, low / len(shards), top_value / len(shards))
        return jnp.repeat(jnp.exp(heights), shape[axis_at] // shards_of).reshape((-1,) + (1,) * (len(shape) - axis_at - 1))

    level = one(*shards[0])
    for cut in shards[1:]:
        level = level * one(*cut)
    return level


def gaussian(rng, extent, deviation, most, pieces=(), kind=jnp.bfloat16):
    drawn = jax.random.normal(rng, extent, jnp.float32) * deviation
    if len(pieces) > 0:
        drawn = block_levels(rng, extent, pieces, -0.22, 0.18) * drawn
    return jnp.clip(drawn, min=-most, max=most).astype(kind)


def setup_inputs(seed: int = 0) -> dict:
    arg_keys = jax.random.split(jax.random.key(seed), 14)
    latent_feat = gaussian(arg_keys[0], (ROWS, WL, CH), 1.0, 6.0, ((0, 512),))
    reward_grad = gaussian(arg_keys[1], (PR, PC, STEM), 1.0, 6.0, ((0, 8), (1, 64)))
    patches = jnp.clip(jax.random.uniform(arg_keys[2], (PR, PC * PIX), jnp.float32, -1.0, 1.0) * block_levels(arg_keys[2], (PR, PC * PIX), ((0, 8), (1, 64)), -0.4, 0.0), -1.0, 1.0).astype(jnp.bfloat16)
    up_weight = gaussian(arg_keys[3], (3, 3, CH, CH), (9 * CH) ** -0.5, 0.125)
    up_bias = gaussian(arg_keys[4], (CH,), 0.5, 3.0, (), jnp.float32)
    norm_gain = jnp.clip(jnp.exp(jax.random.uniform(arg_keys[5], (CH,), jnp.float32, math.log(0.5), math.log(2.0))), 0.5, 2.0)
    norm_bias = gaussian(arg_keys[6], (CH,), 0.5, 3.0, (), jnp.float32)
    out_weight = gaussian(arg_keys[7], (3, 3, CH, 3), 27 ** -0.5, 1.25)
    stem_weight = gaussian(arg_keys[8], (PIX, STEM), PIX ** -0.5, 0.875)
    stem_bias = gaussian(arg_keys[9], (STEM,), 1.0, 4.0, (), jnp.float32)
    stem_gain = jnp.clip(jnp.exp(jax.random.uniform(arg_keys[10], (STEM,), jnp.float32, math.log(0.5), math.log(2.0))), 0.5, 2.0)
    tile_count = draw_tile_count(jax.random.fold_in(arg_keys[13], 71), 0)
    tile_cols = draw_tile_cols(jax.random.fold_in(arg_keys[13], 71), 0)
    return {"latent_feat": latent_feat, "reward_grad": reward_grad, "patches": patches, "up_weight": up_weight, "up_bias": up_bias, "norm_gain": norm_gain, "norm_bias": norm_bias, "out_weight": out_weight, "stem_weight": stem_weight, "stem_bias": stem_bias, "stem_gain": stem_gain, "tile_count": tile_count, "tile_cols": tile_cols}


EPS = 1e-06

def stem_backward(gradient, pixels, stem_weight, stem_bias, stem_gain):
    stem = jnp.dot(pixels, stem_weight, preferred_element_type=jnp.float32) + stem_bias
    centred = stem - lax.optimization_barrier(jnp.mean(stem, axis=-1, keepdims=True))
    inverse = lax.rsqrt(lax.optimization_barrier(jnp.mean(centred * centred, axis=-1, keepdims=True)) + EPS)
    normed = centred * inverse
    scaled = gradient.astype(jnp.float32) * stem_gain
    stem_grad = (scaled - lax.optimization_barrier(jnp.mean(scaled, axis=-1, keepdims=True)) - normed * lax.optimization_barrier(jnp.mean(scaled * normed, axis=-1, keepdims=True))) * inverse
    stem_grad = stem_grad.astype(jnp.bfloat16)
    result = lax.dot_general(stem_grad, stem_weight, (((1,), (1,)), ((), ())), preferred_element_type=jnp.float32)
    return result.astype(jnp.bfloat16)

def to_pixels(rows):
    count = rows.shape[0]
    width = rows.shape[1] // PIX
    grid = rows.reshape(count, width, 3, PATCH, PATCH)
    return grid.transpose(2, 0, 3, 1, 4).reshape(3, count * PATCH, width * PATCH)

def window_columns(padded, offsets, span):
    return jnp.concatenate([padded[top:top + span, left:left + span].reshape(span * span, -1) for top, left in offsets], axis=1)

def tile_backward(inputs, out_grad, forward_matrix, backward_matrix, out_matrix, up_bias, norm_gain, norm_bias):
    span = 2 * inputs.shape[0]
    channels = inputs.shape[2]
    forward_offsets = [(shift_row, shift_col) for shift_row in range(3) for shift_col in range(3)]
    backward_offsets = [(2 - shift_row, 2 - shift_col) for shift_row in range(3) for shift_col in range(3)]
    upsampled = jnp.repeat(jnp.repeat(inputs, 2, axis=0), 2, axis=1)
    padded = jnp.pad(upsampled, ((1, 1), (1, 1), (0, 0)))
    features = window_columns(padded, forward_offsets, span)
    preact = jnp.dot(features, forward_matrix, preferred_element_type=jnp.float32) + up_bias
    grouped = preact.reshape(span * span, GROUPS, channels // GROUPS)
    centred = grouped - lax.optimization_barrier(jnp.mean(grouped, axis=(0, 2), keepdims=True))
    inverse = lax.rsqrt(lax.optimization_barrier(jnp.mean(centred * centred, axis=(0, 2), keepdims=True)) + EPS)
    normed = centred * inverse
    activated = normed.reshape(span * span, channels) * norm_gain + norm_bias
    grad_pad = jnp.pad(out_grad, ((0, 0), (1, 1), (1, 1)))
    out_columns = jnp.concatenate([grad_pad[:, top:top + span, left:left + span].reshape(3, span * span) for top, left in backward_offsets], axis=0)
    act_grad = lax.dot_general(out_columns, out_matrix, (((0,), (0,)), ((), ())), preferred_element_type=jnp.float32)
    sigma = jax.nn.sigmoid(activated)
    norm_grad = act_grad * sigma * (1.0 + activated * (1.0 - sigma))
    scaled = (norm_grad * norm_gain).reshape(span * span, GROUPS, channels // GROUPS)
    pre_grad = (scaled - lax.optimization_barrier(jnp.mean(scaled, axis=(0, 2), keepdims=True)) - normed * lax.optimization_barrier(jnp.mean(scaled * normed, axis=(0, 2), keepdims=True))) * inverse
    pre_grad = pre_grad.reshape(span, span, channels).astype(jnp.bfloat16)
    grad_padded = jnp.pad(pre_grad, ((1, 1), (1, 1), (0, 0)))
    back_features = window_columns(grad_padded, backward_offsets, span)
    up_grad = jnp.dot(back_features, backward_matrix, preferred_element_type=jnp.float32)
    half = span // 2
    return up_grad.reshape(half, 2, half, 2, channels).sum(axis=(1, 3))

def add_block(total, piece, row, column):
    zero_index = jnp.zeros((), jnp.int32)
    current = lax.dynamic_slice(total, (row, column, zero_index), piece.shape)
    return lax.dynamic_update_slice(total, current + piece, (row, column, zero_index))

def reference(latent_feat, reward_grad, patches, up_weight, up_bias, norm_gain, norm_bias, out_weight, stem_weight, stem_bias, stem_gain, tile_count, tile_cols):
    patch_rows = reward_grad.shape[0]
    patch_cols = reward_grad.shape[1]
    pixel = stem_backward(reward_grad.reshape(patch_rows * patch_cols, STEM), patches.reshape(patch_rows * patch_cols, PIX), stem_weight, stem_bias, stem_gain)
    pixel = pixel.reshape(BLOCKS, patch_rows // BLOCKS, patch_cols * PIX)
    blocks = latent_feat.reshape(BLOCKS, CENTRE, WL, CH)
    per_image = BLOCKS // IMAGES
    position = jnp.arange(BLOCKS, dtype=jnp.int32)
    keep_top = position % per_image != 0
    keep_bottom = position % per_image != per_image - 1
    empty = jnp.zeros((1, MARGIN, WL, CH), jnp.bfloat16)
    above = jnp.concatenate([empty, blocks[:-1, CENTRE - MARGIN:]], axis=0)
    below = jnp.concatenate([blocks[1:, :MARGIN], empty], axis=0)
    above = jnp.where(keep_top[:, None, None, None], above, jnp.zeros_like(above))
    below = jnp.where(keep_bottom[:, None, None, None], below, jnp.zeros_like(below))
    forward_matrix = up_weight.reshape(9 * CH, CH)
    backward_matrix = up_weight.transpose(0, 1, 3, 2).reshape(9 * CH, CH)
    out_matrix = out_weight.transpose(0, 1, 3, 2).reshape(27, CH)
    zero_index = jnp.zeros((), jnp.int32)

    def one_block(carry, items):
        upper, middle, lower, pixel_rows, count, columns, top_flag, bottom_flag = items
        extended = jnp.concatenate([upper, middle, lower], axis=0)
        image_grad = to_pixels(pixel_rows)
        total = jnp.zeros((TL, WL, CH), jnp.float32)
        for slot in range(MAXT):
            anchor = columns[slot].astype(jnp.int32)

            def compute():
                inputs = lax.dynamic_slice(extended, (zero_index, anchor, zero_index), (TL, TL, CH))
                centre = lax.dynamic_slice(image_grad, (zero_index, zero_index, 2 * anchor + 2 * MARGIN), (3, 2 * CENTRE, 2 * CENTRE))
                out_grad = jnp.pad(centre, ((0, 0), (2 * MARGIN, 2 * MARGIN), (2 * MARGIN, 2 * MARGIN)))
                return tile_backward(inputs, out_grad, forward_matrix, backward_matrix, out_matrix, up_bias, norm_gain, norm_bias)

            def skipped():
                return jnp.zeros((TL, TL, CH), jnp.float32)
            tile_grad = lax.cond(slot < count, compute, skipped)
            total = add_block(total, tile_grad, zero_index, anchor)
        main = total[MARGIN:MARGIN + CENTRE]
        main = main.at[:MARGIN].add(carry)
        next_carry = jnp.where(bottom_flag, total[TL - MARGIN:], jnp.zeros((MARGIN, WL, CH), jnp.float32))
        upper_part = jnp.where(top_flag, total[:MARGIN], jnp.zeros((MARGIN, WL, CH), jnp.float32))
        return (next_carry, (main, upper_part))
    start = jnp.zeros((MARGIN, WL, CH), jnp.float32)
    final_carry, (mains, uppers) = lax.scan(one_block, start, (above, blocks, below, pixel, tile_count, tile_cols, keep_top, keep_bottom))
    mains = mains.at[:-1, CENTRE - MARGIN:].add(uppers[1:])
    return mains.reshape(BLOCKS * CENTRE, WL, CH).astype(jnp.bfloat16)
```

```python
import functools

import jax
import jax.numpy as jnp
import numpy as np
from jax import lax
from jax.experimental import pallas as pl
from jax.experimental.pallas import tpu as pltpu
from jax.sharding import PartitionSpec as P

EPS = 1e-06
CH = 256
STEM = 192
PIX = 48
TL = 16
SLOTS = 3
LINE = SLOTS * TL
NZ = 16
F32 = jnp.float32
BF16 = jnp.bfloat16
MESH = pl.DeviceIdType.MESH
NT = (((1,), (1,)), ((), ()))
TN = (((0,), (0,)), ((), ()))
(
    LATENT,
    REWARD,
    PIXELS,
    UP_WEIGHT,
    UP_BIAS,
    NORM_GAIN,
    NORM_BIAS,
    OUT_WEIGHT,
    STEM_WEIGHT,
    STEM_BIAS,
    STEM_GAIN,
    TILE_COUNT,
    TILE_COLS,
    TAPS_TABLE,
    LANES_TABLE,
) = range(15)
OPERANDS = 15
STEM_LOADS = (PIXELS, STEM_WEIGHT, STEM_BIAS, REWARD, STEM_GAIN)
OTHER_LOADS = (
    TILE_COLS,
    TILE_COUNT,
    LATENT,
    UP_WEIGHT,
    UP_BIAS,
    NORM_GAIN,
    NORM_BIAS,
    OUT_WEIGHT,
    TAPS_TABLE,
    LANES_TABLE,
)
TAPS = {(0, 0): (0,), (0, 1): (1, 2), (1, 0): (0, 1), (1, 1): (2,)}


def out_taps():
    table = np.zeros((4, 128, 128), np.float32)
    for r in range(2):
        for s in range(2):
            for di in range(3):
                for dj in range(3):
                    for c in range(3):
                        for y in range(2):
                            for x in range(2):
                                a = r + 1 - (2 * (di - 1) + y)
                                e = s + 1 - (2 * (dj - 1) + x)
                                if 0 <= a < 3 and 0 <= e < 3:
                                    lane = (di * 3 + dj) * 12 + c * 4 + y * 2 + x
                                    table[r * 2 + s, lane, (a * 3 + e) * 8 + c] = 1
    return table.reshape(512, 128)


def cell_lanes():
    table = np.zeros((128, 2, 2, 128), np.float32)
    for c in range(3):
        for dy in range(4):
            for dx in range(4):
                for copy in range(9):
                    lane = copy * 12 + c * 4 + (dy % 2) * 2 + dx % 2
                    table[c * 16 + dy * 4 + dx, dx // 2, dy // 2, lane] = 1
    return table.reshape(128, 512)


def iota(shape, axis):
    return lax.broadcasted_iota(jnp.int32, shape, axis)


def dot(a, b):
    return jnp.dot(a, b, preferred_element_type=F32)


def three_rows(row):
    high = row.astype(BF16).astype(F32)
    rest = row - high
    middle = rest.astype(BF16).astype(F32)
    low = rest - middle
    at = iota((16, row.shape[1]), 0)
    rows = jnp.where(at == 0, high, jnp.where(at == 1, middle, jnp.where(at == 2, low, 0.0)))
    return rows.astype(BF16)


def kernel(nx, sections, *refs):
    operands, out, scratch = refs[:OPERANDS], refs[OPERANDS], refs[OPERANDS + 1 :]
    copies, scratch = scratch[:OPERANDS], scratch[OPERANDS:]
    (
        latent,
        reward,
        pixels,
        up_weight,
        up_bias,
        norm_gain,
        norm_bias,
        out_weight,
        stem_weight,
        stem_bias,
        stem_gain,
        tile_count,
        tile_cols,
        taps,
        lanes,
    ) = copies
    (
        wide,
        combined,
        out_matrix,
        out_rows,
        margin_send,
        margin_recv,
        image,
        x_recv,
        z_send,
        z_recv,
        preact,
        slopes,
        grads,
        zgrad,
        cells,
        own_grad,
        grad_send,
        grad_recv,
        groups,
        load_sem,
        msend_sem,
        mrecv_sem,
        xsend_sem,
        xrecv_sem,
        zsend_sem,
        zrecv_sem,
        gsend_sem,
        grecv_sem,
    ) = scratch
    tiles = nx * NZ
    blocks = sections * tiles
    section = lax.axis_index("section")
    tile = lax.axis_index("tile")
    mx = lax.div(tile, NZ)
    mz = lax.rem(tile, NZ)
    block = section * tiles + tile
    before = lax.rem(block + blocks - 1, blocks)
    after = lax.rem(block + 1, blocks)

    def device(index):
        return (lax.div(index, tiles), lax.rem(index, tiles))

    def along_x(index):
        return (section, index * NZ + mz)

    def along_z(index):
        return (section, mx * NZ + index)

    barrier = pltpu.get_barrier_semaphore()

    def greet(target):
        pl.semaphore_signal(barrier, inc=1, device_id=target, device_id_type=MESH)

    def load(n):
        return pltpu.make_async_copy(operands[n], copies[n], load_sem.at[n])

    for n in STEM_LOADS:
        load(n).start()

    def greet_z(d, carry):
        greet(along_z(lax.rem(mz + d, NZ)))
        return carry

    lax.fori_loop(1, NZ, greet_z, 0)
    for d in range(1, nx):
        greet(along_x(lax.rem(mx + d, nx)))
    greet(device(before))
    greet(device(after))
    for n in OTHER_LOADS:
        load(n).start()

    row_at = iota((CH, CH), 0)
    col_at = iota((CH, CH), 1)
    groups[...] = ((row_at >> 3) == (col_at >> 3)).astype(F32).astype(BF16)
    zeros = jnp.zeros((LINE, 4 * CH), BF16)
    zgrad[0:LINE, :] = zeros
    zgrad[17 * LINE : 18 * LINE, :] = zeros
    wide[0:LINE, :] = zeros[:, : 3 * CH]
    wide[17 * LINE : 18 * LINE, :] = zeros[:, : 3 * CH]
    out_rows[...] = jnp.zeros_like(out_rows)
    reorder = (col_at == ((row_at >> 2) & 3) * (NZ * 4) + (row_at >> 4) * 4 + (row_at & 3)).astype(
        F32
    ).astype(BF16)
    shift_low = ((col_at == row_at - 1) & ((row_at & 15) != 0)).astype(F32).astype(BF16)
    shift_high = ((col_at == row_at + 1) & ((row_at & 15) != 15)).astype(F32).astype(BF16)
    keep_before = block != 0
    keep_after = block != blocks - 1

    ones = jnp.ones((16, CH), BF16)

    def column_of(row):
        return lax.dot_general(three_rows(row), ones, TN, preferred_element_type=F32)

    for n in STEM_LOADS:
        load(n).wait()
    weight = stem_weight[...]
    stem = lax.dot_general(weight, pixels[...], TN, preferred_element_type=F32) + column_of(
        stem_bias[...]
    )
    centred = stem - jnp.mean(stem, axis=0, keepdims=True)
    inverse = lax.rsqrt(jnp.mean(centred * centred, axis=0, keepdims=True) + EPS)
    normed = centred * inverse
    scaled = reward[...].astype(F32) * column_of(stem_gain[...])
    stem_grad = (
        scaled
        - jnp.mean(scaled, axis=0, keepdims=True)
        - normed * jnp.mean(scaled * normed, axis=0, keepdims=True)
    ) * inverse
    padded_weight = jnp.concatenate([weight, jnp.zeros((128 - PIX, STEM), BF16)], axis=0)
    pixel_grad = dot(padded_weight, stem_grad.astype(BF16))
    image[...] = pixel_grad.T.astype(BF16).reshape(nx, NZ * 4, 128)
    x_recv[pl.ds(mx, 1)] = image[pl.ds(mx, 1)]

    pl.semaphore_wait(barrier, 2 + (nx - 1) + (NZ - 1))

    def x_copy(d, slot):
        target = lax.rem(mx + d, nx)
        return pltpu.make_async_remote_copy(
            src_ref=image.at[target],
            dst_ref=x_recv.at[slot],
            send_sem=xsend_sem.at[d - 1],
            recv_sem=xrecv_sem.at[d - 1],
            device_id=along_x(target),
            device_id_type=MESH,
        )

    for d in range(1, nx):
        x_copy(d, mx).start()

    at3 = iota((SLOTS, blocks), 1)
    at1 = iota((1, blocks), 1)
    for n in (TILE_COLS, TILE_COUNT, LATENT):
        load(n).wait()
    all_cols = tile_cols[...].astype(F32)
    all_counts = tile_count[...].astype(F32)

    def columns(index):
        return jnp.sum(jnp.where(at3 == index, all_cols, 0.0), axis=1, keepdims=True)

    def count(index):
        return jnp.sum(jnp.where(at1 == index, all_counts, 0.0), axis=1, keepdims=True)

    cols_own, cols_before, cols_after = columns(block), columns(before), columns(after)

    def slot_rows(cols, width):
        return jnp.concatenate(
            [jnp.broadcast_to(cols[k : k + 1, :], (TL, width)) for k in range(SLOTS)], axis=0
        )

    place = (iota((LINE, 128), 0) & 15).astype(F32)
    lane_f = iota((LINE, 128), 1).astype(F32)

    def gather_rows(cols):
        return (lane_f == slot_rows(cols, 128) + place).astype(F32)

    pick_own = gather_rows(cols_own)
    pick_up = jnp.concatenate([pick_own, gather_rows(cols_before)], axis=0).astype(BF16)
    pick_down = jnp.concatenate([pick_own, gather_rows(cols_after)], axis=0).astype(BF16)
    for r in range(8):
        side = r // 4
        rows = dot(pick_down if side else pick_up, latent[r]).astype(BF16)
        wide[(5 + r) * LINE : (6 + r) * LINE, CH : 2 * CH] = rows[0:LINE]
        margin_send[side, (r % 4) * LINE : (r % 4 + 1) * LINE, :] = rows[LINE : 2 * LINE]

    def margin_copy(side, target):
        return pltpu.make_async_remote_copy(
            src_ref=margin_send.at[side],
            dst_ref=margin_recv.at[1 - side],
            send_sem=msend_sem.at[side],
            recv_sem=mrecv_sem.at[1 - side],
            device_id=target,
            device_id_type=MESH,
        )

    margin_copy(0, device(before)).start()
    margin_copy(1, device(after)).start()

    load(UP_WEIGHT).wait()
    for r in range(2):
        for s in range(2):
            for t in range(2):
                for v in range(2):
                    total = None
                    for a in TAPS[r, t]:
                        for e in TAPS[s, v]:
                            term = up_weight[a, e].astype(F32)
                            total = term if total is None else total + term
                    at = (t * 2 + v) * CH
                    combined[r * 2 + s, at : at + CH, :] = total.astype(BF16)

    for n in (UP_BIAS, NORM_GAIN, NORM_BIAS, OUT_WEIGHT, TAPS_TABLE, LANES_TABLE):
        load(n).wait()
    for ae in range(9):
        out_rows[ae * 8 : ae * 8 + 3, :] = out_weight[ae].astype(F32)
    flat_taps = out_rows[...].astype(BF16)
    for ph in range(4):
        out_matrix[:, ph * CH : (ph + 1) * CH] = dot(
            taps[ph * 128 : (ph + 1) * 128, :], flat_taps
        ).astype(BF16)

    source = iota((1, 512), 1)
    source_row = source & 3
    source_x = (source >> 2) & 3
    source_z = (source >> 4) & 15
    cell_of = 2 * (source_x * NZ + source_z) + (source >> 8)
    source_key = (cell_of + 1000 * source_row).astype(F32)
    own_rows = slot_rows(cols_own, 512)
    place_wide = (iota((LINE, 512), 0) & 15).astype(F32)
    inside = (place_wide >= 4.0) & (place_wide < 12.0)
    choose = jnp.concatenate(
        [
            (jnp.where(inside, own_rows + place_wide + 1000.0 * pr, -1.0) == source_key)
            .astype(F32)
            .astype(BF16)
            for pr in range(4)
        ],
        axis=0,
    )

    lane = iota((128, 128), 1)
    column = iota((128, 128), 0).astype(F32)
    slot_of = lane >> 4
    offset_of = (lane & 15).astype(F32)

    def place_columns(cols, live, first_slot):
        start = jnp.where(
            slot_of == first_slot,
            jnp.broadcast_to(cols[0:1, :], (128, 128)),
            jnp.where(
                slot_of == first_slot + 1,
                jnp.broadcast_to(cols[1:2, :], (128, 128)),
                jnp.broadcast_to(cols[2:3, :], (128, 128)),
            ),
        )
        relative = (slot_of - first_slot).astype(F32)
        valid = (relative >= 0.0) & (relative < live) & (relative < float(SLOTS))
        return jnp.where(valid & (column == start + offset_of), 1.0, 0.0)

    none = jnp.zeros((1, 1), F32)
    own_place = place_columns(cols_own, count(block), 0)
    up_place = (
        own_place
        + place_columns(cols_before, jnp.where(keep_before, count(before), none), SLOTS)
    ).astype(BF16)
    down_place = (
        own_place + place_columns(cols_after, jnp.where(keep_after, count(after), none), SLOTS)
    ).astype(BF16)

    for d in range(1, nx):
        x_copy(d, lax.rem(mx + nx - d, nx)).wait_recv()
    by_z = dot(reorder, x_recv[...].reshape(nx * NZ * 4, 128)).astype(BF16)
    z_send[...] = by_z.reshape(NZ, nx * 4, 128)

    def z_copy(d, slot):
        target = lax.rem(mz + d, NZ)
        return pltpu.make_async_remote_copy(
            src_ref=z_send.at[target],
            dst_ref=z_recv.at[slot],
            send_sem=zsend_sem.at[d - 1],
            recv_sem=zrecv_sem.at[d - 1],
            device_id=along_z(target),
            device_id_type=MESH,
        )

    def z_start(n, carry):
        z_copy(1 + lax.rem(n + NZ // 2 - 1, NZ - 1), mz).start()
        return carry

    lax.fori_loop(0, NZ - 1, z_start, 0)
    z_recv[pl.ds(mz, 1)] = z_send[pl.ds(mz, 1)]

    margin_copy(0, device(before)).wait_recv()
    margin_copy(1, device(after)).wait_recv()
    top = margin_recv[0]
    bottom = margin_recv[1]
    wide[LINE : 5 * LINE, CH : 2 * CH] = jnp.where(keep_before, top, jnp.zeros_like(top))
    wide[13 * LINE : 17 * LINE, CH : 2 * CH] = jnp.where(
        keep_after, bottom, jnp.zeros_like(bottom)
    )
    for part in range(SLOTS):
        here = slice(LINE + part * CH, LINE + (part + 1) * CH)
        inputs = wide[here, CH : 2 * CH]
        wide[here, 0:CH] = dot(shift_low, inputs).astype(BF16)
        wide[here, 2 * CH : 3 * CH] = dot(shift_high, inputs).astype(BF16)

    bias = up_bias[...]
    total = jnp.zeros((LINE, CH), F32)
    for ph in range(4):
        r, s = ph // 2, ph % 2
        features = jnp.concatenate(
            [
                wide[(r + t) * LINE : (r + t + TL) * LINE, s * CH : (s + 2) * CH]
                for t in range(2)
            ],
            axis=1,
        )
        value = dot(features, combined[ph]) + bias
        preact[ph] = value
        total = total + jnp.sum(value.reshape(TL, LINE, CH), axis=0)

    def group_means(sums):
        rows = []
        for term in sums:
            high = term.astype(BF16).astype(F32)
            rest = term - high
            middle = rest.astype(BF16).astype(F32)
            rows += [high, middle, rest - middle]
        grouped = dot(jnp.concatenate(rows, axis=0).astype(BF16), groups[...])
        means = []
        for n in range(len(sums)):
            first = grouped[3 * n * LINE : (3 * n + 1) * LINE]
            second = grouped[(3 * n + 1) * LINE : (3 * n + 2) * LINE]
            third = grouped[(3 * n + 2) * LINE : (3 * n + 3) * LINE]
            line = (first + second + third) * (1.0 / 8192.0)
            means.append(
                jnp.concatenate(
                    [
                        jnp.broadcast_to(
                            jnp.sum(line[k * TL : (k + 1) * TL], axis=0, keepdims=True), (TL, CH)
                        )
                        for k in range(SLOTS)
                    ],
                    axis=0,
                )
            )
        return means

    (mean,) = group_means([total])

    def centre_rows(n, square):
        for step in range(4):
            at = pl.ds(pl.multiple_of((n * 4 + step) * LINE, LINE), LINE)
            for ph in range(4):
                off = preact[ph, at, :] - mean
                preact[ph, at, :] = off
                square = square + off * off
        return square

    square = lax.fori_loop(0, 4, centre_rows, jnp.zeros((LINE, CH), F32))
    (variance,) = group_means([square])
    inv = lax.rsqrt(variance + EPS)
    gain = jnp.broadcast_to(norm_gain[...], (LINE, CH))
    shift = jnp.broadcast_to(norm_bias[...], (LINE, CH))
    inv_gain = inv * gain

    def silu_slopes(n, carry):
        for ph in range(4):
            at = pl.ds(pl.multiple_of((n + 3) * LINE, LINE), LINE)
            value = preact[ph, at, :] * inv_gain + shift
            sigma = 0.5 * jnp.tanh(0.5 * value) + 0.5
            slopes[ph, pl.ds(pl.multiple_of(n * LINE, LINE), LINE), :] = (
                sigma * (1.0 + value * (1.0 - sigma)) * gain
            )
        return carry

    lax.fori_loop(0, 10, silu_slopes, 0)

    def z_wait(d, carry):
        z_copy(d, lax.rem(mz + NZ - d, NZ)).wait_recv()
        return carry

    lax.fori_loop(1, NZ, z_wait, 0)
    spread = dot(z_recv[...].reshape(NZ * nx * 4, 128), lanes[...]).astype(BF16)
    stacked = jnp.concatenate([spread[:, 0:256], spread[:, 256:512]], axis=0)
    found = dot(choose, stacked)
    lane_wide = iota((1, 256), 1) & 127
    copy_wide = sum([(lane_wide >= 12 * c).astype(jnp.int32) for c in range(1, 9)])
    col_wide = copy_wide - 3 * (
        (copy_wide >= 3).astype(jnp.int32) + (copy_wide >= 6).astype(jnp.int32)
    )
    copy_one = copy_wide[:, 0:128]
    low = pltpu.roll(found, 1, 0)
    high = pltpu.roll(found, 4 * LINE - 1, 0)
    merged = jnp.where(col_wide == 0, low, jnp.where(col_wide == 1, found, high))
    lines = []
    for pr in range(4):
        line = merged[pr * LINE : (pr + 1) * LINE]
        lines += [line[:, 0:128], line[:, 128:256]]
    nothing = jnp.zeros((LINE, 128), F32)

    def line_at(index):
        return lines[index] if 0 <= index < 8 else nothing

    for i in range(3, 13):
        around = jnp.where(
            copy_one < 3, line_at(i - 5), jnp.where(copy_one < 6, line_at(i - 4), line_at(i - 3))
        )
        cells[(i - 3) * LINE : (i - 2) * LINE, :] = around.astype(BF16)

    first = jnp.zeros((LINE, CH), F32)
    second = jnp.zeros((LINE, CH), F32)
    for ph in range(4):
        act = dot(cells[...], out_matrix[:, ph * CH : (ph + 1) * CH])
        for n in range(10):
            at = slice(n * LINE, (n + 1) * LINE)
            grad = act[at] * slopes[ph, at, :]
            grads[ph, at, :] = grad
            first = first + grad
            second = second + grad * preact[ph, (n + 3) * LINE : (n + 4) * LINE, :]
    first, second = group_means([first, second])
    offset = first * inv
    slope = second * inv * inv * inv

    def normal_grad(i):
        for ph in range(4):
            value = -offset - preact[ph, i * LINE : (i + 1) * LINE, :] * slope
            if 3 <= i < 13:
                value = value + grads[ph, (i - 3) * LINE : (i - 2) * LINE, :] * inv
            zgrad[(i + 1) * LINE : (i + 2) * LINE, ph * CH : (ph + 1) * CH] = value.astype(BF16)

    def input_grad(pieces):
        parts = []
        for pairs in (((0, 0),), ((0, 1), (1, 0)), ((1, 1),)):
            left, right = [], []
            for s, v in pairs:
                for r in range(2):
                    for t in range(2):
                        ph = r * 2 + s
                        rows = [
                            zgrad[
                                (i + 2 - r - t) * LINE : (i + 2 - r - t + lines_of) * LINE,
                                ph * CH : (ph + 1) * CH,
                            ]
                            for i, lines_of in pieces
                        ]
                        left.append(rows[0] if len(rows) == 1 else jnp.concatenate(rows, axis=0))
                        right.append(combined[ph, (t * 2 + v) * CH : (t * 2 + v + 1) * CH, :])
            parts.append(
                lax.dot_general(
                    jnp.concatenate(left, axis=1),
                    jnp.concatenate(right, axis=1),
                    NT,
                    preferred_element_type=F32,
                )
            )
        size = parts[0].shape[0]
        place_rows = iota((size, CH), 0) & 15
        return (
            parts[1]
            + jnp.where(place_rows < 15, pltpu.roll(parts[0], size - 1, 0), 0.0)
            + jnp.where(place_rows > 0, pltpu.roll(parts[2], 1, 0), 0.0)
        ).astype(BF16)

    def grad_copy(side, target):
        return pltpu.make_async_remote_copy(
            src_ref=grad_send.at[side],
            dst_ref=grad_recv.at[1 - side],
            send_sem=gsend_sem.at[side],
            recv_sem=grecv_sem.at[1 - side],
            device_id=target,
            device_id_type=MESH,
        )

    for i in (0, 1, 2, 3, 4, 11, 12, 13, 14, 15):
        normal_grad(i)
    margin_grad = input_grad(((0, 4), (12, 4)))
    grad_send[0] = margin_grad[0 : 4 * LINE]
    grad_send[1] = margin_grad[4 * LINE : 8 * LINE]
    grad_copy(0, device(before)).start()
    grad_copy(1, device(after)).start()
    for i in range(5, 11):
        normal_grad(i)
    own_grad[...] = input_grad(((4, 8),))

    grad_copy(0, device(before)).wait_recv()
    grad_copy(1, device(after)).wait_recv()
    rest = jnp.zeros((128 - 2 * LINE, CH), BF16)
    for r in range(8):
        side = r // 4
        at = (r % 4) * LINE
        terms = jnp.concatenate(
            [
                own_grad[r * LINE : (r + 1) * LINE, :],
                grad_recv[side, at : at + LINE, :],
                rest,
            ],
            axis=0,
        )
        out[r] = dot(down_place if side else up_place, terms).astype(BF16)

    margin_copy(0, device(before)).wait_send()
    margin_copy(1, device(after)).wait_send()
    for d in range(1, nx):
        x_copy(d, mx).wait_send()

    def z_sent(d, carry):
        z_copy(d, mz).wait_send()
        return carry

    lax.fori_loop(1, NZ, z_sent, 0)
    grad_copy(0, device(before)).wait_send()
    grad_copy(1, device(after)).wait_send()


def per_device(
    latent_feat,
    reward_grad,
    patches,
    up_weight,
    up_bias,
    norm_gain,
    norm_bias,
    out_weight,
    stem_weight,
    stem_bias,
    stem_gain,
    tile_count,
    tile_cols,
):
    sections = lax.axis_size("section")
    nx = lax.axis_size("tile") // NZ
    blocks = sections * nx * NZ
    operands = (
        latent_feat,
        reward_grad.reshape(-1, STEM).T,
        patches.T,
        up_weight,
        up_bias.reshape(1, CH),
        norm_gain.reshape(1, CH),
        norm_bias.reshape(1, CH),
        out_weight.transpose(0, 1, 3, 2).reshape(9, 3, CH),
        stem_weight,
        stem_bias.reshape(1, STEM),
        stem_gain.reshape(1, STEM),
        tile_count.reshape(1, blocks),
        tile_cols.T,
        jnp.asarray(out_taps(), BF16),
        jnp.asarray(cell_lanes(), BF16),
    )
    pinned = [pltpu.with_memory_space_constraint(array, pltpu.HBM) for array in operands]
    return pl.pallas_call(
        functools.partial(kernel, nx, sections),
        out_shape=pltpu.VMEM(latent_feat.shape, BF16),
        in_specs=[pl.BlockSpec(memory_space=pltpu.HBM)] * OPERANDS,
        out_specs=pl.BlockSpec(memory_space=pltpu.VMEM),
        scratch_shapes=[pltpu.VMEM(array.shape, array.dtype) for array in operands]
        + [
            pltpu.VMEM((18 * LINE, 3 * CH), BF16),
            pltpu.VMEM((4, 4 * CH, CH), BF16),
            pltpu.VMEM((128, 4 * CH), BF16),
            pltpu.VMEM((128, CH), F32),
            pltpu.VMEM((2, 4 * LINE, CH), BF16),
            pltpu.VMEM((2, 4 * LINE, CH), BF16),
            pltpu.VMEM((nx, NZ * 4, 128), BF16),
            pltpu.VMEM((nx, NZ * 4, 128), BF16),
            pltpu.VMEM((NZ, nx * 4, 128), BF16),
            pltpu.VMEM((NZ, nx * 4, 128), BF16),
            pltpu.VMEM((4, TL * LINE, CH), F32),
            pltpu.VMEM((4, 10 * LINE, CH), F32),
            pltpu.VMEM((4, 10 * LINE, CH), F32),
            pltpu.VMEM((18 * LINE, 4 * CH), BF16),
            pltpu.VMEM((10 * LINE, 128), BF16),
            pltpu.VMEM((8 * LINE, CH), BF16),
            pltpu.VMEM((2, 4 * LINE, CH), BF16),
            pltpu.VMEM((2, 4 * LINE, CH), BF16),
            pltpu.VMEM((CH, CH), BF16),
            pltpu.SemaphoreType.DMA((OPERANDS,)),
            pltpu.SemaphoreType.DMA((2,)),
            pltpu.SemaphoreType.DMA((2,)),
            pltpu.SemaphoreType.DMA((nx - 1,)),
            pltpu.SemaphoreType.DMA((nx - 1,)),
            pltpu.SemaphoreType.DMA((NZ - 1,)),
            pltpu.SemaphoreType.DMA((NZ - 1,)),
            pltpu.SemaphoreType.DMA((2,)),
            pltpu.SemaphoreType.DMA((2,)),
        ],
        compiler_params=pltpu.CompilerParams(
            collective_id=0, has_side_effects=True, vmem_limit_bytes=48 * 1024 * 1024
        ),
    )(*pinned)


def solution(mesh):
    return jax.shard_map(
        per_device,
        mesh=mesh,
        in_specs=(
            P(("section", "tile"), None, None),
            P("section", "tile", None),
            P("section", "tile"),
        )
        + (P(),) * 10,
        out_specs=P(("section", "tile"), None, None),
        check_vma=False,
    )
```

```python
import functools

import jax
import jax.numpy as jnp
import numpy as np
from jax import lax
from jax.experimental import pallas as pl
from jax.experimental.pallas import tpu as pltpu
from jax.sharding import PartitionSpec as P

EPS = 1e-06
CH = 256
STEM = 192
PIX = 48
TL = 16
SLOTS = 3
NZ = 16
LINE = SLOTS * TL
F32 = jnp.float32
BF16 = jnp.bfloat16
MESH = pl.DeviceIdType.MESH
NT = (((1,), (1,)), ((), ()))
TN = (((0,), (0,)), ((), ()))
(
    LATENT,
    REWARD,
    PIXELS,
    UP_WEIGHT,
    UP_BIAS,
    NORM_GAIN,
    NORM_BIAS,
    OUT_WEIGHT,
    STEM_WEIGHT,
    STEM_BIAS,
    STEM_GAIN,
    TILE_COUNT,
    TILE_COLS,
    TAPS_TABLE,
    LANES_TABLE,
) = range(15)
OPERANDS = 15
STEM_LOADS = (PIXELS, STEM_WEIGHT, STEM_BIAS, REWARD, STEM_GAIN)
EARLY_LOADS = (TILE_COLS, LATENT, UP_WEIGHT)
LATE_LOADS = (
    TILE_COUNT,
    OUT_WEIGHT,
    TAPS_TABLE,
    UP_BIAS,
    NORM_GAIN,
    NORM_BIAS,
    LANES_TABLE,
)
TAPS = {(0, 0): (0,), (0, 1): (1, 2), (1, 0): (0, 1), (1, 1): (2,)}


def out_taps():
    table = np.zeros((4, 128, 128), np.float32)
    for r in range(2):
        for s in range(2):
            for di in range(3):
                for dj in range(3):
                    for c in range(3):
                        for y in range(2):
                            for x in range(2):
                                a = r + 1 - (2 * (di - 1) + y)
                                e = s + 1 - (2 * (dj - 1) + x)
                                if 0 <= a < 3 and 0 <= e < 3:
                                    lane = (di * 3 + dj) * 12 + c * 4 + y * 2 + x
                                    table[r * 2 + s, lane, (a * 3 + e) * 8 + c] = 1
    return table.reshape(512, 128)


def cell_lanes():
    table = np.zeros((2, 64, 2, 2, 2, 128), np.float32)
    for odd in range(2):
        for c in range(3):
            for dy in range(4):
                for dx in range(4):
                    for copy in range(9):
                        lane = copy * 12 + c * 4 + (dy % 2) * 2 + dx % 2
                        table[odd, c * 16 + dy * 4 + dx, odd, dx // 2, dy // 2, lane] = 1
    return table.reshape(128, 1024)


def iota(shape, axis):
    return lax.broadcasted_iota(jnp.int32, shape, axis)


def dot(a, b):
    return jnp.dot(a, b, preferred_element_type=F32)


def three_rows(row):
    high = row.astype(BF16).astype(F32)
    rest = row - high
    middle = rest.astype(BF16).astype(F32)
    low = rest - middle
    at = iota((16, row.shape[1]), 0)
    rows = jnp.where(at == 0, high, jnp.where(at == 1, middle, jnp.where(at == 2, low, 0.0)))
    return rows.astype(BF16)


def kernel(nx, sections, *refs):
    operands, out, scratch = refs[:OPERANDS], refs[OPERANDS], refs[OPERANDS + 1 :]
    copies, scratch = scratch[:OPERANDS], scratch[OPERANDS:]
    (
        latent,
        reward,
        pixels,
        up_weight,
        up_bias,
        norm_gain,
        norm_bias,
        out_weight,
        stem_weight,
        stem_bias,
        stem_gain,
        tile_count,
        tile_cols,
        taps,
        lanes,
    ) = copies
    (
        wide,
        combined,
        out_matrix,
        out_rows,
        margin_send,
        margin_recv,
        image,
        x_send,
        x_recv,
        z_send,
        z_recv,
        preact,
        slopes,
        grads,
        zgrad,
        cells,
        own_grad,
        grad_send,
        grad_recv,
        groups,
        load_sem,
        msend_sem,
        mrecv_sem,
        xsend_sem,
        xrecv_sem,
        zsend_sem,
        zrecv_sem,
        gsend_sem,
        grecv_sem,
    ) = scratch
    tiles = nx * NZ
    blocks = sections * tiles
    section = lax.axis_index("section")
    tile = lax.axis_index("tile")
    mx = lax.div(tile, NZ)
    mz = lax.rem(tile, NZ)
    block = section * tiles + tile
    before = lax.rem(block + blocks - 1, blocks)
    after = lax.rem(block + 1, blocks)

    def device(index):
        return (lax.div(index, tiles), lax.rem(index, tiles))

    def along_x(index):
        return (section, index * NZ + mz)

    def along_z(index):
        return (section, mx * NZ + index)

    barrier = pltpu.get_barrier_semaphore()

    def greet(target):
        pl.semaphore_signal(barrier, inc=1, device_id=target, device_id_type=MESH)

    def load(n):
        return pltpu.make_async_copy(operands[n], copies[n], load_sem.at[n])

    for n in STEM_LOADS + EARLY_LOADS:
        load(n).start()

    def greet_z(d, carry):
        greet(along_z(lax.rem(mz + d, NZ)))
        return carry

    lax.fori_loop(1, NZ, greet_z, 0)
    for d in range(1, nx):
        greet(along_x(lax.rem(mx + d, nx)))
    greet(device(before))
    greet(device(after))

    row_at = iota((CH, CH), 0)
    col_at = iota((CH, CH), 1)
    groups[...] = ((row_at >> 3) == (col_at >> 3)).astype(F32).astype(BF16)
    zeros = jnp.zeros((LINE, 4 * CH), BF16)
    zgrad[0:LINE, :] = zeros
    zgrad[17 * LINE : 18 * LINE, :] = zeros
    wide[0:LINE, :] = zeros[:, : 3 * CH]
    wide[17 * LINE : 18 * LINE, :] = zeros[:, : 3 * CH]
    out_rows[...] = jnp.zeros_like(out_rows)
    to_row = iota((128, 128), 0)
    reorder = (
        iota((128, 128), 1) == ((to_row >> 1) & 3) * (2 * NZ) + (to_row & 1) * NZ + (to_row >> 3)
    ).astype(F32).astype(BF16)
    shift_low = ((col_at == row_at - 1) & ((row_at & 15) != 0)).astype(F32).astype(BF16)
    shift_high = ((col_at == row_at + 1) & ((row_at & 15) != 15)).astype(F32).astype(BF16)
    keep_before = block != 0
    keep_after = block != blocks - 1

    ones = jnp.ones((16, CH), BF16)

    def column_of(row):
        return lax.dot_general(three_rows(row), ones, TN, preferred_element_type=F32)

    for n in STEM_LOADS:
        load(n).wait()
    weight = stem_weight[...]
    stem = lax.dot_general(weight, pixels[...], TN, preferred_element_type=F32) + column_of(
        stem_bias[...]
    )
    scaled = reward[...].astype(F32) * column_of(stem_gain[...])
    centred = stem - jnp.mean(stem, axis=0, keepdims=True)
    scaled = scaled - jnp.mean(scaled, axis=0, keepdims=True)
    inverse = lax.rsqrt(jnp.mean(centred * centred, axis=0, keepdims=True) + EPS)
    along = jnp.mean(scaled * centred, axis=0, keepdims=True) * inverse * inverse
    stem_grad = (scaled - centred * along) * inverse
    padded_weight = jnp.concatenate([weight, jnp.zeros((128 - PIX, STEM), BF16)], axis=0)
    pixel_grad = dot(padded_weight, stem_grad.astype(BF16))
    image[...] = pixel_grad.astype(BF16).astype(F32).T
    left_half = iota((tiles, 128), 1) < 64
    for h in range(2):
        even, odd = [image[pl.ds(2 * h + n, tiles, stride=4), :] for n in range(2)]
        both = jnp.where(left_half, even, pltpu.roll(odd, 64, 1)).astype(BF16)
        x_send[:, h * NZ : (h + 1) * NZ, :] = both.reshape(nx, NZ, 128)
    x_recv[pl.ds(mx, 1)] = x_send[pl.ds(mx, 1)]

    pl.semaphore_wait(barrier, 2 + (nx - 1) + (NZ - 1))

    def x_copy(d, slot):
        target = lax.rem(mx + d, nx)
        return pltpu.make_async_remote_copy(
            src_ref=x_send.at[target],
            dst_ref=x_recv.at[slot],
            send_sem=xsend_sem.at[d - 1],
            recv_sem=xrecv_sem.at[d - 1],
            device_id=along_x(target),
            device_id_type=MESH,
        )

    for d in range(1, nx):
        x_copy(d, mx).start()
    for n in LATE_LOADS:
        load(n).start()

    at3 = iota((SLOTS, blocks), 1)
    at1 = iota((1, blocks), 1)
    for n in (TILE_COLS, LATENT):
        load(n).wait()
    all_cols = tile_cols[...].astype(F32)

    def columns(index):
        return jnp.sum(jnp.where(at3 == index, all_cols, 0.0), axis=1, keepdims=True)

    def count(index):
        counts = tile_count[...].astype(F32)
        return jnp.sum(jnp.where(at1 == index, counts, 0.0), axis=1, keepdims=True)

    cols_own, cols_before, cols_after = columns(block), columns(before), columns(after)

    def slot_rows(cols, width):
        return jnp.concatenate(
            [jnp.broadcast_to(cols[k : k + 1, :], (TL, width)) for k in range(SLOTS)], axis=0
        )

    place = (iota((LINE, 128), 0) & 15).astype(F32)
    lane_f = iota((LINE, 128), 1).astype(F32)

    def gather_rows(cols):
        return (lane_f == slot_rows(cols, 128) + place).astype(F32)

    pick_own = gather_rows(cols_own)
    pick_up = jnp.concatenate([pick_own, gather_rows(cols_before)], axis=0).astype(BF16)
    pick_down = jnp.concatenate([pick_own, gather_rows(cols_after)], axis=0).astype(BF16)
    for r in range(8):
        side = r // 4
        rows = dot(pick_down if side else pick_up, latent[r]).astype(BF16)
        wide[(5 + r) * LINE : (6 + r) * LINE, CH : 2 * CH] = rows[0:LINE]
        margin_send[side, (r % 4) * LINE : (r % 4 + 1) * LINE, :] = rows[LINE : 2 * LINE]

    def margin_copy(side, target):
        return pltpu.make_async_remote_copy(
            src_ref=margin_send.at[side],
            dst_ref=margin_recv.at[1 - side],
            send_sem=msend_sem.at[side],
            recv_sem=mrecv_sem.at[1 - side],
            device_id=target,
            device_id_type=MESH,
        )

    margin_copy(0, device(before)).start()
    margin_copy(1, device(after)).start()

    load(UP_WEIGHT).wait()
    for r in range(2):
        for s in range(2):
            for t in range(2):
                for v in range(2):
                    total = None
                    for a in TAPS[r, t]:
                        for e in TAPS[s, v]:
                            term = up_weight[a, e].astype(F32)
                            total = term if total is None else total + term
                    at = (t * 2 + v) * CH
                    combined[r * 2 + s, at : at + CH, :] = total.astype(BF16)

    for n in (TILE_COUNT, UP_BIAS, NORM_GAIN, NORM_BIAS, OUT_WEIGHT, TAPS_TABLE, LANES_TABLE):
        load(n).wait()
    for ae in range(9):
        out_rows[ae * 8 : ae * 8 + 3, :] = out_weight[ae].astype(F32)
    flat_taps = out_rows[...].astype(BF16)
    for ph in range(4):
        out_matrix[:, ph * CH : (ph + 1) * CH] = dot(
            taps[ph * 128 : (ph + 1) * 128, :], flat_taps
        ).astype(BF16)

    source = iota((1, 512), 1)
    source_x, source_z = (source >> 1) & 3, (source >> 3) & 15
    source_row = 2 * (source & 1) + (source >> 8)
    cell_of = 2 * (source_x * NZ + source_z) + ((source >> 7) & 1)
    source_key = (cell_of + 1000 * source_row).astype(F32)
    own_rows = slot_rows(cols_own, 512)
    place_wide = (iota((LINE, 512), 0) & 15).astype(F32)
    inside = (place_wide >= 4.0) & (place_wide < 12.0)
    choose = jnp.concatenate(
        [
            (jnp.where(inside, own_rows + place_wide + 1000.0 * pr, -1.0) == source_key)
            .astype(F32)
            .astype(BF16)
            for pr in range(4)
        ],
        axis=0,
    )

    lane = iota((128, 128), 1)
    column = iota((128, 128), 0).astype(F32)
    slot_of = lane >> 4
    offset_of = (lane & 15).astype(F32)

    def place_columns(cols, live, first_slot):
        start = jnp.where(
            slot_of == first_slot,
            jnp.broadcast_to(cols[0:1, :], (128, 128)),
            jnp.where(
                slot_of == first_slot + 1,
                jnp.broadcast_to(cols[1:2, :], (128, 128)),
                jnp.broadcast_to(cols[2:3, :], (128, 128)),
            ),
        )
        relative = (slot_of - first_slot).astype(F32)
        valid = (relative >= 0.0) & (relative < live) & (relative < float(SLOTS))
        return jnp.where(valid & (column == start + offset_of), 1.0, 0.0)

    none = jnp.zeros((1, 1), F32)
    own_place = place_columns(cols_own, count(block), 0)
    up_place = (
        own_place
        + place_columns(cols_before, jnp.where(keep_before, count(before), none), SLOTS)
    ).astype(BF16)
    down_place = (
        own_place + place_columns(cols_after, jnp.where(keep_after, count(after), none), SLOTS)
    ).astype(BF16)

    for d in range(1, nx):
        x_copy(d, lax.rem(mx + nx - d, nx)).wait_recv()
    by_z = dot(reorder, x_recv[...].reshape(2 * tiles, 128))
    z_send[...] = by_z.reshape(NZ, 2 * nx, 128).astype(BF16)

    def z_copy(far, slot):
        target = lax.rem(mz + far, NZ)
        return pltpu.make_async_remote_copy(
            src_ref=z_send.at[target],
            dst_ref=z_recv.at[slot],
            send_sem=zsend_sem,
            recv_sem=zrecv_sem,
            device_id=along_z(target),
            device_id_type=MESH,
        )

    def z_start(n, carry):
        z_copy(NZ // 2 + (1 - 2 * lax.rem(n, 2)) * lax.div(n + 1, 2), mz).start()
        return carry

    lax.fori_loop(0, NZ - 1, z_start, 0)
    z_recv[pl.ds(mz, 1)] = z_send[pl.ds(mz, 1)]

    margin_copy(0, device(before)).wait_recv()
    margin_copy(1, device(after)).wait_recv()
    top = margin_recv[0]
    bottom = margin_recv[1]
    wide[LINE : 5 * LINE, CH : 2 * CH] = jnp.where(keep_before, top, jnp.zeros_like(top))
    wide[13 * LINE : 17 * LINE, CH : 2 * CH] = jnp.where(
        keep_after, bottom, jnp.zeros_like(bottom)
    )
    for part in range(SLOTS):
        here = slice(LINE + part * CH, LINE + (part + 1) * CH)
        inputs = wide[here, CH : 2 * CH]
        wide[here, 0:CH] = dot(shift_low, inputs).astype(BF16)
        wide[here, 2 * CH : 3 * CH] = dot(shift_high, inputs).astype(BF16)

    bias = up_bias[...]
    total = jnp.zeros((LINE, CH), F32)
    for ph in range(4):
        r, s = ph // 2, ph % 2
        features = jnp.concatenate(
            [
                wide[(r + t) * LINE : (r + t + TL) * LINE, s * CH : (s + 2) * CH]
                for t in range(2)
            ],
            axis=1,
        )
        value = dot(features, combined[ph]) + bias
        preact[ph] = value
        total = total + jnp.sum(value.reshape(TL, LINE, CH), axis=0)

    def group_means(sums):
        rows = []
        for term in sums:
            high = term.astype(BF16).astype(F32)
            rest = term - high
            middle = rest.astype(BF16).astype(F32)
            rows += [high, middle, rest - middle]
        grouped = dot(jnp.concatenate(rows, axis=0).astype(BF16), groups[...])
        means = []
        for n in range(len(sums)):
            first = grouped[3 * n * LINE : (3 * n + 1) * LINE]
            second = grouped[(3 * n + 1) * LINE : (3 * n + 2) * LINE]
            third = grouped[(3 * n + 2) * LINE : (3 * n + 3) * LINE]
            line = (first + second + third) * (1.0 / 8192.0)
            means.append(
                jnp.concatenate(
                    [
                        jnp.broadcast_to(
                            jnp.sum(line[k * TL : (k + 1) * TL], axis=0, keepdims=True), (TL, CH)
                        )
                        for k in range(SLOTS)
                    ],
                    axis=0,
                )
            )
        return means

    (mean,) = group_means([total])

    def centre_rows(n, square):
        for step in range(4):
            at = pl.ds(pl.multiple_of((n * 4 + step) * LINE, LINE), LINE)
            for ph in range(4):
                off = preact[ph, at, :] - mean
                preact[ph, at, :] = off
                square = square + off * off
        return square

    square = lax.fori_loop(0, 4, centre_rows, jnp.zeros((LINE, CH), F32))
    (variance,) = group_means([square])
    inv = lax.rsqrt(variance + EPS)
    gain = jnp.broadcast_to(norm_gain[...], (LINE, CH))
    shift = jnp.broadcast_to(norm_bias[...], (LINE, CH))
    inv_gain = inv * gain

    def silu_slopes(n, carry):
        for ph in range(4):
            at = pl.ds(pl.multiple_of((n + 3) * LINE, LINE), LINE)
            value = preact[ph, at, :] * inv_gain + shift
            sigma = 0.5 * jnp.tanh(0.5 * value) + 0.5
            slopes[ph, pl.ds(pl.multiple_of(n * LINE, LINE), LINE), :] = (
                sigma * (1.0 + value * (1.0 - sigma)) * gain
            )
        return carry

    lax.fori_loop(0, 10, silu_slopes, 0)

    others = pl.ds(0, NZ - 1)
    pltpu.make_async_copy(z_recv.at[others], z_recv.at[others], zrecv_sem).wait()
    arrived = z_recv[...].astype(F32).reshape(2 * tiles, 128).astype(BF16)
    spread = dot(arrived, lanes[...]).astype(BF16)
    stacked = jnp.concatenate([spread[:, 256 * n : 256 * (n + 1)] for n in range(4)], axis=0)
    found = dot(choose, stacked)
    lane_wide = iota((1, 256), 1) & 127
    copy_wide = sum([(lane_wide >= 12 * c).astype(jnp.int32) for c in range(1, 9)])
    col_wide = copy_wide - 3 * (
        (copy_wide >= 3).astype(jnp.int32) + (copy_wide >= 6).astype(jnp.int32)
    )
    copy_one = copy_wide[:, 0:128]
    low = pltpu.roll(found, 1, 0)
    high = pltpu.roll(found, 4 * LINE - 1, 0)
    merged = jnp.where(col_wide == 0, low, jnp.where(col_wide == 1, found, high))
    lines = []
    for pr in range(4):
        line = merged[pr * LINE : (pr + 1) * LINE]
        lines += [line[:, 0:128], line[:, 128:256]]
    nothing = jnp.zeros((LINE, 128), F32)

    def line_at(index):
        return lines[index] if 0 <= index < 8 else nothing

    for i in range(3, 13):
        around = jnp.where(
            copy_one < 3, line_at(i - 5), jnp.where(copy_one < 6, line_at(i - 4), line_at(i - 3))
        )
        cells[(i - 3) * LINE : (i - 2) * LINE, :] = around.astype(BF16)

    first = jnp.zeros((LINE, CH), F32)
    second = jnp.zeros((LINE, CH), F32)
    for ph in range(4):
        act = dot(cells[...], out_matrix[:, ph * CH : (ph + 1) * CH])
        for n in range(10):
            at = slice(n * LINE, (n + 1) * LINE)
            grad = act[at] * slopes[ph, at, :]
            grads[ph, at, :] = grad
            first = first + grad
            second = second + grad * preact[ph, (n + 3) * LINE : (n + 4) * LINE, :]
    first, second = group_means([first, second])
    offset = first * inv
    slope = second * inv * inv * inv

    def normal_grad(i):
        for ph in range(4):
            value = -offset - preact[ph, i * LINE : (i + 1) * LINE, :] * slope
            if 3 <= i < 13:
                value = value + grads[ph, (i - 3) * LINE : (i - 2) * LINE, :] * inv
            zgrad[(i + 1) * LINE : (i + 2) * LINE, ph * CH : (ph + 1) * CH] = value.astype(BF16)

    def input_grad(pieces):
        parts = []
        for pairs in (((0, 0),), ((0, 1), (1, 0)), ((1, 1),)):
            left, right = [], []
            for s, v in pairs:
                for r in range(2):
                    for t in range(2):
                        ph = r * 2 + s
                        rows = [
                            zgrad[
                                (i + 2 - r - t) * LINE : (i + 2 - r - t + lines_of) * LINE,
                                ph * CH : (ph + 1) * CH,
                            ]
                            for i, lines_of in pieces
                        ]
                        left.append(rows[0] if len(rows) == 1 else jnp.concatenate(rows, axis=0))
                        right.append(combined[ph, (t * 2 + v) * CH : (t * 2 + v + 1) * CH, :])
            parts.append(
                lax.dot_general(
                    jnp.concatenate(left, axis=1),
                    jnp.concatenate(right, axis=1),
                    NT,
                    preferred_element_type=F32,
                )
            )
        size = parts[0].shape[0]
        place_rows = iota((size, CH), 0) & 15
        return (
            parts[1]
            + jnp.where(place_rows < 15, pltpu.roll(parts[0], size - 1, 0), 0.0)
            + jnp.where(place_rows > 0, pltpu.roll(parts[2], 1, 0), 0.0)
        ).astype(BF16)

    def grad_copy(side, target):
        return pltpu.make_async_remote_copy(
            src_ref=grad_send.at[side],
            dst_ref=grad_recv.at[1 - side],
            send_sem=gsend_sem.at[side],
            recv_sem=grecv_sem.at[1 - side],
            device_id=target,
            device_id_type=MESH,
        )

    for i in (0, 1, 2, 3, 4, 11, 12, 13, 14, 15):
        normal_grad(i)
    margin_grad = input_grad(((0, 4), (12, 4)))
    grad_send[0] = margin_grad[0 : 4 * LINE]
    grad_send[1] = margin_grad[4 * LINE : 8 * LINE]
    grad_copy(0, device(before)).start()
    grad_copy(1, device(after)).start()
    for i in range(5, 11):
        normal_grad(i)
    own_grad[...] = input_grad(((4, 8),))

    grad_copy(0, device(before)).wait_recv()
    grad_copy(1, device(after)).wait_recv()
    rest = jnp.zeros((128 - 2 * LINE, CH), BF16)
    for r in range(8):
        side = r // 4
        at = (r % 4) * LINE
        terms = jnp.concatenate(
            [
                own_grad[r * LINE : (r + 1) * LINE, :],
                grad_recv[side, at : at + LINE, :],
                rest,
            ],
            axis=0,
        )
        out[r] = dot(down_place if side else up_place, terms).astype(BF16)

    margin_copy(0, device(before)).wait_send()
    margin_copy(1, device(after)).wait_send()
    for d in range(1, nx):
        x_copy(d, mx).wait_send()
    pltpu.make_async_copy(z_send.at[others], z_send.at[others], zsend_sem).wait()
    grad_copy(0, device(before)).wait_send()
    grad_copy(1, device(after)).wait_send()


def per_device(
    latent_feat,
    reward_grad,
    patches,
    up_weight,
    up_bias,
    norm_gain,
    norm_bias,
    out_weight,
    stem_weight,
    stem_bias,
    stem_gain,
    tile_count,
    tile_cols,
):
    sections = lax.axis_size("section")
    nx = lax.axis_size("tile") // NZ
    blocks = sections * nx * NZ
    operands = (
        latent_feat,
        reward_grad.reshape(-1, STEM).T,
        patches.T,
        up_weight,
        up_bias.reshape(1, CH),
        norm_gain.reshape(1, CH),
        norm_bias.reshape(1, CH),
        out_weight.transpose(0, 1, 3, 2).reshape(9, 3, CH),
        stem_weight,
        stem_bias.reshape(1, STEM),
        stem_gain.reshape(1, STEM),
        tile_count.reshape(1, blocks),
        tile_cols.T,
        jnp.asarray(out_taps(), BF16),
        jnp.asarray(cell_lanes(), BF16),
    )
    pinned = [pltpu.with_memory_space_constraint(array, pltpu.HBM) for array in operands]
    return pl.pallas_call(
        functools.partial(kernel, nx, sections),
        out_shape=pltpu.VMEM(latent_feat.shape, BF16),
        in_specs=[pl.BlockSpec(memory_space=pltpu.HBM)] * OPERANDS,
        out_specs=pl.BlockSpec(memory_space=pltpu.VMEM),
        scratch_shapes=[pltpu.VMEM(array.shape, array.dtype) for array in operands]
        + [
            pltpu.VMEM((18 * LINE, 3 * CH), BF16),
            pltpu.VMEM((4, 4 * CH, CH), BF16),
            pltpu.VMEM((128, 4 * CH), BF16),
            pltpu.VMEM((128, CH), F32),
            pltpu.VMEM((2, 4 * LINE, CH), BF16),
            pltpu.VMEM((2, 4 * LINE, CH), BF16),
            pltpu.VMEM((4 * nx * NZ, 128), F32),
            pltpu.VMEM((nx, 2 * NZ, 128), BF16),
            pltpu.VMEM((nx, 2 * NZ, 128), BF16),
            pltpu.VMEM((NZ, 2 * nx, 128), BF16),
            pltpu.VMEM((NZ, 2 * nx, 128), BF16),
            pltpu.VMEM((4, TL * LINE, CH), F32),
            pltpu.VMEM((4, 10 * LINE, CH), F32),
            pltpu.VMEM((4, 10 * LINE, CH), F32),
            pltpu.VMEM((18 * LINE, 4 * CH), BF16),
            pltpu.VMEM((10 * LINE, 128), BF16),
            pltpu.VMEM((8 * LINE, CH), BF16),
            pltpu.VMEM((2, 4 * LINE, CH), BF16),
            pltpu.VMEM((2, 4 * LINE, CH), BF16),
            pltpu.VMEM((CH, CH), BF16),
            pltpu.SemaphoreType.DMA((OPERANDS,)),
            pltpu.SemaphoreType.DMA((2,)),
            pltpu.SemaphoreType.DMA((2,)),
            pltpu.SemaphoreType.DMA((nx - 1,)),
            pltpu.SemaphoreType.DMA((nx - 1,)),
            pltpu.SemaphoreType.DMA,
            pltpu.SemaphoreType.DMA,
            pltpu.SemaphoreType.DMA((2,)),
            pltpu.SemaphoreType.DMA((2,)),
        ],
        compiler_params=pltpu.CompilerParams(
            collective_id=0, has_side_effects=True, vmem_limit_bytes=48 * 1024 * 1024
        ),
    )(*pinned)


def solution(mesh):
    return jax.shard_map(
        per_device,
        mesh=mesh,
        in_specs=(
            P(("section", "tile"), None, None),
            P("section", "tile", None),
            P("section", "tile"),
        )
        + (P(),) * 10,
        out_specs=P(("section", "tile"), None, None),
        check_vma=False,
    )
```

```python
import functools

import jax
import jax.numpy as jnp
import numpy as np
from jax import lax
from jax.experimental import pallas as pl
from jax.experimental.pallas import tpu as pltpu
from jax.sharding import PartitionSpec as P

EPS = 1e-06
CH = 256
STEM = 192
PIX = 48
TL = 16
SLOTS = 3
NZ = 16
LINE = SLOTS * TL
F32 = jnp.float32
BF16 = jnp.bfloat16
MESH = pl.DeviceIdType.MESH
NT = (((1,), (1,)), ((), ()))
TN = (((0,), (0,)), ((), ()))
(
    LATENT,
    REWARD,
    PIXELS,
    UP_WEIGHT,
    UP_BIAS,
    NORM_GAIN,
    NORM_BIAS,
    OUT_WEIGHT,
    STEM_WEIGHT,
    STEM_BIAS,
    STEM_GAIN,
    TILE_COUNT,
    TILE_COLS,
    TAPS_TABLE,
    LANES_TABLE,
) = range(15)
OPERANDS = 15
STEM_LOADS = (PIXELS, STEM_WEIGHT, STEM_BIAS, REWARD, STEM_GAIN)
EARLY_LOADS = (TILE_COLS, LATENT, UP_WEIGHT)
LATE_LOADS = (
    TILE_COUNT,
    OUT_WEIGHT,
    TAPS_TABLE,
    UP_BIAS,
    NORM_GAIN,
    NORM_BIAS,
    LANES_TABLE,
)
TAPS = ((0, 0), (0, 1), (1, 0), (1, 1))


def out_taps():
    table = np.zeros((4, 128, 128), np.float32)
    for r in range(2):
        for s in range(2):
            for di in range(3):
                for dj in range(3):
                    for c in range(3):
                        for y in range(2):
                            for x in range(2):
                                a = r + 1 - (2 * (di - 1) + y)
                                e = s + 1 - (2 * (dj - 1) + x)
                                if 0 <= a < 3 and 0 <= e < 3:
                                    lane = (di * 3 + dj) * 12 + c * 4 + y * 2 + x
                                    table[r * 2 + s, lane, (a * 3 + e) * 8 + c] = 1
    return table.reshape(512, 128)


def cell_lanes():
    table = np.zeros((2, 64, 2, 2, 2, 128), np.float32)
    for odd in range(2):
        for c in range(3):
            for dy in range(4):
                for dx in range(4):
                    for copy in range(9):
                        lane = copy * 12 + c * 4 + (dy % 2) * 2 + dx % 2
                        table[odd, c * 16 + dy * 4 + dx, odd, dx // 2, dy // 2, lane] = 1
    return table.reshape(128, 1024)


def iota(shape, axis):
    return lax.broadcasted_iota(jnp.int32, shape, axis)


def dot(a, b):
    return jnp.dot(a, b, preferred_element_type=F32)


def three_rows(row):
    high = row.astype(BF16).astype(F32)
    rest = row - high
    middle = rest.astype(BF16).astype(F32)
    low = rest - middle
    at = iota((16, row.shape[1]), 0)
    rows = jnp.where(at == 0, high, jnp.where(at == 1, middle, jnp.where(at == 2, low, 0.0)))
    return rows.astype(BF16)


def kernel(nx, sections, *refs):
    operands, out, scratch = refs[:OPERANDS], refs[OPERANDS], refs[OPERANDS + 1 :]
    copies, scratch = scratch[:OPERANDS], scratch[OPERANDS:]
    (
        latent,
        reward,
        pixels,
        up_weight,
        up_bias,
        norm_gain,
        norm_bias,
        out_weight,
        stem_weight,
        stem_bias,
        stem_gain,
        tile_count,
        tile_cols,
        taps,
        lanes,
    ) = copies
    (
        wide,
        combined,
        out_matrix,
        out_rows,
        margin_send,
        margin_recv,
        image,
        x_send,
        x_recv,
        z_send,
        z_recv,
        preact,
        slopes,
        grads,
        zgrad,
        cells,
        own_grad,
        grad_send,
        grad_recv,
        groups,
        load_sem,
        msend_sem,
        mrecv_sem,
        xsend_sem,
        xrecv_sem,
        zsend_sem,
        zrecv_sem,
        gsend_sem,
        grecv_sem,
    ) = scratch
    tiles = nx * NZ
    blocks = sections * tiles
    section = lax.axis_index("section")
    tile = lax.axis_index("tile")
    mx = lax.div(tile, NZ)
    mz = lax.rem(tile, NZ)
    block = section * tiles + tile
    before = lax.rem(block + blocks - 1, blocks)
    after = lax.rem(block + 1, blocks)

    def device(index):
        return (lax.div(index, tiles), lax.rem(index, tiles))

    def along_x(index):
        return (section, index * NZ + mz)

    def along_z(index):
        return (section, mx * NZ + index)

    barrier = pltpu.get_barrier_semaphore()

    def greet(target):
        pl.semaphore_signal(barrier, inc=1, device_id=target, device_id_type=MESH)

    def load(n):
        return pltpu.make_async_copy(operands[n], copies[n], load_sem.at[n])

    for n in STEM_LOADS + EARLY_LOADS:
        load(n).start()

    for d in range(1, NZ):
        greet(along_z(lax.rem(mz + d, NZ)))
    for d in range(1, nx):
        greet(along_x(lax.rem(mx + d, nx)))
    greet(device(before))
    greet(device(after))

    row_at = iota((CH, CH), 0)
    col_at = iota((CH, CH), 1)
    groups[...] = ((row_at >> 3) == (col_at >> 3)).astype(F32).astype(BF16)
    zeros = jnp.zeros((LINE, 4 * CH), BF16)
    zgrad[0:LINE, :] = zeros
    zgrad[17 * LINE : 18 * LINE, :] = zeros
    wide[0:LINE, :] = zeros[:, : 3 * CH]
    wide[17 * LINE : 18 * LINE, :] = zeros[:, : 3 * CH]
    out_rows[...] = jnp.zeros_like(out_rows)
    to_row = iota((128, 128), 0)
    reorder = (
        iota((128, 128), 1) == ((to_row >> 1) & 3) * (2 * NZ) + (to_row & 1) * NZ + (to_row >> 3)
    ).astype(F32).astype(BF16)
    shift_low = ((col_at == row_at - 1) & ((row_at & 15) != 0)).astype(F32).astype(BF16)
    shift_high = ((col_at == row_at + 1) & ((row_at & 15) != 15)).astype(F32).astype(BF16)
    keep_before = block != 0
    keep_after = block != blocks - 1

    ones = jnp.ones((16, CH), BF16)

    def column_of(row):
        return lax.dot_general(three_rows(row), ones, TN, preferred_element_type=F32)

    for n in STEM_LOADS:
        load(n).wait()
    weight = stem_weight[...]
    stem = lax.dot_general(weight, pixels[...], TN, preferred_element_type=F32) + column_of(
        stem_bias[...]
    )
    scaled = reward[...].astype(F32) * column_of(stem_gain[...])
    centred = stem - jnp.mean(stem, axis=0, keepdims=True)
    scaled = scaled - jnp.mean(scaled, axis=0, keepdims=True)
    inverse = lax.rsqrt(jnp.mean(centred * centred, axis=0, keepdims=True) + EPS)
    along = jnp.mean(scaled * centred, axis=0, keepdims=True) * inverse * inverse
    stem_grad = (scaled - centred * along) * inverse
    padded_weight = jnp.concatenate([weight, jnp.zeros((128 - PIX, STEM), BF16)], axis=0)
    pixel_grad = dot(padded_weight, stem_grad.astype(BF16))
    image[...] = pixel_grad.astype(BF16).astype(F32).T
    left_half = iota((tiles, 128), 1) < 64
    for h in range(2):
        even, odd = [image[pl.ds(2 * h + n, tiles, stride=4), :] for n in range(2)]
        both = jnp.where(left_half, even, pltpu.roll(odd, 64, 1)).astype(BF16)
        x_send[:, h * NZ : (h + 1) * NZ, :] = both.reshape(nx, NZ, 128)
    x_recv[pl.ds(mx, 1)] = x_send[pl.ds(mx, 1)]

    pl.semaphore_wait(barrier, 2 + (nx - 1) + (NZ - 1))

    def x_copy(d, slot):
        target = lax.rem(mx + d, nx)
        return pltpu.make_async_remote_copy(
            src_ref=x_send.at[target],
            dst_ref=x_recv.at[slot],
            send_sem=xsend_sem.at[d - 1],
            recv_sem=xrecv_sem.at[d - 1],
            device_id=along_x(target),
            device_id_type=MESH,
        )

    for d in range(1, nx):
        x_copy(d, mx).start()
    at3 = iota((SLOTS, blocks), 1)
    at1 = iota((1, blocks), 1)
    for n in (TILE_COLS, LATENT):
        load(n).wait()
    all_cols = tile_cols[...].astype(F32)

    def columns(index):
        return jnp.sum(jnp.where(at3 == index, all_cols, 0.0), axis=1, keepdims=True)

    def count(index):
        counts = tile_count[...].astype(F32)
        return jnp.sum(jnp.where(at1 == index, counts, 0.0), axis=1, keepdims=True)

    cols_own, cols_before, cols_after = columns(block), columns(before), columns(after)

    def slot_rows(cols, width):
        return jnp.concatenate(
            [jnp.broadcast_to(cols[k : k + 1, :], (TL, width)) for k in range(SLOTS)], axis=0
        )

    place = (iota((LINE, 128), 0) & 15).astype(F32)
    lane_f = iota((LINE, 128), 1).astype(F32)

    def gather_rows(cols):
        return (lane_f == slot_rows(cols, 128) + place).astype(F32)

    pick_own = gather_rows(cols_own)
    pick_up = jnp.concatenate([pick_own, gather_rows(cols_before)], axis=0).astype(BF16)
    pick_down = jnp.concatenate([pick_own, gather_rows(cols_after)], axis=0).astype(BF16)
    for r in range(8):
        side = r // 4
        rows = dot(pick_down if side else pick_up, latent[r]).astype(BF16)
        wide[(5 + r) * LINE : (6 + r) * LINE, CH : 2 * CH] = rows[0:LINE]
        margin_send[side, (r % 4) * LINE : (r % 4 + 1) * LINE, :] = rows[LINE : 2 * LINE]

    def margin_copy(side, target):
        return pltpu.make_async_remote_copy(
            src_ref=margin_send.at[side],
            dst_ref=margin_recv.at[1 - side],
            send_sem=msend_sem.at[side],
            recv_sem=mrecv_sem.at[1 - side],
            device_id=target,
            device_id_type=MESH,
        )

    margin_copy(0, device(before)).start()
    margin_copy(1, device(after)).start()
    for n in LATE_LOADS:
        load(n).start()

    source = iota((1, 512), 1)
    source_x, source_z = (source >> 1) & 3, (source >> 3) & 15
    source_row = 2 * (source & 1) + (source >> 8)
    cell_of = 2 * (source_x * NZ + source_z) + ((source >> 7) & 1)
    source_key = (cell_of + 1000 * source_row).astype(F32)
    own_rows = slot_rows(cols_own, 512)
    place_wide = (iota((LINE, 512), 0) & 15).astype(F32)
    inside = (place_wide >= 4.0) & (place_wide < 12.0)
    choose = jnp.concatenate(
        [
            (jnp.where(inside, own_rows + place_wide + 1000.0 * pr, -1.0) == source_key)
            .astype(F32)
            .astype(BF16)
            for pr in range(4)
        ],
        axis=0,
    )

    for d in range(1, nx):
        x_copy(d, lax.rem(mx + nx - d, nx)).wait_recv()
    by_z = dot(reorder, x_recv[...].reshape(2 * tiles, 128))
    z_send[...] = by_z.reshape(NZ, 2 * nx, 128).astype(BF16)

    def z_copy(far, slot):
        target = lax.rem(mz + far, NZ)
        return pltpu.make_async_remote_copy(
            src_ref=z_send.at[target],
            dst_ref=z_recv.at[slot],
            send_sem=zsend_sem,
            recv_sem=zrecv_sem,
            device_id=along_z(target),
            device_id_type=MESH,
        )

    def z_start(n):
        far = NZ // 2 + (1 - 2 * lax.rem(n, 2)) * lax.div(n + 1, 2)
        target = lax.rem(mz + far, NZ)
        pltpu.make_async_remote_copy(
            src_ref=z_send.at[target],
            dst_ref=z_recv.at[mz],
            send_sem=zsend_sem,
            recv_sem=zrecv_sem,
            device_id=along_z(target),
            device_id_type=MESH,
        ).start()

    def sums(first, second, third):
        return {(0, 0): first, (0, 1): second + third, (1, 0): first + second, (1, 1): third}

    def weight_rows(n):
        rows = pl.ds(pl.multiple_of(n * 16, 16), 16)
        by_col = []
        for e in range(3):
            by_col.append(sums(*[up_weight[a, e, rows, :].astype(F32) for a in range(3)]))
        for r, t in TAPS:
            by_tap = sums(*[by_col[e][r, t] for e in range(3)])
            for s, v in TAPS:
                at = pl.ds(pl.multiple_of((t * 2 + v) * CH + n * 16, 16), 16)
                combined[r * 2 + s, at, :] = by_tap[s, v].astype(BF16)

    def send_and_sum(n, carry):
        z_start(n)
        weight_rows(n)
        return carry

    load(UP_WEIGHT).wait()
    lax.fori_loop(0, NZ - 1, send_and_sum, 0)
    weight_rows(NZ - 1)
    z_recv[pl.ds(mz, 1)] = z_send[pl.ds(mz, 1)]

    for n in (TILE_COUNT, UP_BIAS, NORM_GAIN, NORM_BIAS, OUT_WEIGHT, TAPS_TABLE, LANES_TABLE):
        load(n).wait()
    for ae in range(9):
        out_rows[ae * 8 : ae * 8 + 3, :] = out_weight[ae].astype(F32)
    flat_taps = out_rows[...].astype(BF16)
    for ph in range(4):
        out_matrix[:, ph * CH : (ph + 1) * CH] = dot(
            taps[ph * 128 : (ph + 1) * 128, :], flat_taps
        ).astype(BF16)

    lane = iota((128, 128), 1)
    column = iota((128, 128), 0).astype(F32)
    slot_of = lane >> 4
    offset_of = (lane & 15).astype(F32)

    def place_columns(cols, live, first_slot):
        start = jnp.where(
            slot_of == first_slot,
            jnp.broadcast_to(cols[0:1, :], (128, 128)),
            jnp.where(
                slot_of == first_slot + 1,
                jnp.broadcast_to(cols[1:2, :], (128, 128)),
                jnp.broadcast_to(cols[2:3, :], (128, 128)),
            ),
        )
        relative = (slot_of - first_slot).astype(F32)
        valid = (relative >= 0.0) & (relative < live) & (relative < float(SLOTS))
        return jnp.where(valid & (column == start + offset_of), 1.0, 0.0)

    none = jnp.zeros((1, 1), F32)
    own_place = place_columns(cols_own, count(block), 0)
    up_place = (
        own_place
        + place_columns(cols_before, jnp.where(keep_before, count(before), none), SLOTS)
    ).astype(BF16)
    down_place = (
        own_place + place_columns(cols_after, jnp.where(keep_after, count(after), none), SLOTS)
    ).astype(BF16)

    margin_copy(0, device(before)).wait_recv()
    margin_copy(1, device(after)).wait_recv()
    top = margin_recv[0]
    bottom = margin_recv[1]
    wide[LINE : 5 * LINE, CH : 2 * CH] = jnp.where(keep_before, top, jnp.zeros_like(top))
    wide[13 * LINE : 17 * LINE, CH : 2 * CH] = jnp.where(
        keep_after, bottom, jnp.zeros_like(bottom)
    )
    for part in range(SLOTS):
        here = slice(LINE + part * CH, LINE + (part + 1) * CH)
        inputs = wide[here, CH : 2 * CH]
        wide[here, 0:CH] = dot(shift_low, inputs).astype(BF16)
        wide[here, 2 * CH : 3 * CH] = dot(shift_high, inputs).astype(BF16)

    bias = up_bias[...]
    total = jnp.zeros((LINE, CH), F32)
    for ph in range(4):
        r, s = ph // 2, ph % 2
        features = jnp.concatenate(
            [
                wide[(r + t) * LINE : (r + t + TL) * LINE, s * CH : (s + 2) * CH]
                for t in range(2)
            ],
            axis=1,
        )
        value = dot(features, combined[ph]) + bias
        preact[ph] = value
        total = total + jnp.sum(value.reshape(TL, LINE, CH), axis=0)

    def group_means(sums):
        rows = []
        for term in sums:
            high = term.astype(BF16).astype(F32)
            rest = term - high
            middle = rest.astype(BF16).astype(F32)
            rows += [high, middle, rest - middle]
        grouped = dot(jnp.concatenate(rows, axis=0).astype(BF16), groups[...])
        means = []
        for n in range(len(sums)):
            first = grouped[3 * n * LINE : (3 * n + 1) * LINE]
            second = grouped[(3 * n + 1) * LINE : (3 * n + 2) * LINE]
            third = grouped[(3 * n + 2) * LINE : (3 * n + 3) * LINE]
            line = (first + second + third) * (1.0 / 8192.0)
            means.append(
                jnp.concatenate(
                    [
                        jnp.broadcast_to(
                            jnp.sum(line[k * TL : (k + 1) * TL], axis=0, keepdims=True), (TL, CH)
                        )
                        for k in range(SLOTS)
                    ],
                    axis=0,
                )
            )
        return means

    (mean,) = group_means([total])

    def centre_rows(n, square):
        for step in range(4):
            at = pl.ds(pl.multiple_of((n * 4 + step) * LINE, LINE), LINE)
            for ph in range(4):
                off = preact[ph, at, :] - mean
                preact[ph, at, :] = off
                square = square + off * off
        return square

    square = lax.fori_loop(0, 4, centre_rows, jnp.zeros((LINE, CH), F32))
    (variance,) = group_means([square])
    inv = lax.rsqrt(variance + EPS)
    gain = jnp.broadcast_to(norm_gain[...], (LINE, CH))
    shift = jnp.broadcast_to(norm_bias[...], (LINE, CH))
    half_gain = 0.5 * gain
    half_scale = inv * half_gain
    half_shift = 0.5 * shift

    def silu_slopes(n, carry):
        for step in range(2):
            source_at = pl.ds(pl.multiple_of((2 * n + step + 3) * LINE, LINE), LINE)
            target_at = pl.ds(pl.multiple_of((2 * n + step) * LINE, LINE), LINE)
            for ph in range(4):
                half = preact[ph, source_at, :] * half_scale + half_shift
                curve = jnp.tanh(half)
                slopes[ph, target_at, :] = (
                    (1.0 + curve) + half * (1.0 - curve * curve)
                ) * half_gain
        return carry

    lax.fori_loop(0, 5, silu_slopes, 0)

    others = pl.ds(0, NZ - 1)
    pltpu.make_async_copy(z_recv.at[others], z_recv.at[others], zrecv_sem).wait()
    arrived = z_recv[...].astype(F32).reshape(2 * tiles, 128).astype(BF16)
    spread = dot(arrived, lanes[...]).astype(BF16)
    stacked = jnp.concatenate([spread[:, 256 * n : 256 * (n + 1)] for n in range(4)], axis=0)
    found = dot(choose, stacked)
    lane_wide = iota((1, 256), 1) & 127
    copy_wide = sum([(lane_wide >= 12 * c).astype(jnp.int32) for c in range(1, 9)])
    col_wide = copy_wide - 3 * (
        (copy_wide >= 3).astype(jnp.int32) + (copy_wide >= 6).astype(jnp.int32)
    )
    copy_one = copy_wide[:, 0:128]
    low = pltpu.roll(found, 1, 0)
    high = pltpu.roll(found, 4 * LINE - 1, 0)
    merged = jnp.where(col_wide == 0, low, jnp.where(col_wide == 1, found, high))
    lines = []
    for pr in range(4):
        line = merged[pr * LINE : (pr + 1) * LINE]
        lines += [line[:, 0:128], line[:, 128:256]]
    nothing = jnp.zeros((LINE, 128), F32)

    def line_at(index):
        return lines[index] if 0 <= index < 8 else nothing

    for i in range(3, 13):
        around = jnp.where(
            copy_one < 3, line_at(i - 5), jnp.where(copy_one < 6, line_at(i - 4), line_at(i - 3))
        )
        cells[(i - 3) * LINE : (i - 2) * LINE, :] = around.astype(BF16)

    first = jnp.zeros((LINE, CH), F32)
    second = jnp.zeros((LINE, CH), F32)
    for ph in range(4):
        act = dot(cells[...], out_matrix[:, ph * CH : (ph + 1) * CH])
        for n in range(10):
            at = slice(n * LINE, (n + 1) * LINE)
            grad = act[at] * slopes[ph, at, :]
            grads[ph, at, :] = grad
            first = first + grad
            second = second + grad * preact[ph, (n + 3) * LINE : (n + 4) * LINE, :]
    first, second = group_means([first, second])
    offset = first * inv
    slope = second * inv * inv * inv

    def normal_grad(i):
        for ph in range(4):
            value = -offset - preact[ph, i * LINE : (i + 1) * LINE, :] * slope
            if 3 <= i < 13:
                value = value + grads[ph, (i - 3) * LINE : (i - 2) * LINE, :] * inv
            zgrad[(i + 1) * LINE : (i + 2) * LINE, ph * CH : (ph + 1) * CH] = value.astype(BF16)

    def input_grad(pieces):
        parts = []
        for pairs in (((0, 0),), ((0, 1), (1, 0)), ((1, 1),)):
            left, right = [], []
            for s, v in pairs:
                for r in range(2):
                    for t in range(2):
                        ph = r * 2 + s
                        rows = [
                            zgrad[
                                (i + 2 - r - t) * LINE : (i + 2 - r - t + lines_of) * LINE,
                                ph * CH : (ph + 1) * CH,
                            ]
                            for i, lines_of in pieces
                        ]
                        left.append(rows[0] if len(rows) == 1 else jnp.concatenate(rows, axis=0))
                        right.append(combined[ph, (t * 2 + v) * CH : (t * 2 + v + 1) * CH, :])
            parts.append(
                lax.dot_general(
                    jnp.concatenate(left, axis=1),
                    jnp.concatenate(right, axis=1),
                    NT,
                    preferred_element_type=F32,
                )
            )
        size = parts[0].shape[0]
        place_rows = iota((size, CH), 0) & 15
        return (
            parts[1]
            + jnp.where(place_rows < 15, pltpu.roll(parts[0], size - 1, 0), 0.0)
            + jnp.where(place_rows > 0, pltpu.roll(parts[2], 1, 0), 0.0)
        ).astype(BF16)

    def grad_copy(side, part):
        rows = pl.ds((part if side == 0 else 1 - part) * 2 * LINE, 2 * LINE)
        return pltpu.make_async_remote_copy(
            src_ref=grad_send.at[side, rows],
            dst_ref=grad_recv.at[1 - side, rows],
            send_sem=gsend_sem.at[side, part],
            recv_sem=grecv_sem.at[1 - side, part],
            device_id=device(after if side else before),
            device_id_type=MESH,
        )

    for i in (0, 1, 2, 13, 14, 15):
        normal_grad(i)
    margin_grad = input_grad(((0, 2), (14, 2)))
    grad_send[0, 0 : 2 * LINE, :] = margin_grad[0 : 2 * LINE]
    grad_send[1, 2 * LINE : 4 * LINE, :] = margin_grad[2 * LINE : 4 * LINE]
    grad_copy(0, 0).start()
    grad_copy(1, 0).start()
    for i in (3, 4, 11, 12):
        normal_grad(i)
    margin_grad = input_grad(((2, 2), (12, 2)))
    grad_send[0, 2 * LINE : 4 * LINE, :] = margin_grad[0 : 2 * LINE]
    grad_send[1, 0 : 2 * LINE, :] = margin_grad[2 * LINE : 4 * LINE]
    grad_copy(0, 1).start()
    grad_copy(1, 1).start()
    for i in range(5, 11):
        normal_grad(i)
    own_grad[...] = input_grad(((4, 8),))

    rest = jnp.zeros((128 - 2 * LINE, CH), BF16)
    for part, rows in ((0, (2, 3, 4, 5)), (1, (0, 1, 6, 7))):
        grad_copy(0, part).wait_recv()
        grad_copy(1, part).wait_recv()
        for r in rows:
            side = r // 4
            at = (r % 4) * LINE
            terms = jnp.concatenate(
                [
                    own_grad[r * LINE : (r + 1) * LINE, :],
                    grad_recv[side, at : at + LINE, :],
                    rest,
                ],
                axis=0,
            )
            out[r] = dot(down_place if side else up_place, terms).astype(BF16)

    margin_copy(0, device(before)).wait_send()
    margin_copy(1, device(after)).wait_send()
    for d in range(1, nx):
        x_copy(d, mx).wait_send()
    pltpu.make_async_copy(z_send.at[others], z_send.at[others], zsend_sem).wait()
    for side in range(2):
        for part in range(2):
            grad_copy(side, part).wait_send()


def per_device(
    latent_feat,
    reward_grad,
    patches,
    up_weight,
    up_bias,
    norm_gain,
    norm_bias,
    out_weight,
    stem_weight,
    stem_bias,
    stem_gain,
    tile_count,
    tile_cols,
):
    sections = lax.axis_size("section")
    nx = lax.axis_size("tile") // NZ
    blocks = sections * nx * NZ
    operands = (
        latent_feat,
        reward_grad.reshape(-1, STEM).T,
        patches.T,
        up_weight,
        up_bias.reshape(1, CH),
        norm_gain.reshape(1, CH),
        norm_bias.reshape(1, CH),
        out_weight.transpose(0, 1, 3, 2).reshape(9, 3, CH),
        stem_weight,
        stem_bias.reshape(1, STEM),
        stem_gain.reshape(1, STEM),
        tile_count.reshape(1, blocks),
        tile_cols.T,
        jnp.asarray(out_taps(), BF16),
        jnp.asarray(cell_lanes(), BF16),
    )
    pinned = [pltpu.with_memory_space_constraint(array, pltpu.HBM) for array in operands]
    return pl.pallas_call(
        functools.partial(kernel, nx, sections),
        out_shape=pltpu.VMEM(latent_feat.shape, BF16),
        in_specs=[pl.BlockSpec(memory_space=pltpu.HBM)] * OPERANDS,
        out_specs=pl.BlockSpec(memory_space=pltpu.VMEM),
        scratch_shapes=[pltpu.VMEM(array.shape, array.dtype) for array in operands]
        + [
            pltpu.VMEM((18 * LINE, 3 * CH), BF16),
            pltpu.VMEM((4, 4 * CH, CH), BF16),
            pltpu.VMEM((128, 4 * CH), BF16),
            pltpu.VMEM((128, CH), F32),
            pltpu.VMEM((2, 4 * LINE, CH), BF16),
            pltpu.VMEM((2, 4 * LINE, CH), BF16),
            pltpu.VMEM((4 * nx * NZ, 128), F32),
            pltpu.VMEM((nx, 2 * NZ, 128), BF16),
            pltpu.VMEM((nx, 2 * NZ, 128), BF16),
            pltpu.VMEM((NZ, 2 * nx, 128), BF16),
            pltpu.VMEM((NZ, 2 * nx, 128), BF16),
            pltpu.VMEM((4, TL * LINE, CH), F32),
            pltpu.VMEM((4, 10 * LINE, CH), F32),
            pltpu.VMEM((4, 10 * LINE, CH), F32),
            pltpu.VMEM((18 * LINE, 4 * CH), BF16),
            pltpu.VMEM((10 * LINE, 128), BF16),
            pltpu.VMEM((8 * LINE, CH), BF16),
            pltpu.VMEM((2, 4 * LINE, CH), BF16),
            pltpu.VMEM((2, 4 * LINE, CH), BF16),
            pltpu.VMEM((CH, CH), BF16),
            pltpu.SemaphoreType.DMA((OPERANDS,)),
            pltpu.SemaphoreType.DMA((2,)),
            pltpu.SemaphoreType.DMA((2,)),
            pltpu.SemaphoreType.DMA((nx - 1,)),
            pltpu.SemaphoreType.DMA((nx - 1,)),
            pltpu.SemaphoreType.DMA,
            pltpu.SemaphoreType.DMA,
            pltpu.SemaphoreType.DMA((2, 2)),
            pltpu.SemaphoreType.DMA((2, 2)),
        ],
        compiler_params=pltpu.CompilerParams(
            collective_id=0, has_side_effects=True, vmem_limit_bytes=48 * 1024 * 1024
        ),
    )(*pinned)


def solution(mesh):
    return jax.shard_map(
        per_device,
        mesh=mesh,
        in_specs=(
            P(("section", "tile"), None, None),
            P("section", "tile", None),
            P("section", "tile"),
        )
        + (P(),) * 10,
        out_specs=P(("section", "tile"), None, None),
        check_vma=False,
    )
```

```python
import functools

import jax
import jax.numpy as jnp
import numpy as np
from jax import lax
from jax.experimental import pallas as pl
from jax.experimental.pallas import tpu as pltpu
from jax.sharding import PartitionSpec as P

EPS = 1e-06
CH = 256
STEM = 192
PIX = 48
TL = 16
SLOTS = 3
NZ = 16
LINE = SLOTS * TL
F32 = jnp.float32
BF16 = jnp.bfloat16
MESH = pl.DeviceIdType.MESH
NT = (((1,), (1,)), ((), ()))
TN = (((0,), (0,)), ((), ()))
(
    LATENT,
    REWARD,
    PIXELS,
    UP_WEIGHT,
    UP_BIAS,
    NORM_GAIN,
    NORM_BIAS,
    OUT_WEIGHT,
    STEM_WEIGHT,
    STEM_BIAS,
    STEM_GAIN,
    TILE_COUNT,
    TILE_COLS,
    TABLES,
) = range(14)
OPERANDS = 14
STEM_LOADS = (PIXELS, STEM_WEIGHT, STEM_BIAS, REWARD, STEM_GAIN)
BLOCK_LOADS = (TILE_COLS, TILE_COUNT)
LARGE_LOADS = (LATENT, UP_WEIGHT)
LATE_LOADS = (OUT_WEIGHT, TABLES, UP_BIAS, NORM_GAIN, NORM_BIAS)
TAPS = ((0, 0), (0, 1), (1, 0), (1, 1))


def out_taps():
    table = np.zeros((4, 128, 128), np.float32)
    for r in range(2):
        for s in range(2):
            for di in range(3):
                for dj in range(3):
                    for c in range(3):
                        for y in range(2):
                            for x in range(2):
                                a = r + 1 - (2 * (di - 1) + y)
                                e = s + 1 - (2 * (dj - 1) + x)
                                if 0 <= a < 3 and 0 <= e < 3:
                                    lane = (di * 3 + dj) * 12 + c * 4 + y * 2 + x
                                    table[r * 2 + s, lane, (a * 3 + e) * 8 + c] = 1
    return table.transpose(1, 0, 2).reshape(128, 512)


def cell_lanes():
    table = np.zeros((2, 64, 2, 2, 2, 128), np.float32)
    for odd in range(2):
        for c in range(3):
            for dy in range(4):
                for dx in range(4):
                    for copy in range(9):
                        lane = copy * 12 + c * 4 + (dy % 2) * 2 + dx % 2
                        table[odd, c * 16 + dy * 4 + dx, odd, dx // 2, dy // 2, lane] = 1
    return table.reshape(128, 1024)


def iota(shape, axis):
    return lax.broadcasted_iota(jnp.int32, shape, axis)


def dot(a, b):
    return jnp.dot(a, b, preferred_element_type=F32)


def three_rows(row):
    high = row.astype(BF16).astype(F32)
    rest = row - high
    middle = rest.astype(BF16).astype(F32)
    low = rest - middle
    at = iota((16, row.shape[1]), 0)
    rows = jnp.where(at == 0, high, jnp.where(at == 1, middle, jnp.where(at == 2, low, 0.0)))
    return rows.astype(BF16)


def kernel(nx, sections, *refs):
    operands, out, scratch = refs[:OPERANDS], refs[OPERANDS], refs[OPERANDS + 1 :]
    copies, scratch = scratch[:OPERANDS], scratch[OPERANDS:]
    (
        latent,
        reward,
        pixels,
        up_weight,
        up_bias,
        norm_gain,
        norm_bias,
        out_weight,
        stem_weight,
        stem_bias,
        stem_gain,
        tile_count,
        tile_cols,
        tables,
    ) = copies
    (
        wide,
        combined,
        folded,
        out_matrix,
        out_rows,
        margin_send,
        margin_recv,
        image,
        x_send,
        x_recv,
        z_send,
        z_recv,
        preact,
        slopes,
        grads,
        zgrad,
        cells,
        own_grad,
        grad_send,
        grad_recv,
        groups,
        load_sem,
        msend_sem,
        mrecv_sem,
        xsend_sem,
        xrecv_sem,
        zsend_sem,
        zrecv_sem,
        gsend_sem,
        grecv_sem,
    ) = scratch
    tiles = nx * NZ
    blocks = sections * tiles
    section = lax.axis_index("section")
    tile = lax.axis_index("tile")
    mx = lax.div(tile, NZ)
    mz = lax.rem(tile, NZ)
    block = section * tiles + tile
    before = lax.rem(block + blocks - 1, blocks)
    after = lax.rem(block + 1, blocks)

    def device(index):
        return (lax.div(index, tiles), lax.rem(index, tiles))

    def along_x(index):
        return (section, index * NZ + mz)

    def along_z(index):
        return (section, mx * NZ + index)

    barrier = pltpu.get_barrier_semaphore()

    def greet(target):
        pl.semaphore_signal(barrier, inc=1, device_id=target, device_id_type=MESH)

    def load(n):
        return pltpu.make_async_copy(operands[n], copies[n], load_sem.at[n])

    for n in BLOCK_LOADS + STEM_LOADS + LARGE_LOADS:
        load(n).start()

    for d in range(1, NZ):
        greet(along_z(lax.rem(mz + d, NZ)))
    for d in range(1, nx):
        greet(along_x(lax.rem(mx + d, nx)))
    greet(device(before))
    greet(device(after))

    row_at = iota((CH, CH), 0)
    col_at = iota((CH, CH), 1)
    groups[...] = ((row_at >> 3) == (col_at >> 3)).astype(F32).astype(BF16)
    zeros = jnp.zeros((LINE, 3 * CH), BF16)
    wide[0:LINE, :] = zeros
    wide[17 * LINE : 18 * LINE, :] = zeros
    out_rows[...] = jnp.zeros_like(out_rows)
    to_row = iota((128, 128), 0)
    reorder = (
        iota((128, 128), 1) == ((to_row >> 1) & 3) * (2 * NZ) + (to_row & 1) * NZ + (to_row >> 3)
    ).astype(F32).astype(BF16)
    shift_low = ((col_at == row_at - 1) & ((row_at & 15) != 0)).astype(F32).astype(BF16)
    shift_high = ((col_at == row_at + 1) & ((row_at & 15) != 15)).astype(F32).astype(BF16)
    keep_before = block != 0
    keep_after = block != blocks - 1

    at3 = iota((SLOTS, blocks), 1)
    at1 = iota((1, blocks), 1)
    for n in BLOCK_LOADS:
        load(n).wait()
    all_cols = tile_cols[...].astype(F32)

    def columns(index):
        return jnp.sum(jnp.where(at3 == index, all_cols, 0.0), axis=1, keepdims=True)

    def count(index):
        counts = tile_count[...].astype(F32)
        return jnp.sum(jnp.where(at1 == index, counts, 0.0), axis=1, keepdims=True)

    cols_own, cols_before, cols_after = columns(block), columns(before), columns(after)

    def slot_rows(cols, width):
        return jnp.concatenate(
            [jnp.broadcast_to(cols[k : k + 1, :], (TL, width)) for k in range(SLOTS)], axis=0
        )

    place = (iota((LINE, 128), 0) & 15).astype(F32)
    lane_f = iota((LINE, 128), 1).astype(F32)

    def gather_rows(cols):
        return (lane_f == slot_rows(cols, 128) + place).astype(F32)

    pick_own = gather_rows(cols_own)
    pick_up = jnp.concatenate([pick_own, gather_rows(cols_before)], axis=0).astype(BF16)
    pick_down = jnp.concatenate([pick_own, gather_rows(cols_after)], axis=0).astype(BF16)
    source = iota((1, 512), 1)
    source_x, source_z = (source >> 1) & 3, (source >> 3) & 15
    source_row = 2 * (source & 1) + (source >> 8)
    cell_of = 2 * (source_x * NZ + source_z) + ((source >> 7) & 1)
    source_key = (cell_of + 1000 * source_row).astype(F32)
    own_rows = slot_rows(cols_own, 512)
    place_wide = (iota((LINE, 512), 0) & 15).astype(F32)
    inside = (place_wide >= 4.0) & (place_wide < 12.0)
    choose = jnp.concatenate(
        [
            (jnp.where(inside, own_rows + place_wide + 1000.0 * pr, -1.0) == source_key)
            .astype(F32)
            .astype(BF16)
            for pr in range(4)
        ],
        axis=0,
    )

    lane = iota((128, 128), 1)
    column = iota((128, 128), 0).astype(F32)
    slot_of = lane >> 4
    offset_of = (lane & 15).astype(F32)

    def place_columns(cols, live, first_slot):
        start = jnp.where(
            slot_of == first_slot,
            jnp.broadcast_to(cols[0:1, :], (128, 128)),
            jnp.where(
                slot_of == first_slot + 1,
                jnp.broadcast_to(cols[1:2, :], (128, 128)),
                jnp.broadcast_to(cols[2:3, :], (128, 128)),
            ),
        )
        relative = (slot_of - first_slot).astype(F32)
        valid = (relative >= 0.0) & (relative < live) & (relative < float(SLOTS))
        return jnp.where(valid & (column == start + offset_of), 1.0, 0.0)

    none = jnp.zeros((1, 1), F32)
    own_place = place_columns(cols_own, count(block), 0)
    up_place = (
        own_place
        + place_columns(cols_before, jnp.where(keep_before, count(before), none), SLOTS)
    ).astype(BF16)
    down_place = (
        own_place + place_columns(cols_after, jnp.where(keep_after, count(after), none), SLOTS)
    ).astype(BF16)

    ones = jnp.ones((16, CH), BF16)

    def column_of(row):
        return lax.dot_general(three_rows(row), ones, TN, preferred_element_type=F32)

    for n in STEM_LOADS:
        load(n).wait()
    weight = stem_weight[...]
    stem = lax.dot_general(weight, pixels[...], TN, preferred_element_type=F32) + column_of(
        stem_bias[...]
    )
    scaled = reward[...].astype(F32) * column_of(stem_gain[...])
    centred = stem - jnp.mean(stem, axis=0, keepdims=True)
    scaled = scaled - jnp.mean(scaled, axis=0, keepdims=True)
    inverse = lax.rsqrt(jnp.mean(centred * centred, axis=0, keepdims=True) + EPS)
    along = jnp.mean(scaled * centred, axis=0, keepdims=True) * inverse * inverse
    stem_grad = (scaled - centred * along) * inverse
    padded_weight = jnp.concatenate([weight, jnp.zeros((128 - PIX, STEM), BF16)], axis=0)
    pixel_grad = dot(padded_weight, stem_grad.astype(BF16))
    image[...] = pixel_grad.astype(BF16).astype(F32).T
    left_half = iota((tiles, 128), 1) < 64
    for h in range(2):
        even, odd = [image[pl.ds(2 * h + n, tiles, stride=4), :] for n in range(2)]
        both = jnp.where(left_half, even, pltpu.roll(odd, 64, 1)).astype(BF16)
        x_send[:, h * NZ : (h + 1) * NZ, :] = both.reshape(nx, NZ, 128)
    x_recv[pl.ds(mx, 1)] = x_send[pl.ds(mx, 1)]

    pl.semaphore_wait(barrier, 2 + (nx - 1) + (NZ - 1))

    def x_copy(d, slot):
        target = lax.rem(mx + d, nx)
        return pltpu.make_async_remote_copy(
            src_ref=x_send.at[target],
            dst_ref=x_recv.at[slot],
            send_sem=xsend_sem.at[d - 1],
            recv_sem=xrecv_sem.at[d - 1],
            device_id=along_x(target),
            device_id_type=MESH,
        )

    for d in range(1, nx):
        x_copy(d, mx).start()
    load(LATENT).wait()
    for r in range(8):
        side = r // 4
        rows = dot(pick_down if side else pick_up, latent[r]).astype(BF16)
        wide[(5 + r) * LINE : (6 + r) * LINE, CH : 2 * CH] = rows[0:LINE]
        margin_send[side, (r % 4) * LINE : (r % 4 + 1) * LINE, :] = rows[LINE : 2 * LINE]

    def margin_copy(side, target):
        return pltpu.make_async_remote_copy(
            src_ref=margin_send.at[side],
            dst_ref=margin_recv.at[1 - side],
            send_sem=msend_sem.at[side],
            recv_sem=mrecv_sem.at[1 - side],
            device_id=target,
            device_id_type=MESH,
        )

    margin_copy(0, device(before)).start()
    margin_copy(1, device(after)).start()
    for n in LATE_LOADS:
        load(n).start()

    for d in range(1, nx):
        x_copy(d, lax.rem(mx + nx - d, nx)).wait_recv()
    by_z = dot(reorder, x_recv[...].reshape(2 * tiles, 128))
    z_send[...] = by_z.reshape(NZ, 2 * nx, 128).astype(BF16)

    def z_copy(far, slot):
        target = lax.rem(mz + far, NZ)
        return pltpu.make_async_remote_copy(
            src_ref=z_send.at[target],
            dst_ref=z_recv.at[slot],
            send_sem=zsend_sem,
            recv_sem=zrecv_sem,
            device_id=along_z(target),
            device_id_type=MESH,
        )

    def z_start(n):
        far = NZ // 2 + (1 - 2 * lax.rem(n, 2)) * lax.div(n + 1, 2)
        target = lax.rem(mz + far, NZ)
        pltpu.make_async_remote_copy(
            src_ref=z_send.at[target],
            dst_ref=z_recv.at[mz],
            send_sem=zsend_sem,
            recv_sem=zrecv_sem,
            device_id=along_z(target),
            device_id_type=MESH,
        ).start()

    def sums(first, second, third):
        return {(0, 0): first, (0, 1): second + third, (1, 0): first + second, (1, 1): third}

    def weight_rows(n):
        rows = pl.ds(pl.multiple_of(n * 16, 16), 16)
        by_col = [sums(*[up_weight[a, e, rows, :].astype(F32) for e in range(3)]) for a in range(3)]
        for s, v in TAPS:
            for a in range(3):
                folded[a, s * 2 + v, rows, :] = by_col[a][s, v].astype(BF16)
            by_tap = sums(*[by_col[a][s, v] for a in range(3)])
            for r, t in TAPS:
                at = pl.ds(pl.multiple_of((t * 2 + v) * CH + n * 16, 16), 16)
                combined[r * 2 + s, at, :] = by_tap[r, t].astype(BF16)

    def send_and_sum(n, carry):
        z_start(n)
        weight_rows(n)
        return carry

    load(UP_WEIGHT).wait()
    lax.fori_loop(0, NZ - 1, send_and_sum, 0)
    weight_rows(NZ - 1)
    z_recv[pl.ds(mz, 1)] = z_send[pl.ds(mz, 1)]

    for n in LATE_LOADS:
        load(n).wait()
    for ae in range(9):
        out_rows[ae * 8 : ae * 8 + 3, :] = out_weight[ae].astype(F32)
    flat_taps = out_rows[...].astype(BF16)
    for ph in range(4):
        out_matrix[:, ph * CH : (ph + 1) * CH] = dot(
            tables[:, 1024 + ph * 128 : 1024 + (ph + 1) * 128], flat_taps
        ).astype(BF16)

    margin_copy(0, device(before)).wait_recv()
    margin_copy(1, device(after)).wait_recv()
    top = margin_recv[0]
    bottom = margin_recv[1]
    wide[LINE : 5 * LINE, CH : 2 * CH] = jnp.where(keep_before, top, jnp.zeros_like(top))
    wide[13 * LINE : 17 * LINE, CH : 2 * CH] = jnp.where(
        keep_after, bottom, jnp.zeros_like(bottom)
    )
    for part in range(SLOTS):
        here = slice(LINE + part * CH, LINE + (part + 1) * CH)
        inputs = wide[here, CH : 2 * CH]
        wide[here, 0:CH] = dot(shift_low, inputs).astype(BF16)
        wide[here, 2 * CH : 3 * CH] = dot(shift_high, inputs).astype(BF16)

    bias = up_bias[...]
    def group_means(parts):
        rows = []
        for term in parts:
            high = term.astype(BF16).astype(F32)
            rest = term - high
            middle = rest.astype(BF16).astype(F32)
            rows += [high, middle, rest - middle]
        grouped = dot(jnp.concatenate(rows, axis=0).astype(BF16), groups[...])
        means = []
        for n in range(len(parts)):
            first = grouped[3 * n * LINE : (3 * n + 1) * LINE]
            second = grouped[(3 * n + 1) * LINE : (3 * n + 2) * LINE]
            third = grouped[(3 * n + 2) * LINE : (3 * n + 3) * LINE]
            line = (first + second + third) * (1.0 / 8192.0)
            means.append(
                jnp.concatenate(
                    [
                        jnp.broadcast_to(
                            jnp.sum(line[k * TL : (k + 1) * TL], axis=0, keepdims=True), (TL, CH)
                        )
                        for k in range(SLOTS)
                    ],
                    axis=0,
                )
            )
        return means

    def outputs(ph):
        r, s = ph // 2, ph % 2
        features = jnp.concatenate(
            [
                wide[(r + t) * LINE : (r + t + TL) * LINE, s * CH : (s + 2) * CH]
                for t in range(2)
            ],
            axis=1,
        )
        return dot(features, combined[ph]).reshape(TL, LINE, CH)

    value = outputs(0)
    (centre,) = group_means([jnp.sum(value, axis=0) + bias * float(TL)])
    to_centre = bias - 4.0 * centre
    total = jnp.zeros((LINE, CH), F32)
    square = jnp.zeros((LINE, CH), F32)
    for ph in range(4):
        off = (value if ph == 0 else outputs(ph)) + to_centre
        preact[ph] = off.reshape(TL * LINE, CH)
        total = total + jnp.sum(off, axis=0)
        square = square + jnp.sum(off * off, axis=0)
    mean, square = group_means([total, square])
    inv = lax.rsqrt(jnp.maximum(square - mean * mean, 0.0) + EPS)
    gain = jnp.broadcast_to(norm_gain[...], (LINE, CH))
    shift = jnp.broadcast_to(norm_bias[...], (LINE, CH))
    half_gain = 0.5 * gain
    half_scale = inv * half_gain
    half_shift = 0.5 * shift - mean * half_scale

    def silu_slopes(n, carry):
        for step in range(2):
            source_at = pl.ds(pl.multiple_of((2 * n + step + 3) * LINE, LINE), LINE)
            target_at = pl.ds(pl.multiple_of((2 * n + step) * LINE, LINE), LINE)
            for ph in range(4):
                half = preact[ph, source_at, :] * half_scale + half_shift
                curve = jnp.tanh(half)
                slopes[ph, target_at, :] = (
                    (1.0 + curve) + half * (1.0 - curve * curve)
                ) * half_gain
        return carry

    lax.fori_loop(0, 5, silu_slopes, 0)

    others = pl.ds(0, NZ - 1)
    pltpu.make_async_copy(z_recv.at[others], z_recv.at[others], zrecv_sem).wait()
    arrived = z_recv[...].astype(F32).reshape(2 * tiles, 128).astype(BF16)
    spread = dot(arrived, tables[:, 0:1024]).astype(BF16)
    stacked = jnp.concatenate([spread[:, 256 * n : 256 * (n + 1)] for n in range(4)], axis=0)
    found = dot(choose, stacked)
    lane_wide = iota((1, 256), 1) & 127
    copy_wide = sum([(lane_wide >= 12 * c).astype(jnp.int32) for c in range(1, 9)])
    col_wide = copy_wide - 3 * (
        (copy_wide >= 3).astype(jnp.int32) + (copy_wide >= 6).astype(jnp.int32)
    )
    copy_one = copy_wide[:, 0:128]
    low = pltpu.roll(found, 1, 0)
    high = pltpu.roll(found, 4 * LINE - 1, 0)
    merged = jnp.where(col_wide == 0, low, jnp.where(col_wide == 1, found, high))
    lines = []
    for pr in range(4):
        line = merged[pr * LINE : (pr + 1) * LINE]
        lines += [line[:, 0:128], line[:, 128:256]]
    nothing = jnp.zeros((LINE, 128), F32)

    def line_at(index):
        return lines[index] if 0 <= index < 8 else nothing

    for i in range(3, 13):
        around = jnp.where(
            copy_one < 3, line_at(i - 5), jnp.where(copy_one < 6, line_at(i - 4), line_at(i - 3))
        )
        cells[(i - 3) * LINE : (i - 2) * LINE, :] = around.astype(BF16)

    first = jnp.zeros((LINE, CH), F32)
    second = jnp.zeros((LINE, CH), F32)
    for ph in range(4):
        act = dot(cells[...], out_matrix[:, ph * CH : (ph + 1) * CH])
        for n in range(10):
            at = slice(n * LINE, (n + 1) * LINE)
            grad = act[at] * slopes[ph, at, :]
            grads[ph, at, :] = grad
            first = first + grad
            second = second + grad * preact[ph, (n + 3) * LINE : (n + 4) * LINE, :]
    first, second = group_means([first, second])
    offset = first * inv
    slope = (second - mean * first) * inv * inv * inv
    base = mean * slope - offset

    def row_sums(evens, odds):
        known = {}

        def normal_grad(i, ph):
            if (i, ph) not in known:
                value = base - preact[ph, i * LINE : (i + 1) * LINE, :] * slope
                if 3 <= i < 13:
                    value = value + grads[ph, (i - 3) * LINE : (i - 2) * LINE, :] * inv
                known[i, ph] = value
            return known[i, ph]

        for s in range(2):
            lanes = slice(s * CH, (s + 1) * CH)
            for i in sorted(set(evens) | set(odds)):
                if i in evens:
                    pair = normal_grad(i, s) + normal_grad(i, 2 + s)
                    zgrad[0, i * LINE : (i + 1) * LINE, lanes] = pair.astype(BF16)
                if i in odds:
                    pair = [normal_grad(i, 2 + s)] if i >= 0 else []
                    pair += [normal_grad(i + 1, s)] if i + 1 < TL else []
                    zgrad[1, (i + 1) * LINE : (i + 2) * LINE, lanes] = sum(pair).astype(BF16)

    def input_grad(pieces):
        parts = []
        for pairs in (((0, 0),), ((0, 1), (1, 0)), ((1, 1),)):
            left, right = [], []
            for s, v in pairs:
                for a, kind, start in ((0, 1, 1), (1, 0, 0), (2, 1, 0)):
                    rows = [
                        zgrad[
                            kind,
                            (i + start) * LINE : (i + start + lines_of) * LINE,
                            s * CH : (s + 1) * CH,
                        ]
                        for i, lines_of in pieces
                    ]
                    left.append(rows[0] if len(rows) == 1 else jnp.concatenate(rows, axis=0))
                    right.append(folded[a, s * 2 + v])
            parts.append(
                lax.dot_general(
                    jnp.concatenate(left, axis=1),
                    jnp.concatenate(right, axis=1),
                    NT,
                    preferred_element_type=F32,
                )
            )
        size = parts[0].shape[0]
        place_rows = iota((size, CH), 0) & 15
        return (
            parts[1]
            + jnp.where(place_rows < 15, pltpu.roll(parts[0], size - 1, 0), 0.0)
            + jnp.where(place_rows > 0, pltpu.roll(parts[2], 1, 0), 0.0)
        ).astype(BF16)

    def grad_copy(side, part):
        rows = pl.ds((part if side == 0 else 1 - part) * 2 * LINE, 2 * LINE)
        return pltpu.make_async_remote_copy(
            src_ref=grad_send.at[side, rows],
            dst_ref=grad_recv.at[1 - side, rows],
            send_sem=gsend_sem.at[side, part],
            recv_sem=grecv_sem.at[1 - side, part],
            device_id=device(after if side else before),
            device_id_type=MESH,
        )

    row_sums((0, 1, 14, 15), (-1, 0, 1, 13, 14, 15))
    margin_grad = input_grad(((0, 2), (14, 2)))
    grad_send[0, 0 : 2 * LINE, :] = margin_grad[0 : 2 * LINE]
    grad_send[1, 2 * LINE : 4 * LINE, :] = margin_grad[2 * LINE : 4 * LINE]
    grad_copy(0, 0).start()
    grad_copy(1, 0).start()
    row_sums((2, 3, 12, 13), (2, 3, 11, 12))
    margin_grad = input_grad(((2, 2), (12, 2)))
    grad_send[0, 2 * LINE : 4 * LINE, :] = margin_grad[0 : 2 * LINE]
    grad_send[1, 0 : 2 * LINE, :] = margin_grad[2 * LINE : 4 * LINE]
    grad_copy(0, 1).start()
    grad_copy(1, 1).start()
    row_sums(range(4, 12), range(4, 11))
    own_grad[...] = input_grad(((4, 8),))

    rest = jnp.zeros((128 - 2 * LINE, CH), BF16)
    for part, rows in ((0, (2, 3, 4, 5)), (1, (0, 1, 6, 7))):
        grad_copy(0, part).wait_recv()
        grad_copy(1, part).wait_recv()
        for r in rows:
            side = r // 4
            at = (r % 4) * LINE
            terms = jnp.concatenate(
                [
                    own_grad[r * LINE : (r + 1) * LINE, :],
                    grad_recv[side, at : at + LINE, :],
                    rest,
                ],
                axis=0,
            )
            out[r] = dot(down_place if side else up_place, terms).astype(BF16)

    margin_copy(0, device(before)).wait_send()
    margin_copy(1, device(after)).wait_send()
    for d in range(1, nx):
        x_copy(d, mx).wait_send()
    pltpu.make_async_copy(z_send.at[others], z_send.at[others], zsend_sem).wait()
    for side in range(2):
        for part in range(2):
            grad_copy(side, part).wait_send()


def per_device(
    latent_feat,
    reward_grad,
    patches,
    up_weight,
    up_bias,
    norm_gain,
    norm_bias,
    out_weight,
    stem_weight,
    stem_bias,
    stem_gain,
    tile_count,
    tile_cols,
):
    sections = lax.axis_size("section")
    nx = lax.axis_size("tile") // NZ
    blocks = sections * nx * NZ
    operands = (
        latent_feat,
        reward_grad.reshape(-1, STEM).T,
        patches.T,
        up_weight,
        up_bias.reshape(1, CH),
        norm_gain.reshape(1, CH),
        norm_bias.reshape(1, CH),
        out_weight.transpose(0, 1, 3, 2).reshape(9, 3, CH),
        stem_weight,
        stem_bias.reshape(1, STEM),
        stem_gain.reshape(1, STEM),
        tile_count.reshape(1, blocks),
        tile_cols.T,
        jnp.asarray(np.concatenate([cell_lanes(), out_taps()], axis=1), BF16),
    )
    pinned = [pltpu.with_memory_space_constraint(array, pltpu.HBM) for array in operands]
    return pl.pallas_call(
        functools.partial(kernel, nx, sections),
        out_shape=pltpu.VMEM(latent_feat.shape, BF16),
        in_specs=[pl.BlockSpec(memory_space=pltpu.HBM)] * OPERANDS,
        out_specs=pl.BlockSpec(memory_space=pltpu.VMEM),
        scratch_shapes=[pltpu.VMEM(array.shape, array.dtype) for array in operands]
        + [
            pltpu.VMEM((18 * LINE, 3 * CH), BF16),
            pltpu.VMEM((4, 4 * CH, CH), BF16),
            pltpu.VMEM((3, 4, CH, CH), BF16),
            pltpu.VMEM((128, 4 * CH), BF16),
            pltpu.VMEM((128, CH), F32),
            pltpu.VMEM((2, 4 * LINE, CH), BF16),
            pltpu.VMEM((2, 4 * LINE, CH), BF16),
            pltpu.VMEM((4 * nx * NZ, 128), F32),
            pltpu.VMEM((nx, 2 * NZ, 128), BF16),
            pltpu.VMEM((nx, 2 * NZ, 128), BF16),
            pltpu.VMEM((NZ, 2 * nx, 128), BF16),
            pltpu.VMEM((NZ, 2 * nx, 128), BF16),
            pltpu.VMEM((4, TL * LINE, CH), F32),
            pltpu.VMEM((4, 10 * LINE, CH), F32),
            pltpu.VMEM((4, 10 * LINE, CH), F32),
            pltpu.VMEM((2, 17 * LINE, 2 * CH), BF16),
            pltpu.VMEM((10 * LINE, 128), BF16),
            pltpu.VMEM((8 * LINE, CH), BF16),
            pltpu.VMEM((2, 4 * LINE, CH), BF16),
            pltpu.VMEM((2, 4 * LINE, CH), BF16),
            pltpu.VMEM((CH, CH), BF16),
            pltpu.SemaphoreType.DMA((OPERANDS,)),
            pltpu.SemaphoreType.DMA((2,)),
            pltpu.SemaphoreType.DMA((2,)),
            pltpu.SemaphoreType.DMA((nx - 1,)),
            pltpu.SemaphoreType.DMA((nx - 1,)),
            pltpu.SemaphoreType.DMA,
            pltpu.SemaphoreType.DMA,
            pltpu.SemaphoreType.DMA((2, 2)),
            pltpu.SemaphoreType.DMA((2, 2)),
        ],
        compiler_params=pltpu.CompilerParams(
            collective_id=0, has_side_effects=True, vmem_limit_bytes=48 * 1024 * 1024
        ),
    )(*pinned)


def solution(mesh):
    return jax.shard_map(
        per_device,
        mesh=mesh,
        in_specs=(
            P(("section", "tile"), None, None),
            P("section", "tile", None),
            P("section", "tile"),
        )
        + (P(),) * 10,
        out_specs=P(("section", "tile"), None, None),
        check_vma=False,
    )
```

```python
import functools

import jax
import jax.numpy as jnp
import numpy as np
from jax import lax
from jax.experimental import pallas as pl
from jax.experimental.pallas import tpu as pltpu
from jax.sharding import PartitionSpec as P

EPS = 1e-06
CH = 256
STEM = 192
PIX = 48
TL = 16
SLOTS = 3
NZ = 16
LINE = SLOTS * TL
F32 = jnp.float32
BF16 = jnp.bfloat16
MESH = pl.DeviceIdType.MESH
NT = (((1,), (1,)), ((), ()))
TN = (((0,), (0,)), ((), ()))
(
    LATENT,
    REWARD,
    PIXELS,
    UP_WEIGHT,
    UP_BIAS,
    NORM_GAIN,
    NORM_BIAS,
    OUT_WEIGHT,
    STEM_WEIGHT,
    STEM_BIAS,
    STEM_GAIN,
    TILE_COUNT,
    TILE_COLS,
    TABLES,
) = range(14)
OPERANDS = 14
STEM_LOADS = (PIXELS, STEM_WEIGHT, STEM_BIAS, REWARD, STEM_GAIN)
BLOCK_LOADS = (TILE_COLS, TILE_COUNT)
LARGE_LOADS = (LATENT, UP_WEIGHT)
LATE_LOADS = (OUT_WEIGHT, TABLES, UP_BIAS, NORM_GAIN, NORM_BIAS)
TAPS = ((0, 0), (0, 1), (1, 0), (1, 1))


def out_taps():
    table = np.zeros((4, 128, 128), np.float32)
    for r in range(2):
        for s in range(2):
            for di in range(3):
                for dj in range(3):
                    for c in range(3):
                        for y in range(2):
                            for x in range(2):
                                a = r + 1 - (2 * (di - 1) + y)
                                e = s + 1 - (2 * (dj - 1) + x)
                                if 0 <= a < 3 and 0 <= e < 3:
                                    lane = (di * 3 + dj) * 12 + c * 4 + y * 2 + x
                                    table[r * 2 + s, lane, (a * 3 + e) * 8 + c] = 1
    return table.transpose(1, 0, 2).reshape(128, 512)


def cell_lanes():
    table = np.zeros((2, 64, 2, 2, 2, 128), np.float32)
    for odd in range(2):
        for c in range(3):
            for dy in range(4):
                for dx in range(4):
                    for copy in range(9):
                        lane = copy * 12 + c * 4 + (dy % 2) * 2 + dx % 2
                        table[odd, c * 16 + dy * 4 + dx, odd, dx // 2, dy // 2, lane] = 1
    return table.reshape(128, 1024)


def iota(shape, axis):
    return lax.broadcasted_iota(jnp.int32, shape, axis)


def dot(a, b):
    return jnp.dot(a, b, preferred_element_type=F32)


def three_rows(row):
    high = row.astype(BF16).astype(F32)
    rest = row - high
    middle = rest.astype(BF16).astype(F32)
    low = rest - middle
    at = iota((16, row.shape[1]), 0)
    rows = jnp.where(at == 0, high, jnp.where(at == 1, middle, jnp.where(at == 2, low, 0.0)))
    return rows.astype(BF16)


def kernel(nx, sections, *refs):
    operands, out, scratch = refs[:OPERANDS], refs[OPERANDS], refs[OPERANDS + 1 :]
    copies, scratch = scratch[:OPERANDS], scratch[OPERANDS:]
    (
        latent,
        reward,
        pixels,
        up_weight,
        up_bias,
        norm_gain,
        norm_bias,
        out_weight,
        stem_weight,
        stem_bias,
        stem_gain,
        tile_count,
        tile_cols,
        tables,
    ) = copies
    (
        wide,
        combined,
        folded,
        out_matrix,
        out_rows,
        margin_send,
        margin_recv,
        image,
        x_send,
        x_recv,
        z_send,
        z_recv,
        preact,
        slopes,
        grads,
        zgrad,
        cells,
        own_grad,
        grad_send,
        grad_recv,
        groups,
        load_sem,
        msend_sem,
        mrecv_sem,
        xsend_sem,
        xrecv_sem,
        zsend_sem,
        zrecv_sem,
        gsend_sem,
        grecv_sem,
    ) = scratch
    tiles = nx * NZ
    blocks = sections * tiles
    section = lax.axis_index("section")
    tile = lax.axis_index("tile")
    mx = lax.div(tile, NZ)
    mz = lax.rem(tile, NZ)
    block = section * tiles + tile
    before = lax.rem(block + blocks - 1, blocks)
    after = lax.rem(block + 1, blocks)

    def device(index):
        return (lax.div(index, tiles), lax.rem(index, tiles))

    def along_x(index):
        return (section, index * NZ + mz)

    def along_z(index):
        return (section, mx * NZ + index)

    barrier = pltpu.get_barrier_semaphore()

    def greet(target):
        pl.semaphore_signal(barrier, inc=1, device_id=target, device_id_type=MESH)

    def load(n):
        return pltpu.make_async_copy(operands[n], copies[n], load_sem.at[n])

    for n in BLOCK_LOADS + STEM_LOADS + LARGE_LOADS:
        load(n).start()

    for d in range(1, NZ):
        greet(along_z(lax.rem(mz + d, NZ)))
    for d in range(1, nx):
        greet(along_x(lax.rem(mx + d, nx)))
    greet(device(before))
    greet(device(after))

    row_at = iota((CH, CH), 0)
    col_at = iota((CH, CH), 1)
    groups[...] = ((row_at >> 3) == (col_at >> 3)).astype(F32).astype(BF16)
    zeros = jnp.zeros((LINE, 3 * CH), BF16)
    wide[0:LINE, :] = zeros
    wide[17 * LINE : 18 * LINE, :] = zeros
    out_rows[...] = jnp.zeros_like(out_rows)
    to_row = iota((128, 128), 0)
    reorder = (
        iota((128, 128), 1) == ((to_row >> 1) & 3) * (2 * NZ) + (to_row & 1) * NZ + (to_row >> 3)
    ).astype(F32).astype(BF16)
    shift_low = ((col_at == row_at - 1) & ((row_at & 15) != 0)).astype(F32).astype(BF16)
    shift_high = ((col_at == row_at + 1) & ((row_at & 15) != 15)).astype(F32).astype(BF16)
    keep_before = block != 0
    keep_after = block != blocks - 1

    at3 = iota((SLOTS, blocks), 1)
    at1 = iota((1, blocks), 1)
    for n in BLOCK_LOADS + STEM_LOADS + (LATENT,):
        load(n).wait()
    all_cols = tile_cols[...].astype(F32)

    def columns(index):
        return jnp.sum(jnp.where(at3 == index, all_cols, 0.0), axis=1, keepdims=True)

    def count(index):
        counts = tile_count[...].astype(F32)
        return jnp.sum(jnp.where(at1 == index, counts, 0.0), axis=1, keepdims=True)

    cols_own, cols_before, cols_after = columns(block), columns(before), columns(after)

    def slot_rows(cols, width):
        return jnp.concatenate(
            [jnp.broadcast_to(cols[k : k + 1, :], (TL, width)) for k in range(SLOTS)], axis=0
        )

    place = (iota((LINE, 128), 0) & 15).astype(F32)
    lane_f = iota((LINE, 128), 1).astype(F32)

    def gather_rows(cols):
        return (lane_f == slot_rows(cols, 128) + place).astype(F32)

    pick_own = gather_rows(cols_own)
    pick_up = jnp.concatenate([pick_own, gather_rows(cols_before)], axis=0).astype(BF16)
    pick_down = jnp.concatenate([pick_own, gather_rows(cols_after)], axis=0).astype(BF16)
    source = iota((1, 512), 1)
    source_x, source_z = (source >> 1) & 3, (source >> 3) & 15
    source_row = 2 * (source & 1) + (source >> 8)
    cell_of = 2 * (source_x * NZ + source_z) + ((source >> 7) & 1)
    source_key = (cell_of + 1000 * source_row).astype(F32)
    own_rows = slot_rows(cols_own, 512)
    place_wide = (iota((LINE, 512), 0) & 15).astype(F32)
    inside = (place_wide >= 4.0) & (place_wide < 12.0)
    choose = jnp.concatenate(
        [
            (jnp.where(inside, own_rows + place_wide + 1000.0 * pr, -1.0) == source_key)
            .astype(F32)
            .astype(BF16)
            for pr in range(4)
        ],
        axis=0,
    )

    lane = iota((128, 128), 1)
    column = iota((128, 128), 0).astype(F32)
    slot_of = lane >> 4
    offset_of = (lane & 15).astype(F32)

    def place_columns(cols, live, first_slot):
        start = jnp.where(
            slot_of == first_slot,
            jnp.broadcast_to(cols[0:1, :], (128, 128)),
            jnp.where(
                slot_of == first_slot + 1,
                jnp.broadcast_to(cols[1:2, :], (128, 128)),
                jnp.broadcast_to(cols[2:3, :], (128, 128)),
            ),
        )
        relative = (slot_of - first_slot).astype(F32)
        valid = (relative >= 0.0) & (relative < live) & (relative < float(SLOTS))
        return jnp.where(valid & (column == start + offset_of), 1.0, 0.0)

    none = jnp.zeros((1, 1), F32)
    own_place = place_columns(cols_own, count(block), 0)
    up_place = (
        own_place
        + place_columns(cols_before, jnp.where(keep_before, count(before), none), SLOTS)
    ).astype(BF16)
    down_place = (
        own_place + place_columns(cols_after, jnp.where(keep_after, count(after), none), SLOTS)
    ).astype(BF16)

    for r in range(8):
        side = r // 4
        rows = dot(pick_down if side else pick_up, latent[r]).astype(BF16)
        wide[(5 + r) * LINE : (6 + r) * LINE, CH : 2 * CH] = rows[0:LINE]
        margin_send[side, (r % 4) * LINE : (r % 4 + 1) * LINE, :] = rows[LINE : 2 * LINE]


    ones = jnp.ones((16, CH), BF16)

    def column_of(row):
        return lax.dot_general(three_rows(row), ones, TN, preferred_element_type=F32)

    weight = stem_weight[...]
    stem = lax.dot_general(weight, pixels[...], TN, preferred_element_type=F32) + column_of(
        stem_bias[...]
    )
    scaled = reward[...].astype(F32) * column_of(stem_gain[...])
    centred = stem - jnp.mean(stem, axis=0, keepdims=True)
    scaled = scaled - jnp.mean(scaled, axis=0, keepdims=True)
    inverse = lax.rsqrt(jnp.mean(centred * centred, axis=0, keepdims=True) + EPS)
    along = jnp.mean(scaled * centred, axis=0, keepdims=True) * inverse * inverse
    stem_grad = (scaled - centred * along) * inverse
    padded_weight = jnp.concatenate([weight, jnp.zeros((128 - PIX, STEM), BF16)], axis=0)
    pixel_grad = dot(padded_weight, stem_grad.astype(BF16))
    image[...] = pixel_grad.astype(BF16).astype(F32).T
    left_half = iota((tiles, 128), 1) < 64
    for h in range(2):
        even, odd = [image[pl.ds(2 * h + n, tiles, stride=4), :] for n in range(2)]
        both = jnp.where(left_half, even, pltpu.roll(odd, 64, 1)).astype(BF16)
        x_send[:, h * NZ : (h + 1) * NZ, :] = both.reshape(nx, NZ, 128)
    x_recv[pl.ds(mx, 1)] = x_send[pl.ds(mx, 1)]

    pl.semaphore_wait(barrier, 2 + (nx - 1) + (NZ - 1))

    def margin_copy(side, target):
        return pltpu.make_async_remote_copy(
            src_ref=margin_send.at[side],
            dst_ref=margin_recv.at[1 - side],
            send_sem=msend_sem.at[side],
            recv_sem=mrecv_sem.at[1 - side],
            device_id=target,
            device_id_type=MESH,
        )

    margin_copy(0, device(before)).start()
    margin_copy(1, device(after)).start()

    def x_copy(d, slot):
        target = lax.rem(mx + d, nx)
        return pltpu.make_async_remote_copy(
            src_ref=x_send.at[target],
            dst_ref=x_recv.at[slot],
            send_sem=xsend_sem.at[d - 1],
            recv_sem=xrecv_sem.at[d - 1],
            device_id=along_x(target),
            device_id_type=MESH,
        )

    for d in range(1, nx):
        x_copy(d, mx).start()
    for n in LATE_LOADS:
        load(n).start()

    def sums(first, second, third):
        return {(0, 0): first, (0, 1): second + third, (1, 0): first + second, (1, 1): third}

    def weight_rows(n):
        rows = pl.ds(pl.multiple_of(n * 16, 16), 16)
        by_col = [sums(*[up_weight[a, e, rows, :].astype(F32) for e in range(3)]) for a in range(3)]
        for s, v in TAPS:
            for a in range(3):
                folded[a, s * 2 + v, rows, :] = by_col[a][s, v].astype(BF16)
            by_tap = sums(*[by_col[a][s, v] for a in range(3)])
            for r, t in TAPS:
                at = pl.ds(pl.multiple_of((t * 2 + v) * CH + n * 16, 16), 16)
                combined[r * 2 + s, at, :] = by_tap[r, t].astype(BF16)

    def weight_chunk(n, carry):
        weight_rows(n)
        return carry

    load(UP_WEIGHT).wait()
    lax.fori_loop(0, CH // 16, weight_chunk, 0)
    for n in LATE_LOADS:
        load(n).wait()
    for ae in range(9):
        out_rows[ae * 8 : ae * 8 + 3, :] = out_weight[ae].astype(F32)
    flat_taps = out_rows[...].astype(BF16)
    for ph in range(4):
        out_matrix[:, ph * CH : (ph + 1) * CH] = dot(
            tables[:, 1024 + ph * 128 : 1024 + (ph + 1) * 128], flat_taps
        ).astype(BF16)

    for d in range(1, nx):
        x_copy(d, lax.rem(mx + nx - d, nx)).wait_recv()
    by_z = dot(reorder, x_recv[...].reshape(2 * tiles, 128))
    z_send[...] = by_z.reshape(NZ, 2 * nx, 128).astype(BF16)

    def z_start(n):
        far = NZ // 2 + (1 - 2 * lax.rem(n, 2)) * lax.div(n + 1, 2)
        target = lax.rem(mz + far, NZ)
        pltpu.make_async_remote_copy(
            src_ref=z_send.at[target],
            dst_ref=z_recv.at[mz],
            send_sem=zsend_sem,
            recv_sem=zrecv_sem,
            device_id=along_z(target),
            device_id_type=MESH,
        ).start()

    def z_send_one(n, carry):
        z_start(n)
        return carry

    lax.fori_loop(0, NZ - 1, z_send_one, 0)
    z_recv[pl.ds(mz, 1)] = z_send[pl.ds(mz, 1)]

    margin_copy(0, device(before)).wait_recv()
    margin_copy(1, device(after)).wait_recv()
    top = margin_recv[0]
    bottom = margin_recv[1]
    wide[LINE : 5 * LINE, CH : 2 * CH] = jnp.where(keep_before, top, jnp.zeros_like(top))
    wide[13 * LINE : 17 * LINE, CH : 2 * CH] = jnp.where(
        keep_after, bottom, jnp.zeros_like(bottom)
    )
    for part in range(SLOTS):
        here = slice(LINE + part * CH, LINE + (part + 1) * CH)
        inputs = wide[here, CH : 2 * CH]
        wide[here, 0:CH] = dot(shift_low, inputs).astype(BF16)
        wide[here, 2 * CH : 3 * CH] = dot(shift_high, inputs).astype(BF16)

    bias = up_bias[...]
    def group_means(parts):
        rows = []
        for term in parts:
            high = term.astype(BF16).astype(F32)
            rest = term - high
            middle = rest.astype(BF16).astype(F32)
            rows += [high, middle, rest - middle]
        grouped = dot(jnp.concatenate(rows, axis=0).astype(BF16), groups[...])
        means = []
        for n in range(len(parts)):
            first = grouped[3 * n * LINE : (3 * n + 1) * LINE]
            second = grouped[(3 * n + 1) * LINE : (3 * n + 2) * LINE]
            third = grouped[(3 * n + 2) * LINE : (3 * n + 3) * LINE]
            line = (first + second + third) * (1.0 / 8192.0)
            means.append(
                jnp.concatenate(
                    [
                        jnp.broadcast_to(
                            jnp.sum(line[k * TL : (k + 1) * TL], axis=0, keepdims=True), (TL, CH)
                        )
                        for k in range(SLOTS)
                    ],
                    axis=0,
                )
            )
        return means

    def outputs(ph):
        r, s = ph // 2, ph % 2
        features = jnp.concatenate(
            [
                wide[(r + t) * LINE : (r + t + TL) * LINE, s * CH : (s + 2) * CH]
                for t in range(2)
            ],
            axis=1,
        )
        return dot(features, combined[ph]).reshape(TL, LINE, CH)

    value = outputs(0)
    (centre,) = group_means([jnp.sum(value, axis=0) + bias * float(TL)])
    to_centre = bias - 4.0 * centre
    total = jnp.zeros((LINE, CH), F32)
    square = jnp.zeros((LINE, CH), F32)
    for ph in range(4):
        off = (value if ph == 0 else outputs(ph)) + to_centre
        preact[ph] = off.reshape(TL * LINE, CH)
        total = total + jnp.sum(off, axis=0)
        square = square + jnp.sum(off * off, axis=0)
    mean, square = group_means([total, square])
    inv = lax.rsqrt(jnp.maximum(square - mean * mean, 0.0) + EPS)
    gain = jnp.broadcast_to(norm_gain[...], (LINE, CH))
    shift = jnp.broadcast_to(norm_bias[...], (LINE, CH))
    half_gain = 0.5 * gain
    half_scale = inv * half_gain
    half_shift = 0.5 * shift - mean * half_scale

    def silu_slopes(n, carry):
        for step in range(2):
            source_at = pl.ds(pl.multiple_of((2 * n + step + 3) * LINE, LINE), LINE)
            target_at = pl.ds(pl.multiple_of((2 * n + step) * LINE, LINE), LINE)
            for ph in range(4):
                half = preact[ph, source_at, :] * half_scale + half_shift
                curve = jnp.tanh(half)
                slopes[ph, target_at, :] = (
                    (1.0 + curve) + half * (1.0 - curve * curve)
                ) * half_gain
        return carry

    lax.fori_loop(0, 5, silu_slopes, 0)

    others = pl.ds(0, NZ - 1)
    pltpu.make_async_copy(z_recv.at[others], z_recv.at[others], zrecv_sem).wait()
    arrived = z_recv[...].astype(F32).reshape(2 * tiles, 128).astype(BF16)
    spread = dot(arrived, tables[:, 0:1024]).astype(BF16)
    stacked = jnp.concatenate([spread[:, 256 * n : 256 * (n + 1)] for n in range(4)], axis=0)
    found = dot(choose, stacked)
    lane_wide = iota((1, 256), 1) & 127
    copy_wide = sum([(lane_wide >= 12 * c).astype(jnp.int32) for c in range(1, 9)])
    col_wide = copy_wide - 3 * (
        (copy_wide >= 3).astype(jnp.int32) + (copy_wide >= 6).astype(jnp.int32)
    )
    copy_one = copy_wide[:, 0:128]
    low = pltpu.roll(found, 1, 0)
    high = pltpu.roll(found, 4 * LINE - 1, 0)
    merged = jnp.where(col_wide == 0, low, jnp.where(col_wide == 1, found, high))
    lines = []
    for pr in range(4):
        line = merged[pr * LINE : (pr + 1) * LINE]
        lines += [line[:, 0:128], line[:, 128:256]]
    nothing = jnp.zeros((LINE, 128), F32)

    def line_at(index):
        return lines[index] if 0 <= index < 8 else nothing

    for i in range(3, 13):
        around = jnp.where(
            copy_one < 3, line_at(i - 5), jnp.where(copy_one < 6, line_at(i - 4), line_at(i - 3))
        )
        cells[(i - 3) * LINE : (i - 2) * LINE, :] = around.astype(BF16)

    first = jnp.zeros((LINE, CH), F32)
    second = jnp.zeros((LINE, CH), F32)
    for ph in range(4):
        act = dot(cells[...], out_matrix[:, ph * CH : (ph + 1) * CH])
        for n in range(10):
            at = slice(n * LINE, (n + 1) * LINE)
            grad = act[at] * slopes[ph, at, :]
            grads[ph, at, :] = grad
            first = first + grad
            second = second + grad * preact[ph, (n + 3) * LINE : (n + 4) * LINE, :]
    first, second = group_means([first, second])
    offset = first * inv
    slope = (second - mean * first) * inv * inv * inv
    base = mean * slope - offset

    def row_sums(evens, odds):
        known = {}

        def normal_grad(i, ph):
            if (i, ph) not in known:
                value = base - preact[ph, i * LINE : (i + 1) * LINE, :] * slope
                if 3 <= i < 13:
                    value = value + grads[ph, (i - 3) * LINE : (i - 2) * LINE, :] * inv
                known[i, ph] = value
            return known[i, ph]

        for s in range(2):
            lanes = slice(s * CH, (s + 1) * CH)
            for i in sorted(set(evens) | set(odds)):
                if i in evens:
                    pair = normal_grad(i, s) + normal_grad(i, 2 + s)
                    zgrad[0, i * LINE : (i + 1) * LINE, lanes] = pair.astype(BF16)
                if i in odds:
                    pair = [normal_grad(i, 2 + s)] if i >= 0 else []
                    pair += [normal_grad(i + 1, s)] if i + 1 < TL else []
                    zgrad[1, (i + 1) * LINE : (i + 2) * LINE, lanes] = sum(pair).astype(BF16)

    def input_grad(pieces):
        parts = []
        for pairs in (((0, 0),), ((0, 1), (1, 0)), ((1, 1),)):
            left, right = [], []
            for s, v in pairs:
                for a, kind, start in ((0, 1, 1), (1, 0, 0), (2, 1, 0)):
                    rows = [
                        zgrad[
                            kind,
                            (i + start) * LINE : (i + start + lines_of) * LINE,
                            s * CH : (s + 1) * CH,
                        ]
                        for i, lines_of in pieces
                    ]
                    left.append(rows[0] if len(rows) == 1 else jnp.concatenate(rows, axis=0))
                    right.append(folded[a, s * 2 + v])
            parts.append(
                lax.dot_general(
                    jnp.concatenate(left, axis=1),
                    jnp.concatenate(right, axis=1),
                    NT,
                    preferred_element_type=F32,
                )
            )
        size = parts[0].shape[0]
        place_rows = iota((size, CH), 0) & 15
        return (
            parts[1]
            + jnp.where(place_rows < 15, pltpu.roll(parts[0], size - 1, 0), 0.0)
            + jnp.where(place_rows > 0, pltpu.roll(parts[2], 1, 0), 0.0)
        ).astype(BF16)

    def grad_copy(side, part):
        rows = pl.ds((part if side == 0 else 1 - part) * 2 * LINE, 2 * LINE)
        return pltpu.make_async_remote_copy(
            src_ref=grad_send.at[side, rows],
            dst_ref=grad_recv.at[1 - side, rows],
            send_sem=gsend_sem.at[side, part],
            recv_sem=grecv_sem.at[1 - side, part],
            device_id=device(after if side else before),
            device_id_type=MESH,
        )

    row_sums((0, 1, 14, 15), (-1, 0, 1, 13, 14, 15))
    margin_grad = input_grad(((0, 2), (14, 2)))
    grad_send[0, 0 : 2 * LINE, :] = margin_grad[0 : 2 * LINE]
    grad_send[1, 2 * LINE : 4 * LINE, :] = margin_grad[2 * LINE : 4 * LINE]
    grad_copy(0, 0).start()
    grad_copy(1, 0).start()
    row_sums((2, 3, 12, 13), (2, 3, 11, 12))
    margin_grad = input_grad(((2, 2), (12, 2)))
    grad_send[0, 2 * LINE : 4 * LINE, :] = margin_grad[0 : 2 * LINE]
    grad_send[1, 0 : 2 * LINE, :] = margin_grad[2 * LINE : 4 * LINE]
    grad_copy(0, 1).start()
    grad_copy(1, 1).start()
    row_sums(range(4, 12), range(4, 11))
    own_grad[...] = input_grad(((4, 8),))

    rest = jnp.zeros((128 - 2 * LINE, CH), BF16)
    for part, rows in ((0, (2, 3, 4, 5)), (1, (0, 1, 6, 7))):
        grad_copy(0, part).wait_recv()
        grad_copy(1, part).wait_recv()
        for r in rows:
            side = r // 4
            at = (r % 4) * LINE
            terms = jnp.concatenate(
                [
                    own_grad[r * LINE : (r + 1) * LINE, :],
                    grad_recv[side, at : at + LINE, :],
                    rest,
                ],
                axis=0,
            )
            out[r] = dot(down_place if side else up_place, terms).astype(BF16)

    margin_copy(0, device(before)).wait_send()
    margin_copy(1, device(after)).wait_send()
    for d in range(1, nx):
        x_copy(d, mx).wait_send()
    pltpu.make_async_copy(z_send.at[others], z_send.at[others], zsend_sem).wait()
    for side in range(2):
        for part in range(2):
            grad_copy(side, part).wait_send()


def per_device(
    latent_feat,
    reward_grad,
    patches,
    up_weight,
    up_bias,
    norm_gain,
    norm_bias,
    out_weight,
    stem_weight,
    stem_bias,
    stem_gain,
    tile_count,
    tile_cols,
):
    sections = lax.axis_size("section")
    nx = lax.axis_size("tile") // NZ
    blocks = sections * nx * NZ
    operands = (
        latent_feat,
        reward_grad.reshape(-1, STEM).T,
        patches.T,
        up_weight,
        up_bias.reshape(1, CH),
        norm_gain.reshape(1, CH),
        norm_bias.reshape(1, CH),
        out_weight.transpose(0, 1, 3, 2).reshape(9, 3, CH),
        stem_weight,
        stem_bias.reshape(1, STEM),
        stem_gain.reshape(1, STEM),
        tile_count.reshape(1, blocks),
        tile_cols.T,
        jnp.asarray(np.concatenate([cell_lanes(), out_taps()], axis=1), BF16),
    )
    pinned = [pltpu.with_memory_space_constraint(array, pltpu.HBM) for array in operands]
    return pl.pallas_call(
        functools.partial(kernel, nx, sections),
        out_shape=pltpu.VMEM(latent_feat.shape, BF16),
        in_specs=[pl.BlockSpec(memory_space=pltpu.HBM)] * OPERANDS,
        out_specs=pl.BlockSpec(memory_space=pltpu.VMEM),
        scratch_shapes=[pltpu.VMEM(array.shape, array.dtype) for array in operands]
        + [
            pltpu.VMEM((18 * LINE, 3 * CH), BF16),
            pltpu.VMEM((4, 4 * CH, CH), BF16),
            pltpu.VMEM((3, 4, CH, CH), BF16),
            pltpu.VMEM((128, 4 * CH), BF16),
            pltpu.VMEM((128, CH), F32),
            pltpu.VMEM((2, 4 * LINE, CH), BF16),
            pltpu.VMEM((2, 4 * LINE, CH), BF16),
            pltpu.VMEM((4 * nx * NZ, 128), F32),
            pltpu.VMEM((nx, 2 * NZ, 128), BF16),
            pltpu.VMEM((nx, 2 * NZ, 128), BF16),
            pltpu.VMEM((NZ, 2 * nx, 128), BF16),
            pltpu.VMEM((NZ, 2 * nx, 128), BF16),
            pltpu.VMEM((4, TL * LINE, CH), F32),
            pltpu.VMEM((4, 10 * LINE, CH), F32),
            pltpu.VMEM((4, 10 * LINE, CH), F32),
            pltpu.VMEM((2, 17 * LINE, 2 * CH), BF16),
            pltpu.VMEM((10 * LINE, 128), BF16),
            pltpu.VMEM((8 * LINE, CH), BF16),
            pltpu.VMEM((2, 4 * LINE, CH), BF16),
            pltpu.VMEM((2, 4 * LINE, CH), BF16),
            pltpu.VMEM((CH, CH), BF16),
            pltpu.SemaphoreType.DMA((OPERANDS,)),
            pltpu.SemaphoreType.DMA((2,)),
            pltpu.SemaphoreType.DMA((2,)),
            pltpu.SemaphoreType.DMA((nx - 1,)),
            pltpu.SemaphoreType.DMA((nx - 1,)),
            pltpu.SemaphoreType.DMA,
            pltpu.SemaphoreType.DMA,
            pltpu.SemaphoreType.DMA((2, 2)),
            pltpu.SemaphoreType.DMA((2, 2)),
        ],
        compiler_params=pltpu.CompilerParams(
            collective_id=0, has_side_effects=True, vmem_limit_bytes=48 * 1024 * 1024
        ),
    )(*pinned)


def solution(mesh):
    return jax.shard_map(
        per_device,
        mesh=mesh,
        in_specs=(
            P(("section", "tile"), None, None),
            P("section", "tile", None),
            P("section", "tile"),
        )
        + (P(),) * 10,
        out_specs=P(("section", "tile"), None, None),
        check_vma=False,
    )
```

```python
import functools

import jax
import jax.numpy as jnp
import numpy as np
from jax import lax
from jax.experimental import pallas as pl
from jax.experimental.pallas import tpu as pltpu
from jax.sharding import PartitionSpec as P

EPS = 1e-06
CH = 256
STEM = 192
PIX = 48
TL = 16
SLOTS = 3
NZ = 16
LINE = SLOTS * TL
F32 = jnp.float32
BF16 = jnp.bfloat16
MESH = pl.DeviceIdType.MESH
NT = (((1,), (1,)), ((), ()))
TN = (((0,), (0,)), ((), ()))
(
    LATENT,
    REWARD,
    PIXELS,
    UP_WEIGHT,
    UP_BIAS,
    NORM_GAIN,
    NORM_BIAS,
    OUT_WEIGHT,
    STEM_WEIGHT,
    STEM_BIAS,
    STEM_GAIN,
    TILE_COUNT,
    TILE_COLS,
    TABLES,
) = range(14)
OPERANDS = 14
STEM_LOADS = (PIXELS, STEM_WEIGHT, STEM_BIAS, REWARD, STEM_GAIN)
BLOCK_LOADS = (TILE_COLS, TILE_COUNT)
LATE_LOADS = (OUT_WEIGHT, TABLES, UP_BIAS, NORM_GAIN, NORM_BIAS)
TAPS = ((0, 0), (0, 1), (1, 0), (1, 1))


def out_taps():
    table = np.zeros((4, 128, 128), np.float32)
    for r in range(2):
        for s in range(2):
            for di in range(3):
                for dj in range(3):
                    for c in range(3):
                        for y in range(2):
                            for x in range(2):
                                a = r + 1 - (2 * (di - 1) + y)
                                e = s + 1 - (2 * (dj - 1) + x)
                                if 0 <= a < 3 and 0 <= e < 3:
                                    lane = (di * 3 + dj) * 12 + c * 4 + y * 2 + x
                                    table[r * 2 + s, lane, (a * 3 + e) * 8 + c] = 1
    return table.transpose(1, 0, 2).reshape(128, 512)


def cell_lanes():
    table = np.zeros((2, 64, 2, 2, 2, 128), np.float32)
    for odd in range(2):
        for c in range(3):
            for dy in range(4):
                for dx in range(4):
                    for copy in range(9):
                        lane = copy * 12 + c * 4 + (dy % 2) * 2 + dx % 2
                        table[odd, c * 16 + dy * 4 + dx, odd, dx // 2, dy // 2, lane] = 1
    return table.reshape(128, 1024)


def iota(shape, axis):
    return lax.broadcasted_iota(jnp.int32, shape, axis)


def dot(a, b):
    return jnp.dot(a, b, preferred_element_type=F32)


def three_rows(row):
    high = row.astype(BF16).astype(F32)
    rest = row - high
    middle = rest.astype(BF16).astype(F32)
    low = rest - middle
    at = iota((16, row.shape[1]), 0)
    rows = jnp.where(at == 0, high, jnp.where(at == 1, middle, jnp.where(at == 2, low, 0.0)))
    return rows.astype(BF16)


def kernel(nx, sections, *refs):
    operands, out, scratch = refs[:OPERANDS], refs[OPERANDS], refs[OPERANDS + 1 :]
    copies, scratch = scratch[:OPERANDS], scratch[OPERANDS:]
    (
        latent,
        reward,
        pixels,
        up_weight,
        up_bias,
        norm_gain,
        norm_bias,
        out_weight,
        stem_weight,
        stem_bias,
        stem_gain,
        tile_count,
        tile_cols,
        tables,
    ) = copies
    (
        wide,
        combined,
        folded,
        out_matrix,
        out_rows,
        margin_send,
        margin_recv,
        image,
        x_send,
        x_recv,
        z_send,
        z_recv,
        preact,
        slopes,
        grads,
        zgrad,
        cells,
        own_grad,
        grad_send,
        grad_recv,
        groups,
        load_sem,
        msend_sem,
        mrecv_sem,
        xsend_sem,
        xrecv_sem,
        zsend_sem,
        zrecv_sem,
        gsend_sem,
        grecv_sem,
    ) = scratch
    tiles = nx * NZ
    blocks = sections * tiles
    section = lax.axis_index("section")
    tile = lax.axis_index("tile")
    mx = lax.div(tile, NZ)
    mz = lax.rem(tile, NZ)
    block = section * tiles + tile
    before = lax.rem(block + blocks - 1, blocks)
    after = lax.rem(block + 1, blocks)

    def device(index):
        return (lax.div(index, tiles), lax.rem(index, tiles))

    def along_x(index):
        return (section, index * NZ + mz)

    def along_z(index):
        return (section, mx * NZ + index)

    barrier = pltpu.get_barrier_semaphore()

    def greet(target):
        pl.semaphore_signal(barrier, inc=1, device_id=target, device_id_type=MESH)

    def load(n):
        return pltpu.make_async_copy(operands[n], copies[n], load_sem.at[n])

    for n in BLOCK_LOADS + (LATENT,) + STEM_LOADS + (UP_WEIGHT,):
        load(n).start()

    for d in range(1, NZ):
        greet(along_z(lax.rem(mz + d, NZ)))
    for d in range(1, nx):
        greet(along_x(lax.rem(mx + d, nx)))
    greet(device(before))
    greet(device(after))

    row_at = iota((CH, CH), 0)
    col_at = iota((CH, CH), 1)
    groups[...] = ((row_at >> 3) == (col_at >> 3)).astype(F32).astype(BF16)
    zeros = jnp.zeros((LINE, 3 * CH), BF16)
    wide[0:LINE, :] = zeros
    wide[17 * LINE : 18 * LINE, :] = zeros
    out_rows[...] = jnp.zeros_like(out_rows)
    to_row = iota((128, 128), 0)
    reorder = (
        iota((128, 128), 1) == ((to_row >> 1) & 3) * (2 * NZ) + (to_row & 1) * NZ + (to_row >> 3)
    ).astype(F32).astype(BF16)
    shift_low = ((col_at == row_at - 1) & ((row_at & 15) != 0)).astype(F32).astype(BF16)
    shift_high = ((col_at == row_at + 1) & ((row_at & 15) != 15)).astype(F32).astype(BF16)
    keep_before = block != 0
    keep_after = block != blocks - 1

    at3 = iota((SLOTS, blocks), 1)
    at1 = iota((1, blocks), 1)
    for n in BLOCK_LOADS + (LATENT,):
        load(n).wait()
    all_cols = tile_cols[...].astype(F32)

    def columns(index):
        return jnp.sum(jnp.where(at3 == index, all_cols, 0.0), axis=1, keepdims=True)

    def count(index):
        counts = tile_count[...].astype(F32)
        return jnp.sum(jnp.where(at1 == index, counts, 0.0), axis=1, keepdims=True)

    cols_own, cols_before, cols_after = columns(block), columns(before), columns(after)

    def slot_rows(cols, width):
        return jnp.concatenate(
            [jnp.broadcast_to(cols[k : k + 1, :], (TL, width)) for k in range(SLOTS)], axis=0
        )

    place = (iota((LINE, 128), 0) & 15).astype(F32)
    lane_f = iota((LINE, 128), 1).astype(F32)

    def gather_rows(cols):
        return (lane_f == slot_rows(cols, 128) + place).astype(F32)

    pick_own = gather_rows(cols_own)
    pick_up = jnp.concatenate([pick_own, gather_rows(cols_before)], axis=0).astype(BF16)
    pick_down = jnp.concatenate([pick_own, gather_rows(cols_after)], axis=0).astype(BF16)
    for r in range(8):
        side = r // 4
        rows = dot(pick_down if side else pick_up, latent[r]).astype(BF16)
        wide[(5 + r) * LINE : (6 + r) * LINE, CH : 2 * CH] = rows[0:LINE]
        margin_send[side, (r % 4) * LINE : (r % 4 + 1) * LINE, :] = rows[LINE : 2 * LINE]


    pl.semaphore_wait(barrier, 2 + (nx - 1) + (NZ - 1))

    def margin_copy(side, target):
        return pltpu.make_async_remote_copy(
            src_ref=margin_send.at[side],
            dst_ref=margin_recv.at[1 - side],
            send_sem=msend_sem.at[side],
            recv_sem=mrecv_sem.at[1 - side],
            device_id=target,
            device_id_type=MESH,
        )

    margin_copy(0, device(before)).start()
    margin_copy(1, device(after)).start()

    ones = jnp.ones((16, CH), BF16)

    def column_of(row):
        return lax.dot_general(three_rows(row), ones, TN, preferred_element_type=F32)

    for n in STEM_LOADS:
        load(n).wait()
    weight = stem_weight[...]
    stem = lax.dot_general(weight, pixels[...], TN, preferred_element_type=F32) + column_of(
        stem_bias[...]
    )
    scaled = reward[...].astype(F32) * column_of(stem_gain[...])
    centred = stem - jnp.mean(stem, axis=0, keepdims=True)
    scaled = scaled - jnp.mean(scaled, axis=0, keepdims=True)
    inverse = lax.rsqrt(jnp.mean(centred * centred, axis=0, keepdims=True) + EPS)
    along = jnp.mean(scaled * centred, axis=0, keepdims=True) * inverse * inverse
    stem_grad = (scaled - centred * along) * inverse
    padded_weight = jnp.concatenate([weight, jnp.zeros((128 - PIX, STEM), BF16)], axis=0)
    pixel_grad = dot(padded_weight, stem_grad.astype(BF16))
    image[...] = pixel_grad.astype(BF16).astype(F32).T
    left_half = iota((tiles, 128), 1) < 64
    for h in range(2):
        even, odd = [image[pl.ds(2 * h + n, tiles, stride=4), :] for n in range(2)]
        both = jnp.where(left_half, even, pltpu.roll(odd, 64, 1)).astype(BF16)
        x_send[:, h * NZ : (h + 1) * NZ, :] = both.reshape(nx, NZ, 128)
    x_recv[pl.ds(mx, 1)] = x_send[pl.ds(mx, 1)]

    def x_copy(d, slot):
        target = lax.rem(mx + d, nx)
        return pltpu.make_async_remote_copy(
            src_ref=x_send.at[target],
            dst_ref=x_recv.at[slot],
            send_sem=xsend_sem.at[d - 1],
            recv_sem=xrecv_sem.at[d - 1],
            device_id=along_x(target),
            device_id_type=MESH,
        )

    for d in range(1, nx):
        x_copy(d, mx).start()
    for n in LATE_LOADS:
        load(n).start()

    source = iota((1, 512), 1)
    source_x, source_z = (source >> 1) & 3, (source >> 3) & 15
    source_row = 2 * (source & 1) + (source >> 8)
    cell_of = 2 * (source_x * NZ + source_z) + ((source >> 7) & 1)
    source_key = (cell_of + 1000 * source_row).astype(F32)
    own_rows = slot_rows(cols_own, 512)
    place_wide = (iota((LINE, 512), 0) & 15).astype(F32)
    inside = (place_wide >= 4.0) & (place_wide < 12.0)
    choose = jnp.concatenate(
        [
            (jnp.where(inside, own_rows + place_wide + 1000.0 * pr, -1.0) == source_key)
            .astype(F32)
            .astype(BF16)
            for pr in range(4)
        ],
        axis=0,
    )

    lane = iota((128, 128), 1)
    column = iota((128, 128), 0).astype(F32)
    slot_of = lane >> 4
    offset_of = (lane & 15).astype(F32)

    def place_columns(cols, live, first_slot):
        start = jnp.where(
            slot_of == first_slot,
            jnp.broadcast_to(cols[0:1, :], (128, 128)),
            jnp.where(
                slot_of == first_slot + 1,
                jnp.broadcast_to(cols[1:2, :], (128, 128)),
                jnp.broadcast_to(cols[2:3, :], (128, 128)),
            ),
        )
        relative = (slot_of - first_slot).astype(F32)
        valid = (relative >= 0.0) & (relative < live) & (relative < float(SLOTS))
        return jnp.where(valid & (column == start + offset_of), 1.0, 0.0)

    none = jnp.zeros((1, 1), F32)
    own_place = place_columns(cols_own, count(block), 0)
    up_place = (
        own_place
        + place_columns(cols_before, jnp.where(keep_before, count(before), none), SLOTS)
    ).astype(BF16)
    down_place = (
        own_place + place_columns(cols_after, jnp.where(keep_after, count(after), none), SLOTS)
    ).astype(BF16)

    def sums(first, second, third):
        return {(0, 0): first, (0, 1): second + third, (1, 0): first + second, (1, 1): third}

    def weight_rows(n):
        rows = pl.ds(pl.multiple_of(n * 16, 16), 16)
        by_col = [sums(*[up_weight[a, e, rows, :].astype(F32) for e in range(3)]) for a in range(3)]
        for s, v in TAPS:
            for a in range(3):
                folded[a, s * 2 + v, rows, :] = by_col[a][s, v].astype(BF16)
            by_tap = sums(*[by_col[a][s, v] for a in range(3)])
            for r, t in TAPS:
                at = pl.ds(pl.multiple_of((t * 2 + v) * CH + n * 16, 16), 16)
                combined[r * 2 + s, at, :] = by_tap[r, t].astype(BF16)

    def weight_chunk(n, carry):
        weight_rows(n)
        return carry

    load(UP_WEIGHT).wait()
    lax.fori_loop(0, CH // 16, weight_chunk, 0)
    for n in LATE_LOADS:
        load(n).wait()
    for ae in range(9):
        out_rows[ae * 8 : ae * 8 + 3, :] = out_weight[ae].astype(F32)
    flat_taps = out_rows[...].astype(BF16)
    for ph in range(4):
        out_matrix[:, ph * CH : (ph + 1) * CH] = dot(
            tables[:, 1024 + ph * 128 : 1024 + (ph + 1) * 128], flat_taps
        ).astype(BF16)

    for d in range(1, nx):
        x_copy(d, lax.rem(mx + nx - d, nx)).wait_recv()
    by_z = dot(reorder, x_recv[...].reshape(2 * tiles, 128))
    z_send[...] = by_z.reshape(NZ, 2 * nx, 128).astype(BF16)

    def z_start(n):
        far = NZ // 2 + (1 - 2 * lax.rem(n, 2)) * lax.div(n + 1, 2)
        target = lax.rem(mz + far, NZ)
        pltpu.make_async_remote_copy(
            src_ref=z_send.at[target],
            dst_ref=z_recv.at[mz],
            send_sem=zsend_sem,
            recv_sem=zrecv_sem,
            device_id=along_z(target),
            device_id_type=MESH,
        ).start()

    def z_send_one(n, carry):
        z_start(n)
        return carry

    lax.fori_loop(0, NZ - 1, z_send_one, 0)
    z_recv[pl.ds(mz, 1)] = z_send[pl.ds(mz, 1)]

    margin_copy(0, device(before)).wait_recv()
    margin_copy(1, device(after)).wait_recv()
    top = margin_recv[0]
    bottom = margin_recv[1]
    wide[LINE : 5 * LINE, CH : 2 * CH] = jnp.where(keep_before, top, jnp.zeros_like(top))
    wide[13 * LINE : 17 * LINE, CH : 2 * CH] = jnp.where(
        keep_after, bottom, jnp.zeros_like(bottom)
    )
    for part in range(SLOTS):
        here = slice(LINE + part * CH, LINE + (part + 1) * CH)
        inputs = wide[here, CH : 2 * CH]
        wide[here, 0:CH] = dot(shift_low, inputs).astype(BF16)
        wide[here, 2 * CH : 3 * CH] = dot(shift_high, inputs).astype(BF16)

    bias = up_bias[...]
    def group_means(parts):
        rows = []
        for term in parts:
            high = term.astype(BF16).astype(F32)
            rest = term - high
            middle = rest.astype(BF16).astype(F32)
            rows += [high, middle, rest - middle]
        grouped = dot(jnp.concatenate(rows, axis=0).astype(BF16), groups[...])
        means = []
        for n in range(len(parts)):
            first = grouped[3 * n * LINE : (3 * n + 1) * LINE]
            second = grouped[(3 * n + 1) * LINE : (3 * n + 2) * LINE]
            third = grouped[(3 * n + 2) * LINE : (3 * n + 3) * LINE]
            line = (first + second + third) * (1.0 / 8192.0)
            means.append(
                jnp.concatenate(
                    [
                        jnp.broadcast_to(
                            jnp.sum(line[k * TL : (k + 1) * TL], axis=0, keepdims=True), (TL, CH)
                        )
                        for k in range(SLOTS)
                    ],
                    axis=0,
                )
            )
        return means

    def outputs(ph):
        r, s = ph // 2, ph % 2
        features = jnp.concatenate(
            [
                wide[(r + t) * LINE : (r + t + TL) * LINE, s * CH : (s + 2) * CH]
                for t in range(2)
            ],
            axis=1,
        )
        return dot(features, combined[ph]).reshape(TL, LINE, CH)

    value = outputs(0)
    (centre,) = group_means([jnp.sum(value, axis=0) + bias * float(TL)])
    to_centre = bias - 4.0 * centre
    total = jnp.zeros((LINE, CH), F32)
    square = jnp.zeros((LINE, CH), F32)
    for ph in range(4):
        off = (value if ph == 0 else outputs(ph)) + to_centre
        preact[ph] = off.reshape(TL * LINE, CH)
        total = total + jnp.sum(off, axis=0)
        square = square + jnp.sum(off * off, axis=0)
    mean, square = group_means([total, square])
    inv = lax.rsqrt(jnp.maximum(square - mean * mean, 0.0) + EPS)
    gain = jnp.broadcast_to(norm_gain[...], (LINE, CH))
    shift = jnp.broadcast_to(norm_bias[...], (LINE, CH))
    half_gain = 0.5 * gain
    half_scale = inv * half_gain
    half_shift = 0.5 * shift - mean * half_scale

    def silu_slopes(n, carry):
        for step in range(2):
            source_at = pl.ds(pl.multiple_of((2 * n + step + 3) * LINE, LINE), LINE)
            target_at = pl.ds(pl.multiple_of((2 * n + step) * LINE, LINE), LINE)
            for ph in range(4):
                half = preact[ph, source_at, :] * half_scale + half_shift
                curve = jnp.tanh(half)
                slopes[ph, target_at, :] = (
                    (1.0 + curve) + half * (1.0 - curve * curve)
                ) * half_gain
        return carry

    lax.fori_loop(0, 5, silu_slopes, 0)

    others = pl.ds(0, NZ - 1)
    pltpu.make_async_copy(z_recv.at[others], z_recv.at[others], zrecv_sem).wait()
    arrived = z_recv[...].astype(F32).reshape(2 * tiles, 128).astype(BF16)
    spread = dot(arrived, tables[:, 0:1024]).astype(BF16)
    stacked = jnp.concatenate([spread[:, 256 * n : 256 * (n + 1)] for n in range(4)], axis=0)
    found = dot(choose, stacked)
    lane_wide = iota((1, 256), 1) & 127
    copy_wide = sum([(lane_wide >= 12 * c).astype(jnp.int32) for c in range(1, 9)])
    col_wide = copy_wide - 3 * (
        (copy_wide >= 3).astype(jnp.int32) + (copy_wide >= 6).astype(jnp.int32)
    )
    copy_one = copy_wide[:, 0:128]
    low = pltpu.roll(found, 1, 0)
    high = pltpu.roll(found, 4 * LINE - 1, 0)
    merged = jnp.where(col_wide == 0, low, jnp.where(col_wide == 1, found, high))
    lines = []
    for pr in range(4):
        line = merged[pr * LINE : (pr + 1) * LINE]
        lines += [line[:, 0:128], line[:, 128:256]]
    nothing = jnp.zeros((LINE, 128), F32)

    def line_at(index):
        return lines[index] if 0 <= index < 8 else nothing

    for i in range(3, 13):
        around = jnp.where(
            copy_one < 3, line_at(i - 5), jnp.where(copy_one < 6, line_at(i - 4), line_at(i - 3))
        )
        cells[(i - 3) * LINE : (i - 2) * LINE, :] = around.astype(BF16)

    first = jnp.zeros((LINE, CH), F32)
    second = jnp.zeros((LINE, CH), F32)
    for ph in range(4):
        act = dot(cells[...], out_matrix[:, ph * CH : (ph + 1) * CH])
        for n in range(10):
            at = slice(n * LINE, (n + 1) * LINE)
            grad = act[at] * slopes[ph, at, :]
            grads[ph, at, :] = grad
            first = first + grad
            second = second + grad * preact[ph, (n + 3) * LINE : (n + 4) * LINE, :]
    first, second = group_means([first, second])
    offset = first * inv
    slope = (second - mean * first) * inv * inv * inv
    base = mean * slope - offset

    def row_sums(evens, odds):
        known = {}

        def normal_grad(i, ph):
            if (i, ph) not in known:
                value = base - preact[ph, i * LINE : (i + 1) * LINE, :] * slope
                if 3 <= i < 13:
                    value = value + grads[ph, (i - 3) * LINE : (i - 2) * LINE, :] * inv
                known[i, ph] = value
            return known[i, ph]

        for s in range(2):
            lanes = slice(s * CH, (s + 1) * CH)
            for i in sorted(set(evens) | set(odds)):
                if i in evens:
                    pair = normal_grad(i, s) + normal_grad(i, 2 + s)
                    zgrad[0, i * LINE : (i + 1) * LINE, lanes] = pair.astype(BF16)
                if i in odds:
                    pair = [normal_grad(i, 2 + s)] if i >= 0 else []
                    pair += [normal_grad(i + 1, s)] if i + 1 < TL else []
                    zgrad[1, (i + 1) * LINE : (i + 2) * LINE, lanes] = sum(pair).astype(BF16)

    def input_grad(pieces):
        parts = []
        for pairs in (((0, 0),), ((0, 1), (1, 0)), ((1, 1),)):
            left, right = [], []
            for s, v in pairs:
                for a, kind, start in ((0, 1, 1), (1, 0, 0), (2, 1, 0)):
                    rows = [
                        zgrad[
                            kind,
                            (i + start) * LINE : (i + start + lines_of) * LINE,
                            s * CH : (s + 1) * CH,
                        ]
                        for i, lines_of in pieces
                    ]
                    left.append(rows[0] if len(rows) == 1 else jnp.concatenate(rows, axis=0))
                    right.append(folded[a, s * 2 + v])
            parts.append(
                lax.dot_general(
                    jnp.concatenate(left, axis=1),
                    jnp.concatenate(right, axis=1),
                    NT,
                    preferred_element_type=F32,
                )
            )
        size = parts[0].shape[0]
        place_rows = iota((size, CH), 0) & 15
        return (
            parts[1]
            + jnp.where(place_rows < 15, pltpu.roll(parts[0], size - 1, 0), 0.0)
            + jnp.where(place_rows > 0, pltpu.roll(parts[2], 1, 0), 0.0)
        ).astype(BF16)

    def grad_copy(side, part):
        rows = pl.ds((part if side == 0 else 1 - part) * 2 * LINE, 2 * LINE)
        return pltpu.make_async_remote_copy(
            src_ref=grad_send.at[side, rows],
            dst_ref=grad_recv.at[1 - side, rows],
            send_sem=gsend_sem.at[side, part],
            recv_sem=grecv_sem.at[1 - side, part],
            device_id=device(after if side else before),
            device_id_type=MESH,
        )

    row_sums((0, 1, 14, 15), (-1, 0, 1, 13, 14, 15))
    margin_grad = input_grad(((0, 2), (14, 2)))
    grad_send[0, 0 : 2 * LINE, :] = margin_grad[0 : 2 * LINE]
    grad_send[1, 2 * LINE : 4 * LINE, :] = margin_grad[2 * LINE : 4 * LINE]
    grad_copy(0, 0).start()
    grad_copy(1, 0).start()
    row_sums((2, 3, 12, 13), (2, 3, 11, 12))
    margin_grad = input_grad(((2, 2), (12, 2)))
    grad_send[0, 2 * LINE : 4 * LINE, :] = margin_grad[0 : 2 * LINE]
    grad_send[1, 0 : 2 * LINE, :] = margin_grad[2 * LINE : 4 * LINE]
    grad_copy(0, 1).start()
    grad_copy(1, 1).start()
    row_sums(range(4, 12), range(4, 11))
    own_grad[...] = input_grad(((4, 8),))

    rest = jnp.zeros((128 - 2 * LINE, CH), BF16)
    for part, rows in ((0, (2, 3, 4, 5)), (1, (0, 1, 6, 7))):
        grad_copy(0, part).wait_recv()
        grad_copy(1, part).wait_recv()
        for r in rows:
            side = r // 4
            at = (r % 4) * LINE
            terms = jnp.concatenate(
                [
                    own_grad[r * LINE : (r + 1) * LINE, :],
                    grad_recv[side, at : at + LINE, :],
                    rest,
                ],
                axis=0,
            )
            out[r] = dot(down_place if side else up_place, terms).astype(BF16)

    margin_copy(0, device(before)).wait_send()
    margin_copy(1, device(after)).wait_send()
    for d in range(1, nx):
        x_copy(d, mx).wait_send()
    pltpu.make_async_copy(z_send.at[others], z_send.at[others], zsend_sem).wait()
    for side in range(2):
        for part in range(2):
            grad_copy(side, part).wait_send()


def per_device(
    latent_feat,
    reward_grad,
    patches,
    up_weight,
    up_bias,
    norm_gain,
    norm_bias,
    out_weight,
    stem_weight,
    stem_bias,
    stem_gain,
    tile_count,
    tile_cols,
):
    sections = lax.axis_size("section")
    nx = lax.axis_size("tile") // NZ
    blocks = sections * nx * NZ
    operands = (
        latent_feat,
        reward_grad.reshape(-1, STEM).T,
        patches.T,
        up_weight,
        up_bias.reshape(1, CH),
        norm_gain.reshape(1, CH),
        norm_bias.reshape(1, CH),
        out_weight.transpose(0, 1, 3, 2).reshape(9, 3, CH),
        stem_weight,
        stem_bias.reshape(1, STEM),
        stem_gain.reshape(1, STEM),
        tile_count.reshape(1, blocks),
        tile_cols.T,
        jnp.asarray(np.concatenate([cell_lanes(), out_taps()], axis=1), BF16),
    )
    pinned = [pltpu.with_memory_space_constraint(array, pltpu.HBM) for array in operands]
    return pl.pallas_call(
        functools.partial(kernel, nx, sections),
        out_shape=pltpu.VMEM(latent_feat.shape, BF16),
        in_specs=[pl.BlockSpec(memory_space=pltpu.HBM)] * OPERANDS,
        out_specs=pl.BlockSpec(memory_space=pltpu.VMEM),
        scratch_shapes=[pltpu.VMEM(array.shape, array.dtype) for array in operands]
        + [
            pltpu.VMEM((18 * LINE, 3 * CH), BF16),
            pltpu.VMEM((4, 4 * CH, CH), BF16),
            pltpu.VMEM((3, 4, CH, CH), BF16),
            pltpu.VMEM((128, 4 * CH), BF16),
            pltpu.VMEM((128, CH), F32),
            pltpu.VMEM((2, 4 * LINE, CH), BF16),
            pltpu.VMEM((2, 4 * LINE, CH), BF16),
            pltpu.VMEM((4 * nx * NZ, 128), F32),
            pltpu.VMEM((nx, 2 * NZ, 128), BF16),
            pltpu.VMEM((nx, 2 * NZ, 128), BF16),
            pltpu.VMEM((NZ, 2 * nx, 128), BF16),
            pltpu.VMEM((NZ, 2 * nx, 128), BF16),
            pltpu.VMEM((4, TL * LINE, CH), F32),
            pltpu.VMEM((4, 10 * LINE, CH), F32),
            pltpu.VMEM((4, 10 * LINE, CH), F32),
            pltpu.VMEM((2, 17 * LINE, 2 * CH), BF16),
            pltpu.VMEM((10 * LINE, 128), BF16),
            pltpu.VMEM((8 * LINE, CH), BF16),
            pltpu.VMEM((2, 4 * LINE, CH), BF16),
            pltpu.VMEM((2, 4 * LINE, CH), BF16),
            pltpu.VMEM((CH, CH), BF16),
            pltpu.SemaphoreType.DMA((OPERANDS,)),
            pltpu.SemaphoreType.DMA((2,)),
            pltpu.SemaphoreType.DMA((2,)),
            pltpu.SemaphoreType.DMA((nx - 1,)),
            pltpu.SemaphoreType.DMA((nx - 1,)),
            pltpu.SemaphoreType.DMA,
            pltpu.SemaphoreType.DMA,
            pltpu.SemaphoreType.DMA((2, 2)),
            pltpu.SemaphoreType.DMA((2, 2)),
        ],
        compiler_params=pltpu.CompilerParams(
            collective_id=0, has_side_effects=True, vmem_limit_bytes=48 * 1024 * 1024
        ),
    )(*pinned)


def solution(mesh):
    return jax.shard_map(
        per_device,
        mesh=mesh,
        in_specs=(
            P(("section", "tile"), None, None),
            P("section", "tile", None),
            P("section", "tile"),
        )
        + (P(),) * 10,
        out_specs=P(("section", "tile"), None, None),
        check_vma=False,
    )
```

```python
import functools

import jax
import jax.numpy as jnp
import numpy as np
from jax import lax
from jax.experimental import pallas as pl
from jax.experimental.pallas import tpu as pltpu
from jax.sharding import PartitionSpec as P

EPS = 1e-06
CH = 256
STEM = 192
PIX = 48
TL = 16
SLOTS = 3
NZ = 16
LINE = SLOTS * TL
F32 = jnp.float32
BF16 = jnp.bfloat16
MESH = pl.DeviceIdType.MESH
NT = (((1,), (1,)), ((), ()))
TN = (((0,), (0,)), ((), ()))
(
    LATENT,
    REWARD,
    PIXELS,
    UP_WEIGHT,
    UP_BIAS,
    NORM_GAIN,
    NORM_BIAS,
    OUT_WEIGHT,
    STEM_WEIGHT,
    STEM_BIAS,
    STEM_GAIN,
    TILE_COUNT,
    TILE_COLS,
    TABLES,
) = range(14)
OPERANDS = 14
STEM_LOADS = (PIXELS, STEM_WEIGHT, STEM_BIAS, REWARD, STEM_GAIN)
BLOCK_LOADS = (TILE_COLS, TILE_COUNT)
LARGE_LOADS = (LATENT, UP_WEIGHT)
LATE_LOADS = (OUT_WEIGHT, TABLES, UP_BIAS, NORM_GAIN, NORM_BIAS)
TAPS = ((0, 0), (0, 1), (1, 0), (1, 1))


def out_taps():
    table = np.zeros((4, 128, 128), np.float32)
    for r in range(2):
        for s in range(2):
            for di in range(3):
                for dj in range(3):
                    for c in range(3):
                        for y in range(2):
                            for x in range(2):
                                a = r + 1 - (2 * (di - 1) + y)
                                e = s + 1 - (2 * (dj - 1) + x)
                                if 0 <= a < 3 and 0 <= e < 3:
                                    lane = (di * 3 + dj) * 12 + c * 4 + y * 2 + x
                                    table[r * 2 + s, lane, (a * 3 + e) * 8 + c] = 1
    return table.transpose(1, 0, 2).reshape(128, 512)


def cell_lanes():
    table = np.zeros((2, 64, 2, 2, 2, 128), np.float32)
    for odd in range(2):
        for c in range(3):
            for dy in range(4):
                for dx in range(4):
                    for copy in range(9):
                        lane = copy * 12 + c * 4 + (dy % 2) * 2 + dx % 2
                        table[odd, c * 16 + dy * 4 + dx, odd, dx // 2, dy // 2, lane] = 1
    return table.reshape(128, 1024)


def iota(shape, axis):
    return lax.broadcasted_iota(jnp.int32, shape, axis)


def dot(a, b):
    return jnp.dot(a, b, preferred_element_type=F32)


def three_rows(row):
    high = row.astype(BF16).astype(F32)
    rest = row - high
    middle = rest.astype(BF16).astype(F32)
    low = rest - middle
    at = iota((16, row.shape[1]), 0)
    rows = jnp.where(at == 0, high, jnp.where(at == 1, middle, jnp.where(at == 2, low, 0.0)))
    return rows.astype(BF16)


def kernel(nx, sections, *refs):
    operands, out, scratch = refs[:OPERANDS], refs[OPERANDS], refs[OPERANDS + 1 :]
    copies, scratch = scratch[:OPERANDS], scratch[OPERANDS:]
    (
        latent,
        reward,
        pixels,
        up_weight,
        up_bias,
        norm_gain,
        norm_bias,
        out_weight,
        stem_weight,
        stem_bias,
        stem_gain,
        tile_count,
        tile_cols,
        tables,
    ) = copies
    (
        wide,
        combined,
        folded,
        out_matrix,
        out_rows,
        margin_send,
        margin_recv,
        image,
        x_send,
        x_recv,
        z_send,
        z_recv,
        preact,
        slopes,
        grads,
        zgrad,
        cells,
        own_grad,
        grad_send,
        grad_recv,
        groups,
        load_sem,
        msend_sem,
        mrecv_sem,
        xsend_sem,
        xrecv_sem,
        zsend_sem,
        zrecv_sem,
        gsend_sem,
        grecv_sem,
    ) = scratch
    tiles = nx * NZ
    blocks = sections * tiles
    section = lax.axis_index("section")
    tile = lax.axis_index("tile")
    mx = lax.div(tile, NZ)
    mz = lax.rem(tile, NZ)
    block = section * tiles + tile
    before = lax.rem(block + blocks - 1, blocks)
    after = lax.rem(block + 1, blocks)

    def device(index):
        return (lax.div(index, tiles), lax.rem(index, tiles))

    def along_x(index):
        return (section, index * NZ + mz)

    def along_z(index):
        return (section, mx * NZ + index)

    barrier = pltpu.get_barrier_semaphore()

    def greet(target):
        pl.semaphore_signal(barrier, inc=1, device_id=target, device_id_type=MESH)

    def load(n):
        return pltpu.make_async_copy(operands[n], copies[n], load_sem.at[n])

    for n in BLOCK_LOADS + STEM_LOADS + LARGE_LOADS:
        load(n).start()

    for d in range(1, NZ):
        greet(along_z(lax.rem(mz + d, NZ)))
    for d in range(1, nx):
        greet(along_x(lax.rem(mx + d, nx)))
    greet(device(before))
    greet(device(after))

    row_at = iota((CH, CH), 0)
    col_at = iota((CH, CH), 1)
    groups[...] = ((row_at >> 3) == (col_at >> 3)).astype(F32).astype(BF16)
    zeros = jnp.zeros((LINE, 3 * CH), BF16)
    wide[0:LINE, :] = zeros
    wide[17 * LINE : 18 * LINE, :] = zeros
    out_rows[...] = jnp.zeros_like(out_rows)
    to_row = iota((128, 128), 0)
    reorder = (
        iota((128, 128), 1) == ((to_row >> 1) & 3) * (2 * NZ) + (to_row & 1) * NZ + (to_row >> 3)
    ).astype(F32).astype(BF16)
    shift_low = ((col_at == row_at - 1) & ((row_at & 15) != 0)).astype(F32).astype(BF16)
    shift_high = ((col_at == row_at + 1) & ((row_at & 15) != 15)).astype(F32).astype(BF16)
    keep_before = block != 0
    keep_after = block != blocks - 1

    at3 = iota((SLOTS, blocks), 1)
    at1 = iota((1, blocks), 1)
    for n in BLOCK_LOADS + STEM_LOADS + (LATENT,):
        load(n).wait()
    all_cols = tile_cols[...].astype(F32)

    def columns(index):
        return jnp.sum(jnp.where(at3 == index, all_cols, 0.0), axis=1, keepdims=True)

    def count(index):
        counts = tile_count[...].astype(F32)
        return jnp.sum(jnp.where(at1 == index, counts, 0.0), axis=1, keepdims=True)

    cols_own, cols_before, cols_after = columns(block), columns(before), columns(after)

    def slot_rows(cols, width):
        return jnp.concatenate(
            [jnp.broadcast_to(cols[k : k + 1, :], (TL, width)) for k in range(SLOTS)], axis=0
        )

    place = (iota((LINE, 128), 0) & 15).astype(F32)
    lane_f = iota((LINE, 128), 1).astype(F32)

    def gather_rows(cols):
        return (lane_f == slot_rows(cols, 128) + place).astype(F32)

    pick_own = gather_rows(cols_own)
    pick_up = jnp.concatenate([pick_own, gather_rows(cols_before)], axis=0).astype(BF16)
    pick_down = jnp.concatenate([pick_own, gather_rows(cols_after)], axis=0).astype(BF16)
    for r in range(8):
        side = r // 4
        rows = dot(pick_down if side else pick_up, latent[r]).astype(BF16)
        wide[(5 + r) * LINE : (6 + r) * LINE, CH : 2 * CH] = rows[0:LINE]
        margin_send[side, (r % 4) * LINE : (r % 4 + 1) * LINE, :] = rows[LINE : 2 * LINE]


    ones = jnp.ones((16, CH), BF16)

    def column_of(row):
        return lax.dot_general(three_rows(row), ones, TN, preferred_element_type=F32)

    weight = stem_weight[...]
    stem = lax.dot_general(weight, pixels[...], TN, preferred_element_type=F32) + column_of(
        stem_bias[...]
    )
    scaled = reward[...].astype(F32) * column_of(stem_gain[...])
    centred = stem - jnp.mean(stem, axis=0, keepdims=True)
    scaled = scaled - jnp.mean(scaled, axis=0, keepdims=True)
    inverse = lax.rsqrt(jnp.mean(centred * centred, axis=0, keepdims=True) + EPS)
    along = jnp.mean(scaled * centred, axis=0, keepdims=True) * inverse * inverse
    stem_grad = (scaled - centred * along) * inverse
    padded_weight = jnp.concatenate([weight, jnp.zeros((128 - PIX, STEM), BF16)], axis=0)
    pixel_grad = dot(padded_weight, stem_grad.astype(BF16))
    image[...] = pixel_grad.astype(BF16).astype(F32).T
    left_half = iota((tiles, 128), 1) < 64
    for h in range(2):
        even, odd = [image[pl.ds(2 * h + n, tiles, stride=4), :] for n in range(2)]
        both = jnp.where(left_half, even, pltpu.roll(odd, 64, 1)).astype(BF16)
        x_send[:, h * NZ : (h + 1) * NZ, :] = both.reshape(nx, NZ, 128)
    x_recv[pl.ds(mx, 1)] = x_send[pl.ds(mx, 1)]

    pl.semaphore_wait(barrier, 2 + (nx - 1) + (NZ - 1))

    def margin_copy(side, target):
        return pltpu.make_async_remote_copy(
            src_ref=margin_send.at[side],
            dst_ref=margin_recv.at[1 - side],
            send_sem=msend_sem.at[side],
            recv_sem=mrecv_sem.at[1 - side],
            device_id=target,
            device_id_type=MESH,
        )

    margin_copy(0, device(before)).start()
    margin_copy(1, device(after)).start()

    def x_copy(d, slot):
        target = lax.rem(mx + d, nx)
        return pltpu.make_async_remote_copy(
            src_ref=x_send.at[target],
            dst_ref=x_recv.at[slot],
            send_sem=xsend_sem.at[d - 1],
            recv_sem=xrecv_sem.at[d - 1],
            device_id=along_x(target),
            device_id_type=MESH,
        )

    for d in range(1, nx):
        x_copy(d, mx).start()
    for n in LATE_LOADS:
        load(n).start()

    def sums(first, second, third):
        return {(0, 0): first, (0, 1): second + third, (1, 0): first + second, (1, 1): third}

    def weight_rows(n):
        rows = pl.ds(pl.multiple_of(n * 16, 16), 16)
        by_col = [sums(*[up_weight[a, e, rows, :].astype(F32) for e in range(3)]) for a in range(3)]
        for s, v in TAPS:
            for a in range(3):
                folded[a, s * 2 + v, rows, :] = by_col[a][s, v].astype(BF16)
            by_tap = sums(*[by_col[a][s, v] for a in range(3)])
            for r, t in TAPS:
                at = pl.ds(pl.multiple_of((t * 2 + v) * CH + n * 16, 16), 16)
                combined[r * 2 + s, at, :] = by_tap[r, t].astype(BF16)

    def weight_chunk(n, carry):
        weight_rows(n)
        return carry

    load(UP_WEIGHT).wait()
    lax.fori_loop(0, CH // 16, weight_chunk, 0)
    source = iota((1, 512), 1)
    source_x, source_z = (source >> 1) & 3, (source >> 3) & 15
    source_row = 2 * (source & 1) + (source >> 8)
    cell_of = 2 * (source_x * NZ + source_z) + ((source >> 7) & 1)
    source_key = (cell_of + 1000 * source_row).astype(F32)
    own_rows = slot_rows(cols_own, 512)
    place_wide = (iota((LINE, 512), 0) & 15).astype(F32)
    inside = (place_wide >= 4.0) & (place_wide < 12.0)
    choose = jnp.concatenate(
        [
            (jnp.where(inside, own_rows + place_wide + 1000.0 * pr, -1.0) == source_key)
            .astype(F32)
            .astype(BF16)
            for pr in range(4)
        ],
        axis=0,
    )

    lane = iota((128, 128), 1)
    column = iota((128, 128), 0).astype(F32)
    slot_of = lane >> 4
    offset_of = (lane & 15).astype(F32)

    def place_columns(cols, live, first_slot):
        start = jnp.where(
            slot_of == first_slot,
            jnp.broadcast_to(cols[0:1, :], (128, 128)),
            jnp.where(
                slot_of == first_slot + 1,
                jnp.broadcast_to(cols[1:2, :], (128, 128)),
                jnp.broadcast_to(cols[2:3, :], (128, 128)),
            ),
        )
        relative = (slot_of - first_slot).astype(F32)
        valid = (relative >= 0.0) & (relative < live) & (relative < float(SLOTS))
        return jnp.where(valid & (column == start + offset_of), 1.0, 0.0)

    none = jnp.zeros((1, 1), F32)
    own_place = place_columns(cols_own, count(block), 0)
    up_place = (
        own_place
        + place_columns(cols_before, jnp.where(keep_before, count(before), none), SLOTS)
    ).astype(BF16)
    down_place = (
        own_place + place_columns(cols_after, jnp.where(keep_after, count(after), none), SLOTS)
    ).astype(BF16)

    for n in LATE_LOADS:
        load(n).wait()
    for ae in range(9):
        out_rows[ae * 8 : ae * 8 + 3, :] = out_weight[ae].astype(F32)
    flat_taps = out_rows[...].astype(BF16)
    for ph in range(4):
        out_matrix[:, ph * CH : (ph + 1) * CH] = dot(
            tables[:, 1024 + ph * 128 : 1024 + (ph + 1) * 128], flat_taps
        ).astype(BF16)

    for d in range(1, nx):
        x_copy(d, lax.rem(mx + nx - d, nx)).wait_recv()
    by_z = dot(reorder, x_recv[...].reshape(2 * tiles, 128))
    z_send[...] = by_z.reshape(NZ, 2 * nx, 128).astype(BF16)

    for far in (8, 7, 9, 6, 10, 5, 11, 4, 12, 3, 13, 2, 14, 1, 15):
        target = lax.rem(mz + far, NZ)
        pltpu.make_async_remote_copy(
            src_ref=z_send.at[target],
            dst_ref=z_recv.at[mz],
            send_sem=zsend_sem,
            recv_sem=zrecv_sem,
            device_id=along_z(target),
            device_id_type=MESH,
        ).start()
    z_recv[pl.ds(mz, 1)] = z_send[pl.ds(mz, 1)]

    margin_copy(0, device(before)).wait_recv()
    margin_copy(1, device(after)).wait_recv()
    top = margin_recv[0]
    bottom = margin_recv[1]
    wide[LINE : 5 * LINE, CH : 2 * CH] = jnp.where(keep_before, top, jnp.zeros_like(top))
    wide[13 * LINE : 17 * LINE, CH : 2 * CH] = jnp.where(
        keep_after, bottom, jnp.zeros_like(bottom)
    )
    for part in range(SLOTS):
        here = slice(LINE + part * CH, LINE + (part + 1) * CH)
        inputs = wide[here, CH : 2 * CH]
        wide[here, 0:CH] = dot(shift_low, inputs).astype(BF16)
        wide[here, 2 * CH : 3 * CH] = dot(shift_high, inputs).astype(BF16)

    bias = up_bias[...]
    def group_means(parts):
        rows = []
        for term in parts:
            high = term.astype(BF16).astype(F32)
            rest = term - high
            middle = rest.astype(BF16).astype(F32)
            rows += [high, middle, rest - middle]
        grouped = dot(jnp.concatenate(rows, axis=0).astype(BF16), groups[...])
        means = []
        for n in range(len(parts)):
            first = grouped[3 * n * LINE : (3 * n + 1) * LINE]
            second = grouped[(3 * n + 1) * LINE : (3 * n + 2) * LINE]
            third = grouped[(3 * n + 2) * LINE : (3 * n + 3) * LINE]
            line = (first + second + third) * (1.0 / 8192.0)
            means.append(
                jnp.concatenate(
                    [
                        jnp.broadcast_to(
                            jnp.sum(line[k * TL : (k + 1) * TL], axis=0, keepdims=True), (TL, CH)
                        )
                        for k in range(SLOTS)
                    ],
                    axis=0,
                )
            )
        return means

    def outputs(ph):
        r, s = ph // 2, ph % 2
        features = jnp.concatenate(
            [
                wide[(r + t) * LINE : (r + t + TL) * LINE, s * CH : (s + 2) * CH]
                for t in range(2)
            ],
            axis=1,
        )
        return dot(features, combined[ph]).reshape(TL, LINE, CH)

    value = outputs(0)
    (centre,) = group_means([jnp.sum(value, axis=0) + bias * float(TL)])
    to_centre = bias - 4.0 * centre
    total = jnp.zeros((LINE, CH), F32)
    square = jnp.zeros((LINE, CH), F32)
    for ph in range(4):
        off = (value if ph == 0 else outputs(ph)) + to_centre
        preact[ph] = off.reshape(TL * LINE, CH)
        total = total + jnp.sum(off, axis=0)
        square = square + jnp.sum(off * off, axis=0)
    mean, square = group_means([total, square])
    inv = lax.rsqrt(jnp.maximum(square - mean * mean, 0.0) + EPS)
    gain = jnp.broadcast_to(norm_gain[...], (LINE, CH))
    shift = jnp.broadcast_to(norm_bias[...], (LINE, CH))
    half_gain = 0.5 * gain
    half_scale = inv * half_gain
    half_shift = 0.5 * shift - mean * half_scale

    def silu_slopes(n, carry):
        for step in range(2):
            source_at = pl.ds(pl.multiple_of((2 * n + step + 3) * LINE, LINE), LINE)
            target_at = pl.ds(pl.multiple_of((2 * n + step) * LINE, LINE), LINE)
            for ph in range(4):
                half = preact[ph, source_at, :] * half_scale + half_shift
                curve = jnp.tanh(half)
                slopes[ph, target_at, :] = (
                    (1.0 + curve) + half * (1.0 - curve * curve)
                ) * half_gain
        return carry

    lax.fori_loop(0, 5, silu_slopes, 0)

    others = pl.ds(0, NZ - 1)
    pltpu.make_async_copy(z_recv.at[others], z_recv.at[others], zrecv_sem).wait()
    arrived = z_recv[...].astype(F32).reshape(2 * tiles, 128).astype(BF16)
    spread = dot(arrived, tables[:, 0:1024]).astype(BF16)
    stacked = jnp.concatenate([spread[:, 256 * n : 256 * (n + 1)] for n in range(4)], axis=0)
    found = dot(choose, stacked)
    lane_wide = iota((1, 256), 1) & 127
    copy_wide = sum([(lane_wide >= 12 * c).astype(jnp.int32) for c in range(1, 9)])
    col_wide = copy_wide - 3 * (
        (copy_wide >= 3).astype(jnp.int32) + (copy_wide >= 6).astype(jnp.int32)
    )
    copy_one = copy_wide[:, 0:128]
    low = pltpu.roll(found, 1, 0)
    high = pltpu.roll(found, 4 * LINE - 1, 0)
    merged = jnp.where(col_wide == 0, low, jnp.where(col_wide == 1, found, high))
    lines = []
    for pr in range(4):
        line = merged[pr * LINE : (pr + 1) * LINE]
        lines += [line[:, 0:128], line[:, 128:256]]
    nothing = jnp.zeros((LINE, 128), F32)

    def line_at(index):
        return lines[index] if 0 <= index < 8 else nothing

    for i in range(3, 13):
        around = jnp.where(
            copy_one < 3, line_at(i - 5), jnp.where(copy_one < 6, line_at(i - 4), line_at(i - 3))
        )
        cells[(i - 3) * LINE : (i - 2) * LINE, :] = around.astype(BF16)

    first = jnp.zeros((LINE, CH), F32)
    second = jnp.zeros((LINE, CH), F32)
    for ph in range(4):
        act = dot(cells[...], out_matrix[:, ph * CH : (ph + 1) * CH])
        for n in range(10):
            at = slice(n * LINE, (n + 1) * LINE)
            grad = act[at] * slopes[ph, at, :]
            grads[ph, at, :] = grad
            first = first + grad
            second = second + grad * preact[ph, (n + 3) * LINE : (n + 4) * LINE, :]
    first, second = group_means([first, second])
    offset = first * inv
    slope = (second - mean * first) * inv * inv * inv
    base = mean * slope - offset

    def row_sums(evens, odds):
        known = {}

        def normal_grad(i, ph):
            if (i, ph) not in known:
                value = base - preact[ph, i * LINE : (i + 1) * LINE, :] * slope
                if 3 <= i < 13:
                    value = value + grads[ph, (i - 3) * LINE : (i - 2) * LINE, :] * inv
                known[i, ph] = value
            return known[i, ph]

        for s in range(2):
            lanes = slice(s * CH, (s + 1) * CH)
            for i in sorted(set(evens) | set(odds)):
                if i in evens:
                    pair = normal_grad(i, s) + normal_grad(i, 2 + s)
                    zgrad[0, i * LINE : (i + 1) * LINE, lanes] = pair.astype(BF16)
                if i in odds:
                    pair = [normal_grad(i, 2 + s)] if i >= 0 else []
                    pair += [normal_grad(i + 1, s)] if i + 1 < TL else []
                    zgrad[1, (i + 1) * LINE : (i + 2) * LINE, lanes] = sum(pair).astype(BF16)

    def input_grad(pieces):
        parts = []
        for pairs in (((0, 0),), ((0, 1), (1, 0)), ((1, 1),)):
            left, right = [], []
            for s, v in pairs:
                for a, kind, start in ((0, 1, 1), (1, 0, 0), (2, 1, 0)):
                    rows = [
                        zgrad[
                            kind,
                            (i + start) * LINE : (i + start + lines_of) * LINE,
                            s * CH : (s + 1) * CH,
                        ]
                        for i, lines_of in pieces
                    ]
                    left.append(rows[0] if len(rows) == 1 else jnp.concatenate(rows, axis=0))
                    right.append(folded[a, s * 2 + v])
            parts.append(
                lax.dot_general(
                    jnp.concatenate(left, axis=1),
                    jnp.concatenate(right, axis=1),
                    NT,
                    preferred_element_type=F32,
                )
            )
        size = parts[0].shape[0]
        place_rows = iota((size, CH), 0) & 15
        return (
            parts[1]
            + jnp.where(place_rows < 15, pltpu.roll(parts[0], size - 1, 0), 0.0)
            + jnp.where(place_rows > 0, pltpu.roll(parts[2], 1, 0), 0.0)
        ).astype(BF16)

    def grad_copy(side, part):
        rows = pl.ds((part if side == 0 else 1 - part) * 2 * LINE, 2 * LINE)
        return pltpu.make_async_remote_copy(
            src_ref=grad_send.at[side, rows],
            dst_ref=grad_recv.at[1 - side, rows],
            send_sem=gsend_sem.at[side, part],
            recv_sem=grecv_sem.at[1 - side, part],
            device_id=device(after if side else before),
            device_id_type=MESH,
        )

    row_sums((0, 1, 14, 15), (-1, 0, 1, 13, 14, 15))
    margin_grad = input_grad(((0, 2), (14, 2)))
    grad_send[0, 0 : 2 * LINE, :] = margin_grad[0 : 2 * LINE]
    grad_send[1, 2 * LINE : 4 * LINE, :] = margin_grad[2 * LINE : 4 * LINE]
    grad_copy(0, 0).start()
    grad_copy(1, 0).start()
    row_sums((2, 3, 12, 13), (2, 3, 11, 12))
    margin_grad = input_grad(((2, 2), (12, 2)))
    grad_send[0, 2 * LINE : 4 * LINE, :] = margin_grad[0 : 2 * LINE]
    grad_send[1, 0 : 2 * LINE, :] = margin_grad[2 * LINE : 4 * LINE]
    grad_copy(0, 1).start()
    grad_copy(1, 1).start()
    row_sums(range(4, 12), range(4, 11))
    own_grad[...] = input_grad(((4, 8),))

    margin_copy(0, device(before)).wait_send()
    margin_copy(1, device(after)).wait_send()
    for d in range(1, nx):
        x_copy(d, mx).wait_send()
    pltpu.make_async_copy(z_send.at[others], z_send.at[others], zsend_sem).wait()

    rest = jnp.zeros((128 - 2 * LINE, CH), BF16)
    for part, rows in ((0, (2, 3, 4, 5)), (1, (0, 1, 6, 7))):
        grad_copy(0, part).wait_recv()
        grad_copy(1, part).wait_recv()
        for r in rows:
            side = r // 4
            at = (r % 4) * LINE
            terms = jnp.concatenate(
                [
                    own_grad[r * LINE : (r + 1) * LINE, :],
                    grad_recv[side, at : at + LINE, :],
                    rest,
                ],
                axis=0,
            )
            out[r] = dot(down_place if side else up_place, terms).astype(BF16)

    for side in range(2):
        for part in range(2):
            grad_copy(side, part).wait_send()


def per_device(
    latent_feat,
    reward_grad,
    patches,
    up_weight,
    up_bias,
    norm_gain,
    norm_bias,
    out_weight,
    stem_weight,
    stem_bias,
    stem_gain,
    tile_count,
    tile_cols,
):
    sections = lax.axis_size("section")
    nx = lax.axis_size("tile") // NZ
    blocks = sections * nx * NZ
    operands = (
        latent_feat,
        reward_grad.reshape(-1, STEM).T,
        patches.T,
        up_weight,
        up_bias.reshape(1, CH),
        norm_gain.reshape(1, CH),
        norm_bias.reshape(1, CH),
        out_weight.transpose(0, 1, 3, 2).reshape(9, 3, CH),
        stem_weight,
        stem_bias.reshape(1, STEM),
        stem_gain.reshape(1, STEM),
        tile_count.reshape(1, blocks),
        tile_cols.T,
        jnp.asarray(np.concatenate([cell_lanes(), out_taps()], axis=1), BF16),
    )
    pinned = [pltpu.with_memory_space_constraint(array, pltpu.HBM) for array in operands]
    return pl.pallas_call(
        functools.partial(kernel, nx, sections),
        out_shape=pltpu.VMEM(latent_feat.shape, BF16),
        in_specs=[pl.BlockSpec(memory_space=pltpu.HBM)] * OPERANDS,
        out_specs=pl.BlockSpec(memory_space=pltpu.VMEM),
        scratch_shapes=[pltpu.VMEM(array.shape, array.dtype) for array in operands]
        + [
            pltpu.VMEM((18 * LINE, 3 * CH), BF16),
            pltpu.VMEM((4, 4 * CH, CH), BF16),
            pltpu.VMEM((3, 4, CH, CH), BF16),
            pltpu.VMEM((128, 4 * CH), BF16),
            pltpu.VMEM((128, CH), F32),
            pltpu.VMEM((2, 4 * LINE, CH), BF16),
            pltpu.VMEM((2, 4 * LINE, CH), BF16),
            pltpu.VMEM((4 * nx * NZ, 128), F32),
            pltpu.VMEM((nx, 2 * NZ, 128), BF16),
            pltpu.VMEM((nx, 2 * NZ, 128), BF16),
            pltpu.VMEM((NZ, 2 * nx, 128), BF16),
            pltpu.VMEM((NZ, 2 * nx, 128), BF16),
            pltpu.VMEM((4, TL * LINE, CH), F32),
            pltpu.VMEM((4, 10 * LINE, CH), F32),
            pltpu.VMEM((4, 10 * LINE, CH), F32),
            pltpu.VMEM((2, 17 * LINE, 2 * CH), BF16),
            pltpu.VMEM((10 * LINE, 128), BF16),
            pltpu.VMEM((8 * LINE, CH), BF16),
            pltpu.VMEM((2, 4 * LINE, CH), BF16),
            pltpu.VMEM((2, 4 * LINE, CH), BF16),
            pltpu.VMEM((CH, CH), BF16),
            pltpu.SemaphoreType.DMA((OPERANDS,)),
            pltpu.SemaphoreType.DMA((2,)),
            pltpu.SemaphoreType.DMA((2,)),
            pltpu.SemaphoreType.DMA((nx - 1,)),
            pltpu.SemaphoreType.DMA((nx - 1,)),
            pltpu.SemaphoreType.DMA,
            pltpu.SemaphoreType.DMA,
            pltpu.SemaphoreType.DMA((2, 2)),
            pltpu.SemaphoreType.DMA((2, 2)),
        ],
        compiler_params=pltpu.CompilerParams(
            collective_id=0, has_side_effects=True, vmem_limit_bytes=48 * 1024 * 1024
        ),
    )(*pinned)


def solution(mesh):
    return jax.shard_map(
        per_device,
        mesh=mesh,
        in_specs=(
            P(("section", "tile"), None, None),
            P("section", "tile", None),
            P("section", "tile"),
        )
        + (P(),) * 10,
        out_specs=P(("section", "tile"), None, None),
        check_vma=False,
    )
```

```python
import functools

import jax
import jax.numpy as jnp
import numpy as np
from jax import lax
from jax.experimental import pallas as pl
from jax.experimental.pallas import tpu as pltpu
from jax.sharding import PartitionSpec as P

EPS = 1e-06
CH = 256
STEM = 192
PIX = 48
TL = 16
SLOTS = 3
NZ = 16
LINE = SLOTS * TL
F32 = jnp.float32
BF16 = jnp.bfloat16
MESH = pl.DeviceIdType.MESH
NT = (((1,), (1,)), ((), ()))
TN = (((0,), (0,)), ((), ()))
(
    LATENT,
    REWARD,
    PIXELS,
    UP_WEIGHT,
    UP_BIAS,
    NORM_GAIN,
    NORM_BIAS,
    OUT_WEIGHT,
    STEM_WEIGHT,
    STEM_BIAS,
    STEM_GAIN,
    TILE_COUNT,
    TILE_COLS,
    TABLES,
) = range(14)
OPERANDS = 14
STEM_LOADS = (PIXELS, STEM_WEIGHT, STEM_BIAS, REWARD, STEM_GAIN)
BLOCK_LOADS = (TILE_COLS, TILE_COUNT)
LARGE_LOADS = (LATENT, UP_WEIGHT)
LATE_LOADS = (OUT_WEIGHT, TABLES, UP_BIAS, NORM_GAIN, NORM_BIAS)
TAPS = ((0, 0), (0, 1), (1, 0), (1, 1))


def out_taps():
    table = np.zeros((4, 128, 128), np.float32)
    for r in range(2):
        for s in range(2):
            for di in range(3):
                for dj in range(3):
                    for c in range(3):
                        for y in range(2):
                            for x in range(2):
                                a = r + 1 - (2 * (di - 1) + y)
                                e = s + 1 - (2 * (dj - 1) + x)
                                if 0 <= a < 3 and 0 <= e < 3:
                                    lane = (di * 3 + dj) * 12 + c * 4 + y * 2 + x
                                    table[r * 2 + s, lane, (a * 3 + e) * 8 + c] = 1
    return table.transpose(1, 0, 2).reshape(128, 512)


def cell_lanes():
    table = np.zeros((2, 64, 2, 2, 2, 128), np.float32)
    for odd in range(2):
        for c in range(3):
            for dy in range(4):
                for dx in range(4):
                    for copy in range(9):
                        lane = copy * 12 + c * 4 + (dy % 2) * 2 + dx % 2
                        table[odd, c * 16 + dy * 4 + dx, odd, dx // 2, dy // 2, lane] = 1
    return table.reshape(128, 1024)


def iota(shape, axis):
    return lax.broadcasted_iota(jnp.int32, shape, axis)


def dot(a, b):
    return jnp.dot(a, b, preferred_element_type=F32)


def three_rows(row):
    high = row.astype(BF16).astype(F32)
    rest = row - high
    middle = rest.astype(BF16).astype(F32)
    low = rest - middle
    at = iota((16, row.shape[1]), 0)
    rows = jnp.where(at == 0, high, jnp.where(at == 1, middle, jnp.where(at == 2, low, 0.0)))
    return rows.astype(BF16)


def kernel(nx, sections, *refs):
    operands, out, scratch = refs[:OPERANDS], refs[OPERANDS], refs[OPERANDS + 1 :]
    copies, scratch = scratch[:OPERANDS], scratch[OPERANDS:]
    (
        latent,
        reward,
        pixels,
        up_weight,
        up_bias,
        norm_gain,
        norm_bias,
        out_weight,
        stem_weight,
        stem_bias,
        stem_gain,
        tile_count,
        tile_cols,
        tables,
    ) = copies
    (
        wide,
        combined,
        folded,
        out_matrix,
        out_rows,
        margin_send,
        margin_recv,
        image,
        x_send,
        x_recv,
        z_send,
        z_recv,
        preact,
        slopes,
        grads,
        zgrad,
        cells,
        own_grad,
        grad_send,
        grad_recv,
        groups,
        load_sem,
        msend_sem,
        mrecv_sem,
        xsend_sem,
        xrecv_sem,
        zsend_sem,
        zrecv_sem,
        gsend_sem,
        grecv_sem,
    ) = scratch
    tiles = nx * NZ
    blocks = sections * tiles
    section = lax.axis_index("section")
    tile = lax.axis_index("tile")
    mx = lax.div(tile, NZ)
    mz = lax.rem(tile, NZ)
    block = section * tiles + tile
    before = lax.rem(block + blocks - 1, blocks)
    after = lax.rem(block + 1, blocks)

    def device(index):
        return (lax.div(index, tiles), lax.rem(index, tiles))

    def along_x(index):
        return (section, index * NZ + mz)

    def along_z(index):
        return (section, mx * NZ + index)

    barrier = pltpu.get_barrier_semaphore()

    def greet(target):
        pl.semaphore_signal(barrier, inc=1, device_id=target, device_id_type=MESH)

    def load(n):
        return pltpu.make_async_copy(operands[n], copies[n], load_sem.at[n])

    for n in BLOCK_LOADS + STEM_LOADS + LARGE_LOADS:
        load(n).start()

    for d in range(1, NZ):
        greet(along_z(lax.rem(mz + d, NZ)))
    for d in range(1, nx):
        greet(along_x(lax.rem(mx + d, nx)))
    greet(device(before))
    greet(device(after))

    row_at = iota((CH, CH), 0)
    col_at = iota((CH, CH), 1)
    groups[...] = ((row_at >> 3) == (col_at >> 3)).astype(F32).astype(BF16)
    zeros = jnp.zeros((LINE, 3 * CH), BF16)
    wide[0:LINE, :] = zeros
    wide[17 * LINE : 18 * LINE, :] = zeros
    out_rows[...] = jnp.zeros_like(out_rows)
    to_row = iota((128, 128), 0)
    reorder = (
        iota((128, 128), 1) == ((to_row >> 1) & 3) * (2 * NZ) + (to_row & 1) * NZ + (to_row >> 3)
    ).astype(F32).astype(BF16)
    shift_low = ((col_at == row_at - 1) & ((row_at & 15) != 0)).astype(F32).astype(BF16)
    shift_high = ((col_at == row_at + 1) & ((row_at & 15) != 15)).astype(F32).astype(BF16)
    keep_before = block != 0
    keep_after = block != blocks - 1

    at3 = iota((SLOTS, blocks), 1)
    at1 = iota((1, blocks), 1)
    for n in BLOCK_LOADS + STEM_LOADS + (LATENT,):
        load(n).wait()
    all_cols = tile_cols[...].astype(F32)

    def columns(index):
        return jnp.sum(jnp.where(at3 == index, all_cols, 0.0), axis=1, keepdims=True)

    def count(index):
        counts = tile_count[...].astype(F32)
        return jnp.sum(jnp.where(at1 == index, counts, 0.0), axis=1, keepdims=True)

    cols_own, cols_before, cols_after = columns(block), columns(before), columns(after)

    def slot_rows(cols, width):
        return jnp.concatenate(
            [jnp.broadcast_to(cols[k : k + 1, :], (TL, width)) for k in range(SLOTS)], axis=0
        )

    place = (iota((LINE, 128), 0) & 15).astype(F32)
    lane_f = iota((LINE, 128), 1).astype(F32)

    def gather_rows(cols):
        return (lane_f == slot_rows(cols, 128) + place).astype(F32)

    pick_own = gather_rows(cols_own)
    pick_up = jnp.concatenate([pick_own, gather_rows(cols_before)], axis=0).astype(BF16)
    pick_down = jnp.concatenate([pick_own, gather_rows(cols_after)], axis=0).astype(BF16)
    for r in range(8):
        side = r // 4
        rows = dot(pick_down if side else pick_up, latent[r]).astype(BF16)
        wide[(5 + r) * LINE : (6 + r) * LINE, CH : 2 * CH] = rows[0:LINE]
        margin_send[side, (r % 4) * LINE : (r % 4 + 1) * LINE, :] = rows[LINE : 2 * LINE]


    ones = jnp.ones((16, CH), BF16)

    def column_of(row):
        return lax.dot_general(three_rows(row), ones, TN, preferred_element_type=F32)

    weight = stem_weight[...]
    stem = lax.dot_general(weight, pixels[...], TN, preferred_element_type=F32) + column_of(
        stem_bias[...]
    )
    scaled = reward[...].astype(F32) * column_of(stem_gain[...])
    centred = stem - jnp.mean(stem, axis=0, keepdims=True)
    scaled = scaled - jnp.mean(scaled, axis=0, keepdims=True)
    inverse = lax.rsqrt(jnp.mean(centred * centred, axis=0, keepdims=True) + EPS)
    along = jnp.mean(scaled * centred, axis=0, keepdims=True) * inverse * inverse
    stem_grad = (scaled - centred * along) * inverse
    padded_weight = jnp.concatenate([weight, jnp.zeros((128 - PIX, STEM), BF16)], axis=0)
    pixel_grad = dot(padded_weight, stem_grad.astype(BF16))
    image[...] = pixel_grad.astype(BF16).astype(F32).T
    left_half = iota((tiles, 128), 1) < 64
    for h in range(2):
        even, odd = [image[pl.ds(2 * h + n, tiles, stride=4), :] for n in range(2)]
        both = jnp.where(left_half, even, pltpu.roll(odd, 64, 1)).astype(BF16)
        x_send[:, h * NZ : (h + 1) * NZ, :] = both.reshape(nx, NZ, 128)
    x_recv[pl.ds(mx, 1)] = x_send[pl.ds(mx, 1)]

    pl.semaphore_wait(barrier, 2 + (nx - 1) + (NZ - 1))

    def margin_copy(side, target):
        return pltpu.make_async_remote_copy(
            src_ref=margin_send.at[side],
            dst_ref=margin_recv.at[1 - side],
            send_sem=msend_sem.at[side],
            recv_sem=mrecv_sem.at[1 - side],
            device_id=target,
            device_id_type=MESH,
        )

    def x_copy(d, slot):
        target = lax.rem(mx + d, nx)
        return pltpu.make_async_remote_copy(
            src_ref=x_send.at[target],
            dst_ref=x_recv.at[slot],
            send_sem=xsend_sem.at[d - 1],
            recv_sem=xrecv_sem.at[d - 1],
            device_id=along_x(target),
            device_id_type=MESH,
        )

    for d in range(1, nx):
        x_copy(d, mx).start()
    margin_copy(0, device(before)).start()
    margin_copy(1, device(after)).start()
    for n in LATE_LOADS:
        load(n).start()

    def sums(first, second, third):
        return {(0, 0): first, (0, 1): second + third, (1, 0): first + second, (1, 1): third}

    def weight_rows(n):
        rows = pl.ds(pl.multiple_of(n * 16, 16), 16)
        by_col = [sums(*[up_weight[a, e, rows, :].astype(F32) for e in range(3)]) for a in range(3)]
        for s, v in TAPS:
            for a in range(3):
                folded[a, s * 2 + v, rows, :] = by_col[a][s, v].astype(BF16)
            by_tap = sums(*[by_col[a][s, v] for a in range(3)])
            for r, t in TAPS:
                at = pl.ds(pl.multiple_of((t * 2 + v) * CH + n * 16, 16), 16)
                combined[r * 2 + s, at, :] = by_tap[r, t].astype(BF16)

    def weight_chunk(n, carry):
        weight_rows(n)
        return carry

    load(UP_WEIGHT).wait()
    lax.fori_loop(0, CH // 16, weight_chunk, 0)
    source = iota((1, 512), 1)
    source_x, source_z = (source >> 1) & 3, (source >> 3) & 15
    source_row = 2 * (source & 1) + (source >> 8)
    cell_of = 2 * (source_x * NZ + source_z) + ((source >> 7) & 1)
    source_key = (cell_of + 1000 * source_row).astype(F32)
    own_rows = slot_rows(cols_own, 512)
    place_wide = (iota((LINE, 512), 0) & 15).astype(F32)
    inside = (place_wide >= 4.0) & (place_wide < 12.0)
    choose = jnp.concatenate(
        [
            (jnp.where(inside, own_rows + place_wide + 1000.0 * pr, -1.0) == source_key)
            .astype(F32)
            .astype(BF16)
            for pr in range(4)
        ],
        axis=0,
    )

    lane = iota((128, 128), 1)
    column = iota((128, 128), 0).astype(F32)
    slot_of = lane >> 4
    offset_of = (lane & 15).astype(F32)

    def place_columns(cols, live, first_slot):
        start = jnp.where(
            slot_of == first_slot,
            jnp.broadcast_to(cols[0:1, :], (128, 128)),
            jnp.where(
                slot_of == first_slot + 1,
                jnp.broadcast_to(cols[1:2, :], (128, 128)),
                jnp.broadcast_to(cols[2:3, :], (128, 128)),
            ),
        )
        relative = (slot_of - first_slot).astype(F32)
        valid = (relative >= 0.0) & (relative < live) & (relative < float(SLOTS))
        return jnp.where(valid & (column == start + offset_of), 1.0, 0.0)

    none = jnp.zeros((1, 1), F32)
    own_place = place_columns(cols_own, count(block), 0)
    up_place = (
        own_place
        + place_columns(cols_before, jnp.where(keep_before, count(before), none), SLOTS)
    ).astype(BF16)
    down_place = (
        own_place + place_columns(cols_after, jnp.where(keep_after, count(after), none), SLOTS)
    ).astype(BF16)

    for n in LATE_LOADS:
        load(n).wait()
    for ae in range(9):
        out_rows[ae * 8 : ae * 8 + 3, :] = out_weight[ae].astype(F32)
    flat_taps = out_rows[...].astype(BF16)
    for ph in range(4):
        out_matrix[:, ph * CH : (ph + 1) * CH] = dot(
            tables[:, 1024 + ph * 128 : 1024 + (ph + 1) * 128], flat_taps
        ).astype(BF16)

    for d in range(1, nx):
        x_copy(d, lax.rem(mx + nx - d, nx)).wait_recv()
    by_z = dot(reorder, x_recv[...].reshape(2 * tiles, 128))
    z_send[...] = by_z.reshape(NZ, 2 * nx, 128).astype(BF16)

    for far in (8, 7, 9, 6, 10, 5, 11, 4, 12, 3, 13, 2, 14, 1, 15):
        target = lax.rem(mz + far, NZ)
        pltpu.make_async_remote_copy(
            src_ref=z_send.at[target],
            dst_ref=z_recv.at[mz],
            send_sem=zsend_sem,
            recv_sem=zrecv_sem,
            device_id=along_z(target),
            device_id_type=MESH,
        ).start()
    z_recv[pl.ds(mz, 1)] = z_send[pl.ds(mz, 1)]

    margin_copy(0, device(before)).wait_recv()
    margin_copy(1, device(after)).wait_recv()
    top = margin_recv[0]
    bottom = margin_recv[1]
    wide[LINE : 5 * LINE, CH : 2 * CH] = jnp.where(keep_before, top, jnp.zeros_like(top))
    wide[13 * LINE : 17 * LINE, CH : 2 * CH] = jnp.where(
        keep_after, bottom, jnp.zeros_like(bottom)
    )
    for part in range(SLOTS):
        here = slice(LINE + part * CH, LINE + (part + 1) * CH)
        inputs = wide[here, CH : 2 * CH]
        wide[here, 0:CH] = dot(shift_low, inputs).astype(BF16)
        wide[here, 2 * CH : 3 * CH] = dot(shift_high, inputs).astype(BF16)

    bias = up_bias[...]
    def group_means(parts):
        rows = []
        for term in parts:
            high = term.astype(BF16).astype(F32)
            rest = term - high
            middle = rest.astype(BF16).astype(F32)
            rows += [high, middle, rest - middle]
        grouped = dot(jnp.concatenate(rows, axis=0).astype(BF16), groups[...])
        means = []
        for n in range(len(parts)):
            first = grouped[3 * n * LINE : (3 * n + 1) * LINE]
            second = grouped[(3 * n + 1) * LINE : (3 * n + 2) * LINE]
            third = grouped[(3 * n + 2) * LINE : (3 * n + 3) * LINE]
            line = (first + second + third) * (1.0 / 8192.0)
            means.append(
                jnp.concatenate(
                    [
                        jnp.broadcast_to(
                            jnp.sum(line[k * TL : (k + 1) * TL], axis=0, keepdims=True), (TL, CH)
                        )
                        for k in range(SLOTS)
                    ],
                    axis=0,
                )
            )
        return means

    def outputs(ph):
        r, s = ph // 2, ph % 2
        features = jnp.concatenate(
            [
                wide[(r + t) * LINE : (r + t + TL) * LINE, s * CH : (s + 2) * CH]
                for t in range(2)
            ],
            axis=1,
        )
        return dot(features, combined[ph]).reshape(TL, LINE, CH)

    value = outputs(0)
    (centre,) = group_means([jnp.sum(value, axis=0) + bias * float(TL)])
    to_centre = bias - 4.0 * centre
    total = jnp.zeros((LINE, CH), F32)
    square = jnp.zeros((LINE, CH), F32)
    for ph in range(4):
        off = (value if ph == 0 else outputs(ph)) + to_centre
        preact[ph] = off.reshape(TL * LINE, CH)
        total = total + jnp.sum(off, axis=0)
        square = square + jnp.sum(off * off, axis=0)
    mean, square = group_means([total, square])
    inv = lax.rsqrt(jnp.maximum(square - mean * mean, 0.0) + EPS)
    gain = jnp.broadcast_to(norm_gain[...], (LINE, CH))
    shift = jnp.broadcast_to(norm_bias[...], (LINE, CH))
    half_gain = 0.5 * gain
    half_scale = inv * half_gain
    half_shift = 0.5 * shift - mean * half_scale

    def silu_slopes(n, carry):
        for step in range(2):
            source_at = pl.ds(pl.multiple_of((2 * n + step + 3) * LINE, LINE), LINE)
            target_at = pl.ds(pl.multiple_of((2 * n + step) * LINE, LINE), LINE)
            for ph in range(4):
                half = preact[ph, source_at, :] * half_scale + half_shift
                curve = jnp.tanh(half)
                slopes[ph, target_at, :] = (
                    (1.0 + curve) + half * (1.0 - curve * curve)
                ) * half_gain
        return carry

    lax.fori_loop(0, 5, silu_slopes, 0)

    others = pl.ds(0, NZ - 1)
    pltpu.make_async_copy(z_recv.at[others], z_recv.at[others], zrecv_sem).wait()
    arrived = z_recv[...].astype(F32).reshape(2 * tiles, 128).astype(BF16)
    spread = dot(arrived, tables[:, 0:1024]).astype(BF16)
    stacked = jnp.concatenate([spread[:, 256 * n : 256 * (n + 1)] for n in range(4)], axis=0)
    found = dot(choose, stacked)
    lane_wide = iota((1, 256), 1) & 127
    copy_wide = sum([(lane_wide >= 12 * c).astype(jnp.int32) for c in range(1, 9)])
    col_wide = copy_wide - 3 * (
        (copy_wide >= 3).astype(jnp.int32) + (copy_wide >= 6).astype(jnp.int32)
    )
    copy_one = copy_wide[:, 0:128]
    low = pltpu.roll(found, 1, 0)
    high = pltpu.roll(found, 4 * LINE - 1, 0)
    merged = jnp.where(col_wide == 0, low, jnp.where(col_wide == 1, found, high))
    lines = []
    for pr in range(4):
        line = merged[pr * LINE : (pr + 1) * LINE]
        lines += [line[:, 0:128], line[:, 128:256]]
    nothing = jnp.zeros((LINE, 128), F32)

    def line_at(index):
        return lines[index] if 0 <= index < 8 else nothing

    for i in range(3, 13):
        around = jnp.where(
            copy_one < 3, line_at(i - 5), jnp.where(copy_one < 6, line_at(i - 4), line_at(i - 3))
        )
        cells[(i - 3) * LINE : (i - 2) * LINE, :] = around.astype(BF16)

    first = jnp.zeros((LINE, CH), F32)
    second = jnp.zeros((LINE, CH), F32)
    for ph in range(4):
        act = dot(cells[...], out_matrix[:, ph * CH : (ph + 1) * CH])
        for n in range(10):
            at = slice(n * LINE, (n + 1) * LINE)
            grad = act[at] * slopes[ph, at, :]
            grads[ph, at, :] = grad
            first = first + grad
            second = second + grad * preact[ph, (n + 3) * LINE : (n + 4) * LINE, :]
    first, second = group_means([first, second])
    offset = first * inv
    slope = (second - mean * first) * inv * inv * inv
    base = mean * slope - offset

    def row_sums(evens, odds):
        known = {}

        def normal_grad(i, ph):
            if (i, ph) not in known:
                value = base - preact[ph, i * LINE : (i + 1) * LINE, :] * slope
                if 3 <= i < 13:
                    value = value + grads[ph, (i - 3) * LINE : (i - 2) * LINE, :] * inv
                known[i, ph] = value
            return known[i, ph]

        for s in range(2):
            lanes = slice(s * CH, (s + 1) * CH)
            for i in sorted(set(evens) | set(odds)):
                if i in evens:
                    pair = normal_grad(i, s) + normal_grad(i, 2 + s)
                    zgrad[0, i * LINE : (i + 1) * LINE, lanes] = pair.astype(BF16)
                if i in odds:
                    pair = [normal_grad(i, 2 + s)] if i >= 0 else []
                    pair += [normal_grad(i + 1, s)] if i + 1 < TL else []
                    zgrad[1, (i + 1) * LINE : (i + 2) * LINE, lanes] = sum(pair).astype(BF16)

    def input_grad(pieces):
        parts = []
        for pairs in (((0, 0),), ((0, 1), (1, 0)), ((1, 1),)):
            left, right = [], []
            for s, v in pairs:
                for a, kind, start in ((0, 1, 1), (1, 0, 0), (2, 1, 0)):
                    rows = [
                        zgrad[
                            kind,
                            (i + start) * LINE : (i + start + lines_of) * LINE,
                            s * CH : (s + 1) * CH,
                        ]
                        for i, lines_of in pieces
                    ]
                    left.append(rows[0] if len(rows) == 1 else jnp.concatenate(rows, axis=0))
                    right.append(folded[a, s * 2 + v])
            parts.append(
                lax.dot_general(
                    jnp.concatenate(left, axis=1),
                    jnp.concatenate(right, axis=1),
                    NT,
                    preferred_element_type=F32,
                )
            )
        size = parts[0].shape[0]
        place_rows = iota((size, CH), 0) & 15
        return (
            parts[1]
            + jnp.where(place_rows < 15, pltpu.roll(parts[0], size - 1, 0), 0.0)
            + jnp.where(place_rows > 0, pltpu.roll(parts[2], 1, 0), 0.0)
        ).astype(BF16)

    def grad_copy(side, part):
        rows = pl.ds((part if side == 0 else 1 - part) * 2 * LINE, 2 * LINE)
        return pltpu.make_async_remote_copy(
            src_ref=grad_send.at[side, rows],
            dst_ref=grad_recv.at[1 - side, rows],
            send_sem=gsend_sem.at[side, part],
            recv_sem=grecv_sem.at[1 - side, part],
            device_id=device(after if side else before),
            device_id_type=MESH,
        )

    row_sums((0, 1, 14, 15), (-1, 0, 1, 13, 14, 15))
    margin_grad = input_grad(((0, 2), (14, 2)))
    grad_send[0, 0 : 2 * LINE, :] = margin_grad[0 : 2 * LINE]
    grad_send[1, 2 * LINE : 4 * LINE, :] = margin_grad[2 * LINE : 4 * LINE]
    grad_copy(0, 0).start()
    grad_copy(1, 0).start()
    row_sums((2, 3, 12, 13), (2, 3, 11, 12))
    margin_grad = input_grad(((2, 2), (12, 2)))
    grad_send[0, 2 * LINE : 4 * LINE, :] = margin_grad[0 : 2 * LINE]
    grad_send[1, 0 : 2 * LINE, :] = margin_grad[2 * LINE : 4 * LINE]
    grad_copy(0, 1).start()
    grad_copy(1, 1).start()
    row_sums(range(4, 12), range(4, 11))
    own_grad[...] = input_grad(((4, 8),))

    margin_copy(0, device(before)).wait_send()
    margin_copy(1, device(after)).wait_send()
    for d in range(1, nx):
        x_copy(d, mx).wait_send()
    pltpu.make_async_copy(z_send.at[others], z_send.at[others], zsend_sem).wait()

    rest = jnp.zeros((128 - 2 * LINE, CH), BF16)
    for part, rows in ((0, (2, 3, 4, 5)), (1, (0, 1, 6, 7))):
        grad_copy(0, part).wait_recv()
        grad_copy(1, part).wait_recv()
        for r in rows:
            side = r // 4
            at = (r % 4) * LINE
            terms = jnp.concatenate(
                [
                    own_grad[r * LINE : (r + 1) * LINE, :],
                    grad_recv[side, at : at + LINE, :],
                    rest,
                ],
                axis=0,
            )
            out[r] = dot(down_place if side else up_place, terms).astype(BF16)

    for side in range(2):
        for part in range(2):
            grad_copy(side, part).wait_send()


def per_device(
    latent_feat,
    reward_grad,
    patches,
    up_weight,
    up_bias,
    norm_gain,
    norm_bias,
    out_weight,
    stem_weight,
    stem_bias,
    stem_gain,
    tile_count,
    tile_cols,
):
    sections = lax.axis_size("section")
    nx = lax.axis_size("tile") // NZ
    blocks = sections * nx * NZ
    operands = (
        latent_feat,
        reward_grad.reshape(-1, STEM).T,
        patches.T,
        up_weight,
        up_bias.reshape(1, CH),
        norm_gain.reshape(1, CH),
        norm_bias.reshape(1, CH),
        out_weight.transpose(0, 1, 3, 2).reshape(9, 3, CH),
        stem_weight,
        stem_bias.reshape(1, STEM),
        stem_gain.reshape(1, STEM),
        tile_count.reshape(1, blocks),
        tile_cols.T,
        jnp.asarray(np.concatenate([cell_lanes(), out_taps()], axis=1), BF16),
    )
    pinned = [pltpu.with_memory_space_constraint(array, pltpu.HBM) for array in operands]
    return pl.pallas_call(
        functools.partial(kernel, nx, sections),
        out_shape=pltpu.VMEM(latent_feat.shape, BF16),
        in_specs=[pl.BlockSpec(memory_space=pltpu.HBM)] * OPERANDS,
        out_specs=pl.BlockSpec(memory_space=pltpu.VMEM),
        scratch_shapes=[pltpu.VMEM(array.shape, array.dtype) for array in operands]
        + [
            pltpu.VMEM((18 * LINE, 3 * CH), BF16),
            pltpu.VMEM((4, 4 * CH, CH), BF16),
            pltpu.VMEM((3, 4, CH, CH), BF16),
            pltpu.VMEM((128, 4 * CH), BF16),
            pltpu.VMEM((128, CH), F32),
            pltpu.VMEM((2, 4 * LINE, CH), BF16),
            pltpu.VMEM((2, 4 * LINE, CH), BF16),
            pltpu.VMEM((4 * nx * NZ, 128), F32),
            pltpu.VMEM((nx, 2 * NZ, 128), BF16),
            pltpu.VMEM((nx, 2 * NZ, 128), BF16),
            pltpu.VMEM((NZ, 2 * nx, 128), BF16),
            pltpu.VMEM((NZ, 2 * nx, 128), BF16),
            pltpu.VMEM((4, TL * LINE, CH), F32),
            pltpu.VMEM((4, 10 * LINE, CH), F32),
            pltpu.VMEM((4, 10 * LINE, CH), F32),
            pltpu.VMEM((2, 17 * LINE, 2 * CH), BF16),
            pltpu.VMEM((10 * LINE, 128), BF16),
            pltpu.VMEM((8 * LINE, CH), BF16),
            pltpu.VMEM((2, 4 * LINE, CH), BF16),
            pltpu.VMEM((2, 4 * LINE, CH), BF16),
            pltpu.VMEM((CH, CH), BF16),
            pltpu.SemaphoreType.DMA((OPERANDS,)),
            pltpu.SemaphoreType.DMA((2,)),
            pltpu.SemaphoreType.DMA((2,)),
            pltpu.SemaphoreType.DMA((nx - 1,)),
            pltpu.SemaphoreType.DMA((nx - 1,)),
            pltpu.SemaphoreType.DMA,
            pltpu.SemaphoreType.DMA,
            pltpu.SemaphoreType.DMA((2, 2)),
            pltpu.SemaphoreType.DMA((2, 2)),
        ],
        compiler_params=pltpu.CompilerParams(
            collective_id=0, has_side_effects=True, vmem_limit_bytes=48 * 1024 * 1024
        ),
    )(*pinned)


def solution(mesh):
    return jax.shard_map(
        per_device,
        mesh=mesh,
        in_specs=(
            P(("section", "tile"), None, None),
            P("section", "tile", None),
            P("section", "tile"),
        )
        + (P(),) * 10,
        out_specs=P(("section", "tile"), None, None),
        check_vma=False,
    )
```
